512 devices in a mesh: gx: 8 (over x, core), gy: 4 (over z_hi), gz: 16 (over y, z_lo).
Axes of the slice: x: 4, y: 8, z: 8 (z_hi: 4, z_lo: 2; z = z_hi * 2 + z_lo), core: 2. Of those that a mesh axis runs over, the one named last changes fastest.
Arguments:
- state: float32 [19, 64, 32, 1024], P(None, 'gz', 'gy', 'gx'), may hold values from 0 to 0.5, as said below
- adjoint_seed: float32 [19, 64, 32, 1024], P(None, 'gz', 'gy', 'gx'), may hold values from -6 to 6
- eddy_rate: float32 [64, 32, 1024], P('gz', 'gy', 'gx'), may hold values from 0.005 to 3
- smag_coeff: float32 [], replicated, may hold values from 0.1 to 0.3
- heights: int32 [32, 1024], replicated, may hold values from 0 to 32, as said below
Outputs:
- adjoint_state: float32 [19, 64, 32, 1024], P(None, 'gz', 'gy', 'gx')
- viscosity_gradient: float32 [64, 32, 1024], P('gz', 'gy', 'gx')
- totals: float32 [2], replicated
The draws below stay inside these ranges and needn't reach their ends.
Inputs may be any that keep to these rules, and one draw needn't show every extreme that they name: `state`: all populations are positive; each cell's density is near one and its mean velocity is mostly streamwise. `heights`: heights are constant over aligned 4 x 4 footprints of columns.
All inputs are finite; a program needn't handle non-finite values.
Results may differ from the reference program's by a relative error of at most 0.000068.
Values sent between devices are 32-bit elements; how exact they have to be, the bound alone decides.
No kernel may reach another device: no remote copies, remote signals or barrier semaphores. Data moves between devices by JAX's collectives and lax.ppermute only.
A program may use at most 64 MiB of HBM per device.

```python
import math
import jax
import jax.numpy as jnp
import numpy as np
from jax import lax

Q = 19
NX = 1024
NY = 32
NZ = 64


DRAW_VEL = np.array([[0, 0, 0], [1, 0, 0], [-1, 0, 0], [0, 1, 0], [0, -1, 0], [0, 0, 1], [0, 0, -1], [1, 1, 0], [-1, -1, 0], [1, -1, 0], [-1, 1, 0], [1, 0, 1], [-1, 0, -1], [1, 0, -1], [-1, 0, 1], [0, 1, 1], [0, -1, -1], [0, 1, -1], [0, -1, 1]])


DRAW_WEIGHTS = [1.0 / 3.0] + [1.0 / 18.0] * 6 + [1.0 / 36.0] * 12


def draw_state(key, part):
    key = jax.random.fold_in(key, 11)
    keys = jax.random.split(key, 5)
    grid = (NZ, NY, NX)
    density = 1.0 + 0.05 * jax.random.uniform(keys[0], grid, jnp.float32, -1.0, 1.0)
    mean_flow = 0.08
    vel_x = mean_flow + 0.03 * jax.random.uniform(keys[1], grid, jnp.float32, -1.0, 1.0)
    vel_y = 0.03 * jax.random.uniform(keys[2], grid, jnp.float32, -1.0, 1.0)
    vel_z = 0.03 * jax.random.uniform(keys[3], grid, jnp.float32, -1.0, 1.0)
    noise = 0.2 * jax.random.uniform(keys[4], (19,) + grid, jnp.float32, -1.0, 1.0)
    usq = vel_x * vel_x + vel_y * vel_y + vel_z * vel_z
    pieces = []
    for idx in range(19):
        along = float(DRAW_VEL[idx, 0]) * vel_x + float(DRAW_VEL[idx, 1]) * vel_y + float(DRAW_VEL[idx, 2]) * vel_z
        equil = DRAW_WEIGHTS[idx] * density * (1.0 + 3.0 * along + 4.5 * along * along - 1.5 * usq)
        pieces.append(equil * (1.0 + noise[idx]))
    return jnp.stack(pieces, 0)


def draw_eddy_rate(key, part):
    key = jax.random.fold_in(key, 12)
    keys = jax.random.split(key, 1)
    base = jnp.exp(jax.random.uniform(keys[0], (NZ, NY, NX), jnp.float32, jnp.log(0.005), jnp.log(0.25)))
    levels = jnp.arange(NZ).astype(jnp.float32).reshape(NZ, 1, 1)
    rise = 1.0 + 2.0 * levels / (NZ - 1.0)
    return base * rise


def draw_heights(key, part):
    key = jax.random.fold_in(key, 13)
    keys = jax.random.split(key, 2)
    blocks = jax.random.randint(keys[0], (NY // 4, NX // 4), 0, NZ // 2 + 1).astype(jnp.int32)
    streets = jax.random.randint(keys[1], (NY // 4, NX // 4), 0, 2).astype(jnp.int32)
    tops = blocks * streets
    tops = tops.at[0, 0].set(NZ // 2).at[0, 1].set(0)
    return jnp.repeat(jnp.repeat(tops, 4, axis=0), 4, axis=1)


def steps_of(own_key, extent, shards, low, high):
    def one(dim, blocks):
        draws = jax.random.uniform(jax.random.fold_in(jax.random.fold_in(own_key, 6), dim), (blocks,), jnp.float32, low / len(shards), high / len(shards))
        return jnp.repeat(jnp.exp(draws), extent[dim] // blocks).reshape((-1,) + (1,) * (len(extent) - dim - 1))

    level = one(*shards[0])
    for cut in shards[1:]:
        level = level * one(*cut)
    return level


def scatter_about(own_key, dims, width, bound, cuts=(), held_as=jnp.bfloat16):
    values = width * jax.random.normal(own_key, dims, jnp.float32)
    if cuts:
        values = values * steps_of(own_key, dims, cuts, -0.22, 0.18)
    return jnp.clip(values, -bound, bound).astype(held_as)


def setup_inputs(seed: int = 0) -> dict:
    arg_keys = jax.random.split(jax.random.key(seed), 6)
    return {
        "state": draw_state(jax.random.fold_in(arg_keys[5], 71), 0),
        "adjoint_seed": scatter_about(arg_keys[1], (Q, NZ, NY, NX), 1.0, 6.0, ((1, 16), (2, 4), (3, 8)), jnp.float32),
        "eddy_rate": draw_eddy_rate(jax.random.fold_in(arg_keys[5], 71), 0),
        "smag_coeff": jnp.clip(jax.random.uniform(arg_keys[3], (), jnp.float32, 0.1, 0.3), 0.1, 0.3),
        "heights": draw_heights(jax.random.fold_in(arg_keys[5], 71), 0),
    }


VEL = np.array([[0, 0, 0], [1, 0, 0], [-1, 0, 0], [0, 1, 0], [0, -1, 0], [0, 0, 1], [0, 0, -1], [1, 1, 0], [-1, -1, 0], [1, -1, 0], [-1, 1, 0], [1, 0, 1], [-1, 0, -1], [1, 0, -1], [-1, 0, 1], [0, 1, 1], [0, -1, -1], [0, 1, -1], [0, -1, 1]])
OPPOSITE = [0, 2, 1, 4, 3, 6, 5, 8, 7, 10, 9, 12, 11, 14, 13, 16, 15, 18, 17]
LATTICE_WEIGHTS = [1.0 / 3.0] + [1.0 / 18.0] * 6 + [1.0 / 36.0] * 12
UREF = 0.08
NU_BASE = 0.004

def column(values):
    return jnp.array(values, jnp.float32).reshape(19, 1, 1, 1)

def collide(populations, omega):
    comp_x = column([float(v) for v in VEL[:, 0]])
    comp_y = column([float(v) for v in VEL[:, 1]])
    comp_z = column([float(v) for v in VEL[:, 2]])
    weights = column(LATTICE_WEIGHTS)
    density = lax.optimization_barrier(jnp.sum(populations, 0))
    vel_x = lax.optimization_barrier(jnp.sum(comp_x * populations, 0)) / density
    vel_y = lax.optimization_barrier(jnp.sum(comp_y * populations, 0)) / density
    vel_z = lax.optimization_barrier(jnp.sum(comp_z * populations, 0)) / density
    usq = vel_x * vel_x + vel_y * vel_y + vel_z * vel_z
    along = comp_x * vel_x + comp_y * vel_y + comp_z * vel_z
    equil = weights * density * (1.0 + 3.0 * along + 4.5 * along * along - 1.5 * usq)
    return populations - omega * (populations - equil)

def window(grid, index, offset):
    depth, rows, cols = (grid.shape[-3] - 2, grid.shape[-2] - 2, grid.shape[-1] - 2)
    off_x, off_y, off_z = offset
    if index is None:
        return grid[1 + off_z:1 + off_z + depth, 1 + off_y:1 + off_y + rows, 1 + off_x:1 + off_x + cols]
    return grid[index, 1 + off_z:1 + off_z + depth, 1 + off_y:1 + off_y + rows, 1 + off_x:1 + off_x + cols]

def pull(field, extended, solid_ext):
    pieces = []
    for idx in range(19):
        offset = (-int(VEL[idx, 0]), -int(VEL[idx, 1]), -int(VEL[idx, 2]))
        source = window(extended, idx, offset)
        blocked = window(solid_ext, None, offset)
        pieces.append((1.0 - blocked) * source + blocked * field[OPPOSITE[idx]])
    return jnp.stack(pieces, 0)

def drag_links(solid_ext):
    own = window(solid_ext, None, (0, 0, 0))
    pieces = []
    for idx in range(19):
        offset = (int(VEL[idx, 0]), int(VEL[idx, 1]), int(VEL[idx, 2]))
        pieces.append(2.0 * float(VEL[idx, 0]) * (1.0 - own) * window(solid_ext, None, offset))
    return jnp.stack(pieces, 0)

def reference(state, adjoint_seed, eddy_rate, smag_coeff, heights):
    omega = 1.0 / (0.5 + 3.0 * (NU_BASE + smag_coeff * eddy_rate))
    padded = jnp.pad(heights, 1, constant_values=NZ + 2).astype(jnp.int32)
    levels = (jnp.arange(NZ + 2) - 1).astype(jnp.int32).reshape(NZ + 2, 1, 1)
    solid_ext = ((levels < padded[None]) | (levels >= NZ)).astype(jnp.float32)
    links = drag_links(solid_ext)
    scale = 1.0 / (2.0 * UREF * NX * NY)
    step = jax.checkpoint(collide)

    def forward(populations, relax):
        post0 = step(populations, relax)
        f_one = pull(post0, jnp.pad(post0, ((0, 0), (1, 1), (1, 1), (1, 1))), solid_ext)
        post1 = step(f_one, relax)
        f_two = pull(post1, jnp.pad(post1, ((0, 0), (1, 1), (1, 1), (1, 1))), solid_ext)
        drag = scale * jnp.sum(links * (post0 + post1))
        return (f_two, drag)
    outputs, backward = jax.vjp(forward, state, omega)
    adjoint_state, grad_omega = backward((adjoint_seed, jnp.ones((), jnp.float32)))
    viscosity_gradient = -3.0 * omega * omega * grad_omega
    sensitivity = jnp.sum(viscosity_gradient * eddy_rate) / math.sqrt(NX * NY * NZ)
    totals = jnp.stack([outputs[1], sensitivity])
    return (adjoint_state, viscosity_gradient, totals)
```

```python
import math

import jax
import jax.numpy as jnp
import numpy as np
from jax import lax
from jax.sharding import PartitionSpec as P

VEL = [
    (0, 0, 0),
    (1, 0, 0),
    (-1, 0, 0),
    (0, 1, 0),
    (0, -1, 0),
    (0, 0, 1),
    (0, 0, -1),
    (1, 1, 0),
    (-1, -1, 0),
    (1, -1, 0),
    (-1, 1, 0),
    (1, 0, 1),
    (-1, 0, -1),
    (1, 0, -1),
    (-1, 0, 1),
    (0, 1, 1),
    (0, -1, -1),
    (0, 1, -1),
    (0, -1, 1),
]
OPPOSITE = [0, 2, 1, 4, 3, 6, 5, 8, 7, 10, 9, 12, 11, 14, 13, 16, 15, 18, 17]
LATTICE_WEIGHTS = [1.0 / 3.0] + [1.0 / 18.0] * 6 + [1.0 / 36.0] * 12
UREF = 0.08
NU_BASE = 0.004
Q = 19


def signed(terms):
    total = None
    for factor, value in terms:
        if factor == 0:
            continue
        piece = value if factor == 1 else (-value if factor == -1 else factor * value)
        total = piece if total is None else total + piece
    return total


def along(idx, vec):
    return signed([(VEL[idx][axis], vec[axis]) for axis in range(3)])


def flow(pops):
    rho = signed([(1, p) for p in pops])
    inverse = 1.0 / rho
    vel = [signed([(VEL[i][axis], pops[i]) for i in range(Q)]) * inverse for axis in range(3)]
    return rho, vel


def shapes(vel):
    base = 1.0 - 1.5 * (vel[0] * vel[0] + vel[1] * vel[1] + vel[2] * vel[2])
    out = [base] + [None] * (Q - 1)
    for i in range(1, Q, 2):
        cu = along(i, vel)
        even = base + 4.5 * cu * cu
        out[i] = even + 3.0 * cu
        out[i + 1] = even - 3.0 * cu
    return out


def departures(pops):
    rho, vel = flow(pops)
    shape = shapes(vel)
    return [LATTICE_WEIGHTS[i] * rho * shape[i] - pops[i] for i in range(Q)]


def collide_adjoint(pops, omega, cot):
    rho, vel = flow(pops)
    shape = shapes(vel)
    weighted = [LATTICE_WEIGHTS[i] * cot[i] for i in range(Q)]
    level = signed([(1, weighted[i] * shape[i]) for i in range(Q)])
    mass = signed([(1, w) for w in weighted])
    first = [signed([(VEL[i][axis], weighted[i]) for i in range(Q)]) for axis in range(3)]

    def second(a, b):
        return signed([(VEL[i][a] * VEL[i][b], weighted[i]) for i in range(Q)])

    slope = []
    for a in range(3):
        mixed = signed([(1, second(a, b) * vel[b]) for b in range(3)])
        slope.append(3.0 * first[a] + 9.0 * mixed - 3.0 * mass * vel[a])
    base = omega * (level - (slope[0] * vel[0] + slope[1] * vel[1] + slope[2] * vel[2]))
    tilt = [omega * s for s in slope]
    keep = 1.0 - omega
    adjoint = []
    for i in range(Q):
        part = along(i, tilt)
        adjoint.append(keep * cot[i] + (base if part is None else base + part))
    away = [LATTICE_WEIGHTS[i] * rho * shape[i] - pops[i] for i in range(Q)]
    grad = signed([(1, cot[i] * away[i]) for i in range(Q)])
    return adjoint, grad, away


def plus_one(axis):
    count = lax.axis_size(axis)
    return [(i, (i + 1) % count) for i in range(count)]


def minus_one(axis):
    return [(target, source) for source, target in plus_one(axis)]


def pair_pairs(first, second):
    count = lax.axis_size("gz")
    return [(a * count + b, c * count + d) for a, c in first for b, d in second]


def solid_around(heights, depth, rows, cols):
    total_z = depth * lax.axis_size("gz")
    total_y, total_x = heights.shape
    start_z = lax.axis_index("gz") * depth
    start_y = lax.axis_index("gy") * rows
    start_x = lax.axis_index("gx") * cols
    padded = jnp.pad(heights, ((1, 2), (1, 2)), mode="wrap")
    columns = lax.dynamic_slice(padded, (start_y, start_x), (rows + 3, cols + 3))
    z = start_z - 1 + lax.iota(jnp.int32, depth + 3)
    y = start_y - 1 + lax.iota(jnp.int32, rows + 3)
    x = start_x - 1 + lax.iota(jnp.int32, cols + 3)
    wrapped = jnp.where(z < 0, z + total_z, jnp.where(z >= total_z, z - total_z, z))
    solid = wrapped.reshape(-1, 1, 1) < columns[None]

    def border(coord, total):
        return (coord == -1) | (coord == total - 1)

    walls = (
        border(x, total_x).reshape(1, 1, -1),
        border(y, total_y).reshape(1, -1, 1),
        border(z, total_z).reshape(-1, 1, 1),
    )
    return solid, walls


def on_device(state, adjoint_seed, eddy_rate, smag_coeff, heights):
    depth, rows, cols = eddy_rate.shape
    total_x = cols * lax.axis_size("gx")
    total_y = rows * lax.axis_size("gy")
    total_z = depth * lax.axis_size("gz")
    scale = 1.0 / (2.0 * UREF * total_x * total_y)
    solid, walls = solid_around(heights, depth, rows, cols)
    sizes = (cols, rows, depth)

    def box(start, offset):
        return tuple(
            slice(start + offset[a] + 1, start + offset[a] + 1 + sizes[a]) for a in (2, 1, 0)
        )

    def crossing(start, offset):
        flags = None
        for a in range(3):
            if offset[a] == 0:
                continue
            low = start + 1 + (0 if offset[a] > 0 else -1)
            part = lax.slice_in_dim(walls[a], low, low + sizes[a], axis=2 - a)
            flags = part if flags is None else flags | part
        return flags

    def blocked(start, idx, sign):
        offset = tuple(sign * v for v in VEL[idx])
        wet = solid[box(start, offset)]
        return wet if idx == 0 else wet | crossing(start, offset)

    def extend_up(block):
        high = lax.ppermute(block[..., :2], "gx", minus_one("gx"))
        block = jnp.concatenate([block, high], axis=-1)
        y_msg, z_msg, yz_msg = block[:, :, :2], block[:, :2], block[:, :2, :2]
        z_high = lax.ppermute(z_msg, "gz", minus_one("gz"))
        y_high = lax.ppermute(y_msg, "gy", minus_one("gy"))
        yz_high = lax.ppermute(yz_msg, ("gy", "gz"), pair_pairs(minus_one("gy"), minus_one("gz")))
        low_half = jnp.concatenate([block, y_high], axis=2)
        high_half = jnp.concatenate([z_high, yz_high], axis=2)
        return jnp.concatenate([low_half, high_half], axis=1)

    both = jnp.concatenate([state, adjoint_seed, eddy_rate[None]], axis=0)
    ext = extend_up(both)
    eddy_ext = ext[2 * Q]
    omega_ext = 1.0 / (0.5 + 3.0 * (NU_BASE + smag_coeff * eddy_ext))
    pops_ext = [ext[i] for i in range(Q)]
    seed_ext = [ext[Q + i] for i in range(Q)]
    away_ext = departures(pops_ext)
    post_ext = [pops_ext[i] + omega_ext * away_ext[i] for i in range(Q)]
    heat_ext = omega_ext * omega_ext * eddy_ext
    tangent_ext = [heat_ext * away_ext[i] for i in range(Q)]

    def window(field, offset):
        return field[
            tuple(slice(1 + offset[a], 1 + offset[a] + sizes[a]) for a in (2, 1, 0))
        ]

    here = (0, 0, 0)

    def pull(field):
        out = []
        for i in range(Q):
            offset = tuple(-v for v in VEL[i])
            out.append(
                jnp.where(
                    blocked(1, i, -1), window(field[OPPOSITE[i]], here), window(field[i], offset)
                )
            )
        return out

    def push(start, own, target):
        out = []
        fluid = ~solid[box(start, here)]
        for i in range(Q):
            open_way = fluid if i == 0 else fluid & ~crossing(start, VEL[i])
            out.append(
                jnp.where(open_way, target(i), 0.0)
                + jnp.where(blocked(start, i, 1), own(OPPOSITE[i]), 0.0)
            )
        return out

    def drag_links(start):
        fluid = ~solid[box(start, here)]
        return {
            i: jnp.where(fluid & blocked(start, i, 1), 2.0 * scale * VEL[i][0], 0.0)
            for i in range(Q)
            if VEL[i][0] != 0
        }

    links = drag_links(1)
    f_one = pull(post_ext)
    tangent_one = pull(tangent_ext)
    cot_one = push(
        1, lambda i: window(seed_ext[i], here), lambda i: window(seed_ext[i], VEL[i])
    )
    cot_one = [cot_one[i] + links[i] if i in links else cot_one[i] for i in range(Q)]
    omega_one = window(omega_ext, here)
    adjoint_one, grad_one, away_one = collide_adjoint(f_one, omega_one, cot_one)
    drag_local = jnp.sum(
        signed(
            [
                (1, links[i] * (window(post_ext[i], here) + f_one[i] + omega_one * away_one[i]))
                for i in links
            ]
        )
    )
    sens_local = jnp.sum(
        signed([(1, adjoint_one[i] * tangent_one[i]) for i in range(Q)])
        + signed([(1, links[i] * window(tangent_ext[i], here)) for i in links])
        + window(heat_ext, here) * grad_one
    ) * (-3.0 / math.sqrt(total_x * total_y * total_z))

    back = jnp.stack(adjoint_one + [grad_one])
    lanes = lax.iota(jnp.int32, 128).reshape(1, 128)
    sums = jnp.where(lanes == 0, drag_local, jnp.where(lanes == 1, sens_local, 0.0))

    def total_over(axes, row):
        count = math.prod(lax.axis_size(a) for a in axes)
        parts = lax.all_to_all(
            jnp.broadcast_to(row, (count, 128)), axes, split_axis=0, concat_axis=0, tiled=True
        )
        return jnp.sum(parts, 0, keepdims=True)

    back, sums = lax.optimization_barrier((back, sums))
    low = lax.ppermute(back[..., -2:], "gx", plus_one("gx"))
    sums = total_over(("gy", "gz"), sums)
    wide = jnp.concatenate([low, back], axis=-1)
    y_msg, z_msg, yz_msg, sums = lax.optimization_barrier(
        (wide[:, :, -2:], wide[:, -2:], wide[:, -2:, -2:], sums)
    )
    z_low = lax.ppermute(z_msg, "gz", plus_one("gz"))
    y_low = lax.ppermute(y_msg, "gy", plus_one("gy"))
    yz_low = lax.ppermute(yz_msg, ("gy", "gz"), pair_pairs(plus_one("gy"), plus_one("gz")))
    sums = total_over(("gx",), sums)
    high_half = jnp.concatenate([y_low, wide], axis=2)
    low_half = jnp.concatenate([yz_low, z_low], axis=2)
    back_ext = jnp.concatenate([low_half, high_half], axis=1)

    links = drag_links(0)
    cot_zero = push(
        0,
        lambda i: window(back_ext[i], here),
        lambda i: window(back_ext[i], VEL[i]),
    )
    cot_zero = [cot_zero[i] + links[i] if i in links else cot_zero[i] for i in range(Q)]
    omega = 1.0 / (0.5 + 3.0 * (NU_BASE + smag_coeff * eddy_rate))
    adjoint_zero, grad_zero, _ = collide_adjoint([state[i] for i in range(Q)], omega, cot_zero)
    grad = grad_zero + window(back_ext[Q], here)
    return jnp.stack(adjoint_zero), -3.0 * omega * omega * grad, sums[0, :2]


def solution(mesh):
    return jax.shard_map(
        on_device,
        mesh=mesh,
        in_specs=(
            P(None, "gz", "gy", "gx"),
            P(None, "gz", "gy", "gx"),
            P("gz", "gy", "gx"),
            P(),
            P(),
        ),
        out_specs=(P(None, "gz", "gy", "gx"), P("gz", "gy", "gx"), P()),
        check_vma=False,
    )
```

```python
import functools
import math

import jax
import jax.numpy as jnp
from jax import lax
from jax.experimental import pallas as pl
from jax.experimental.pallas import tpu as pltpu
from jax.sharding import PartitionSpec as P

VEL = [
    (0, 0, 0),
    (1, 0, 0),
    (-1, 0, 0),
    (0, 1, 0),
    (0, -1, 0),
    (0, 0, 1),
    (0, 0, -1),
    (1, 1, 0),
    (-1, -1, 0),
    (1, -1, 0),
    (-1, 1, 0),
    (1, 0, 1),
    (-1, 0, -1),
    (1, 0, -1),
    (-1, 0, 1),
    (0, 1, 1),
    (0, -1, -1),
    (0, 1, -1),
    (0, -1, 1),
]
OPPOSITE = [0, 2, 1, 4, 3, 6, 5, 8, 7, 10, 9, 12, 11, 14, 13, 16, 15, 18, 17]
LATTICE_WEIGHTS = [1.0 / 3.0] + [1.0 / 18.0] * 6 + [1.0 / 36.0] * 12
UREF = 0.08
NU_BASE = 0.004
Q = 19
DEPTH = 4
ROWS = 8
COLS = 128
FAR = 1 << 20
UP = [i for i in range(Q) if VEL[i][2] == 1]
DOWN = [i for i in range(Q) if VEL[i][2] == -1]
SIDES = [(dy, dx) for dy in (-1, 0, 1) for dx in (-1, 0, 1)]

N_UP = 2 * Q + 1
N_BACK = Q + 1
UP_Z = [(c, 0) for c in range(N_UP)] + [
    (c, 1) for c in range(N_UP) if c < Q or c == 2 * Q or c - Q in UP
]
BACK_Z = [(c, 2) for c in DOWN] + [(c, 3) for c in range(N_BACK)]


def strips(fields):
    return -(-fields * DEPTH * 2 // COLS)


def signed(terms):
    total = None
    for factor, value in terms:
        if factor == 0:
            continue
        piece = value if factor == 1 else (-value if factor == -1 else factor * value)
        total = piece if total is None else total + piece
    return total


def along(idx, vec):
    return signed([(VEL[idx][axis], vec[axis]) for axis in range(3)])


def flow(pops):
    rho = signed([(1, p) for p in pops])
    inverse = 1.0 / rho
    vel = [signed([(VEL[i][axis], pops[i]) for i in range(Q)]) * inverse for axis in range(3)]
    return rho, vel


def shapes(vel):
    base = 1.0 - 1.5 * (vel[0] * vel[0] + vel[1] * vel[1] + vel[2] * vel[2])
    out = [base] + [None] * (Q - 1)
    for i in range(1, Q, 2):
        cu = along(i, vel)
        even = base + 4.5 * cu * cu
        out[i] = even + 3.0 * cu
        out[i + 1] = even - 3.0 * cu
    return out


def departures(pops):
    rho, vel = flow(pops)
    shape = shapes(vel)
    return [LATTICE_WEIGHTS[i] * rho * shape[i] - pops[i] for i in range(Q)]


def collide_adjoint(pops, omega, cot):
    rho, vel = flow(pops)
    shape = shapes(vel)
    weighted = [LATTICE_WEIGHTS[i] * cot[i] for i in range(Q)]
    level = signed([(1, weighted[i] * shape[i]) for i in range(Q)])
    mass = signed([(1, w) for w in weighted])
    first = [signed([(VEL[i][axis], weighted[i]) for i in range(Q)]) for axis in range(3)]

    def second(a, b):
        return signed([(VEL[i][a] * VEL[i][b], weighted[i]) for i in range(Q)])

    pair = {(a, b): second(a, b) for a in range(3) for b in range(a, 3)}
    slope = []
    for a in range(3):
        mixed = signed([(1, pair[min(a, b), max(a, b)] * vel[b]) for b in range(3)])
        slope.append(3.0 * first[a] + 9.0 * mixed - 3.0 * mass * vel[a])
    base = omega * (level - (slope[0] * vel[0] + slope[1] * vel[1] + slope[2] * vel[2]))
    tilt = [omega * s for s in slope]
    keep = 1.0 - omega
    adjoint = []
    for i in range(Q):
        part = along(i, tilt)
        adjoint.append(keep * cot[i] + (base if part is None else base + part))
    away = [LATTICE_WEIGHTS[i] * rho * shape[i] - pops[i] for i in range(Q)]
    grad = signed([(1, cot[i] * away[i]) for i in range(Q)])
    return adjoint, grad, away


def relaxation(smag, eddy):
    return 1.0 / (0.5 + 3.0 * (NU_BASE + smag * eddy))


def row_ids():
    return lax.broadcasted_iota(jnp.int32, (ROWS, COLS), 0)


def lane_ids():
    return lax.broadcasted_iota(jnp.int32, (ROWS, COLS), 1)


def turn(tile, amount, axis):
    size = tile.shape[axis]
    if isinstance(amount, int):
        amount %= size
        return tile if amount == 0 else pltpu.roll(tile, amount, axis)
    return pltpu.roll(tile, lax.rem(amount + size, size), axis)


def pack_columns(out_ref, planes, start):
    lanes = lane_ids()
    per = COLS // 2
    for strip in range(-(-len(planes) // per)):
        total = None
        for j, plane in enumerate(planes[strip * per : (strip + 1) * per]):
            moved = turn(plane(), 2 * j - start, 1)
            total = moved if total is None else jnp.where(lanes >= 2 * j, moved, total)
        out_ref[:, strip * COLS : (strip + 1) * COLS] = total


def pack_rows(planes, start):
    rows = row_ids()
    total = None
    for j, plane in enumerate(planes):
        moved = turn(plane, 2 * j - start, 0)
        total = moved if total is None else jnp.where(rows >= 2 * j, moved, total)
    return total


def pack_faces(plane, fields, strip, n_strips, layers, z_list, start, z_ref, y_ref, yz_ref):
    for at, (c, z) in enumerate(z_list):
        z_ref[at] = plane(c, z)
    columns = [strip(v) for v in range(n_strips)]
    for v in range(n_strips):
        z_ref[len(z_list) + v] = columns[v]
    for c in range(fields):
        y_ref[c] = pack_rows([plane(c, z) for z in range(DEPTH)], start)
    y_ref[fields] = pack_rows(columns, start)
    pairs = [(c, z) for c in range(fields) for z in layers]
    for at in range(0, len(pairs), 4):
        yz_ref[at // 4] = pack_rows([plane(c, z) for c, z in pairs[at : at + 4]], start)
    yz_ref[-(-len(pairs) // 4)] = pack_rows(columns, start)


def up_columns_kernel(state_ref, seed_ref, eddy_ref, out_ref):
    planes = [
        functools.partial(lambda r, c, z: r[c, z], ref, c, z)
        for ref in (state_ref, seed_ref)
        for c in range(Q)
        for z in range(DEPTH)
    ] + [functools.partial(lambda z: eddy_ref[z], z) for z in range(DEPTH)]
    pack_columns(out_ref, planes, 0)


def up_faces_kernel(state_ref, seed_ref, eddy_ref, x_ref, z_ref, y_ref, yz_ref):
    def plane(c, z):
        if c == 2 * Q:
            return eddy_ref[z]
        return state_ref[c, z] if c < Q else seed_ref[c - Q, z]

    def strip(v):
        return x_ref[:, v * COLS : (v + 1) * COLS]

    pack_faces(plane, N_UP, strip, strips(N_UP), (0, 1), UP_Z, 0, z_ref, y_ref, yz_ref)


def back_faces_kernel(back_ref, x_ref, z_ref, y_ref, yz_ref):
    def plane(c, z):
        return back_ref[c, z]

    def strip(v):
        return x_ref[:, v * COLS : (v + 1) * COLS]

    pack_faces(
        plane, N_BACK, strip, strips(N_BACK), (2, 3), BACK_Z, ROWS - 1, z_ref, y_ref, yz_ref
    )


def level_of(start_z, total_z, plane):
    level = start_z + plane
    return lax.rem(level + total_z, total_z)


def wall_between(start_z, total_z, plane, step):
    upper = start_z + plane + (1 if step > 0 else 0)
    return (upper == total_z) | (upper == 0)


def masks_at(high_ref, own_ref, start_z, total_z, plane):
    solid, way = {}, {}
    here = level_of(start_z, total_z, plane)
    for i in range(Q):
        dx, dy, dz = VEL[i]
        side = SIDES.index((dy, dx))
        there, mine = here, here
        if dz:
            wall = wall_between(start_z, total_z, plane, dz)
            there = jnp.where(wall, -1, level_of(start_z, total_z, plane + dz))
            mine = jnp.where(wall, -1, here)
        solid[VEL[i]] = there < high_ref[side]
        way[VEL[i]] = mine >= own_ref[side]
    return solid, way


def drag_links(solid, way, scale):
    fluid = way[VEL[0]]
    return {
        i: jnp.where(fluid & solid[VEL[i]], 2.0 * scale * VEL[i][0], 0.0)
        for i in range(Q)
        if VEL[i][0] != 0
    }


def pushed(i, own, target, solid, way, links):
    value = jnp.where(way[VEL[i]], target, 0.0) + jnp.where(solid[VEL[i]], own, 0.0)
    return value + links[i] if i in links else value


def middle_kernel(
    total_z,
    scale,
    sens_scale,
    place_ref,
    smag_ref,
    state_ref,
    seed_ref,
    eddy_ref,
    x_ref,
    y_ref,
    z_ref,
    yz_ref,
    high_ref,
    own_ref,
    back_ref,
    columns_ref,
    sums_ref,
    post_main,
    tang_main,
    seed_main,
    post_y,
    tang_y,
    seed_y,
    post_x,
    tang_x,
    seed_x,
):
    smag = smag_ref[0]
    start_z = place_ref[0]
    rows, lanes = row_ids(), lane_ids()
    z_at = {key: at for at, key in enumerate(UP_Z)}
    per = COLS // (2 * DEPTH)

    def collide_into(pops, eddy, store):
        omega = relaxation(smag, eddy)
        away = departures(pops)
        heat = omega * omega * eddy
        for i in range(Q):
            store(i, pops[i] + omega * away[i], heat * away[i])

    def body(z, carry):
        def store(i, post, tang):
            post_main[i, z] = post
            tang_main[i, z] = tang

        collide_into([state_ref[i, z] for i in range(Q)], eddy_ref[z], store)
        for i in range(Q):
            seed_main[i, z] = seed_ref[i, z]
        return carry

    lax.fori_loop(0, DEPTH, body, 0)
    for k in (0, 1):

        def store(i, post, tang, k=k):
            post_main[i, DEPTH + k] = post
            tang_main[i, DEPTH + k] = tang

        collide_into(
            [z_ref[z_at[i, k]] for i in range(Q)], z_ref[z_at[2 * Q, k]], store
        )
        for i in range(Q):
            if (Q + i, k) in z_at:
                seed_main[i, DEPTH + k] = z_ref[z_at[Q + i, k]]

    def corner_rows(c):
        return turn(yz_ref[c // 2], -4 * (c % 2), 0)

    for k, tile in ((0, lambda c: y_ref[c]), (1, corner_rows)):

        def store(i, post, tang, k=k):
            post_y[i, k] = post
            tang_y[i, k] = tang

        collide_into([tile(i) for i in range(Q)], tile(2 * Q), store)
        for i in range(Q):
            seed_y[i, k] = tile(Q + i)

    n_strips = strips(N_UP)
    yx_tiles = [turn(y_ref[N_UP], -2 * v, 0) for v in range(n_strips)]
    yzx_tiles = [turn(yz_ref[-(-N_UP // 2)], -2 * v, 0) for v in range(n_strips)]

    def column_tile(c):
        v, at = c // per, 2 * DEPTH * (c % per)
        near = turn(x_ref[:, v * COLS : (v + 1) * COLS], -at, 1)
        above = turn(z_ref[len(UP_Z) + v], 8 - at, 1)
        near_rows = turn(yx_tiles[v], 16 - at, 1)
        above_rows = turn(yzx_tiles[v], 24 - at, 1)
        return jnp.where(
            lanes < 16,
            jnp.where(lanes < 8, near, above),
            jnp.where(lanes < 24, near_rows, above_rows),
        )

    def store(i, post, tang):
        post_x[i] = post
        tang_x[i] = tang

    collide_into([column_tile(i) for i in range(Q)], column_tile(2 * Q), store)
    for i in range(Q):
        seed_x[i] = column_tile(Q + i)

    def viewer(main, y_tiles, x_tiles, cache):
        def view(c, plane, dy, dx):
            key = (c, id(plane), dy, dx)
            if key in cache:
                return cache[key]
            tile = main[c, plane]
            if dx >= 0:
                tile = jnp.where(lanes <= dx, turn(x_tiles[c], -2 * plane, 1), tile)
            if dy >= 0:
                low = turn(y_tiles[c, plane // DEPTH], -2 * (plane % DEPTH), 0)
                if dx >= 0:
                    low = jnp.where(lanes <= dx, turn(x_tiles[c], -16 - 2 * plane, 1), low)
                tile = jnp.where(rows <= dy, low, tile)
            tile = turn(turn(tile, -dx, 1), -dy, 0)
            cache[key] = tile
            return tile

        return view

    def middle(z, carry):
        drag, sens = carry
        planes = {dz: z + 1 + dz for dz in (-1, 0, 1)}
        solid, way = masks_at(high_ref, own_ref, start_z, total_z, planes[0])
        links = drag_links(solid, way, scale)
        view_post = viewer(post_main, post_y, post_x, {})
        view_tang = viewer(tang_main, tang_y, tang_x, {})
        view_seed = viewer(seed_main, seed_y, seed_x, {})

        def pulled(view, i):
            dx, dy, dz = VEL[i]
            if i == 0:
                return view(0, planes[0], 0, 0)
            return jnp.where(
                solid[-dx, -dy, -dz],
                view(OPPOSITE[i], planes[0], 0, 0),
                view(i, planes[-dz], -dy, -dx),
            )

        f_one = [pulled(view_post, i) for i in range(Q)]
        cot = []
        for i in range(Q):
            dx, dy, dz = VEL[i]
            own = view_seed(OPPOSITE[i], planes[0], 0, 0)
            cot.append(pushed(i, own, view_seed(i, planes[dz], dy, dx), solid, way, links))

        own_plane = z + 1
        last = z == DEPTH - 1
        inside = eddy_ref[lax.rem(own_plane, DEPTH)]
        tile = jnp.where(last, z_ref[z_at[2 * Q, 0]], inside)
        columns = jnp.where(
            last,
            turn(z_ref[len(UP_Z) + 2 * Q // per], -2 * DEPTH * (2 * Q % per), 1),
            turn(
                x_ref[:, (2 * Q // per) * COLS : (2 * Q // per + 1) * COLS],
                -2 * DEPTH * (2 * Q % per) - 2 * own_plane,
                1,
            ),
        )
        low = jnp.where(
            last, corner_rows(2 * Q), turn(y_ref[2 * Q], -2 * lax.rem(own_plane, DEPTH), 0)
        )
        low_columns = jnp.where(
            last,
            turn(yzx_tiles[2 * Q // per], -2 * DEPTH * (2 * Q % per), 1),
            turn(yx_tiles[2 * Q // per], -2 * DEPTH * (2 * Q % per) - 2 * own_plane, 1),
        )
        tile = jnp.where(lanes == 0, columns, tile)
        low = jnp.where(lanes == 0, low_columns, low)
        eddy = jnp.where(rows == 0, low, tile)

        omega = relaxation(smag, eddy)
        adjoint, grad, away = collide_adjoint(f_one, omega, cot)
        for i in range(Q):
            back_ref[i, z] = adjoint[i]
        back_ref[Q, z] = grad
        for i in links:
            drag = drag + links[i] * (
                view_post(i, planes[0], 0, 0) + f_one[i] + omega * away[i]
            )
            sens = sens + links[i] * view_tang(i, planes[0], 0, 0)
        sens = sens + omega * omega * eddy * grad
        for i in range(Q):
            sens = sens + adjoint[i] * pulled(view_tang, i)
        return drag, sens

    zero = jnp.zeros((ROWS, COLS), jnp.float32)
    drag, sens = lax.fori_loop(0, DEPTH, middle, (zero, zero))
    both = jnp.where(
        lax.broadcasted_iota(jnp.int32, sums_ref.shape, 1) == 0,
        jnp.sum(drag),
        jnp.sum(sens) * sens_scale,
    )
    sums_ref[...] = both
    planes = [
        functools.partial(lambda c, z: back_ref[c, z], c, z)
        for c in range(N_BACK)
        for z in range(DEPTH)
    ]
    pack_columns(columns_ref, planes, COLS - 1)


def last_kernel(
    total_z,
    scale,
    place_ref,
    smag_ref,
    state_ref,
    eddy_ref,
    back_ref,
    x_ref,
    y_ref,
    z_ref,
    yz_ref,
    high_ref,
    own_ref,
    out_ref,
    grad_ref,
):
    smag = smag_ref[0]
    start_z = place_ref[0]
    rows, lanes = row_ids(), lane_ids()
    z_at = {key: at for at, key in enumerate(BACK_Z)}
    n_strips = strips(N_BACK)
    per = COLS // 2

    @functools.cache
    def strip(kind, v):
        if kind == "x":
            return x_ref[:, v * COLS : (v + 1) * COLS]
        if kind == "z":
            return z_ref[len(BACK_Z) + v]
        tile = y_ref[N_BACK] if kind == "y" else yz_ref[-(-N_BACK // 2)]
        return turn(tile, -2 * v - 1, 0)

    @functools.cache
    def columns(kind, c, layer):
        p = c * DEPTH + layer
        return turn(strip(kind, p // per), -2 * (p % per) - 1, 1)

    @functools.cache
    def view(c, plane, dy, dx):
        inner = plane >= 1
        layer = plane - 1 if inner else plane + 3
        tile = back_ref[c, layer] if inner else z_ref[z_at[c, layer]]

        def with_columns(tile, kind):
            if dx > 0:
                return tile
            keep = (lanes == 0) if dx == 0 else (lanes == 0) | (lanes == COLS - 1)
            return jnp.where(keep, columns(kind, c, layer), tile)

        tile = with_columns(tile, "x" if inner else "z")
        if dy <= 0:
            if inner:
                low = turn(y_ref[c], -2 * layer - 1, 0)
            else:
                low = turn(yz_ref[c // 2], -4 * (c % 2) - 2 * (layer - 2) - 1, 0)
            low = with_columns(low, "y" if inner else "yz")
            keep = (rows == 0) if dy == 0 else (rows == 0) | (rows == ROWS - 1)
            tile = jnp.where(keep, low, tile)
        return turn(turn(tile, -dx, 1), -dy, 0)

    for z in range(DEPTH):
        solid, way = masks_at(high_ref, own_ref, start_z, total_z, z)
        links = drag_links(solid, way, scale)
        cot = []
        for i in range(Q):
            dx, dy, dz = VEL[i]
            own = view(OPPOSITE[i], z, 0, 0)
            cot.append(pushed(i, own, view(i, z + dz, dy, dx), solid, way, links))
        omega = relaxation(smag, eddy_ref[z])
        adjoint, grad, _ = collide_adjoint([state_ref[i, z] for i in range(Q)], omega, cot)
        for i in range(Q):
            out_ref[i, z] = adjoint[i]
        grad_ref[z] = -3.0 * omega * omega * (grad + view(Q, z, 0, 0))


def plus_one(axis):
    count = lax.axis_size(axis)
    return [(i, (i + 1) % count) for i in range(count)]


def minus_one(axis):
    return [(target, source) for source, target in plus_one(axis)]


def pair_pairs(first, second):
    count = lax.axis_size("gz")
    return [(a * count + b, c * count + d) for a, c in first for b, d in second]


def heights_by_side(heights):
    total_y, total_x = heights.shape
    start_y = lax.axis_index("gy") * ROWS
    start_x = lax.axis_index("gx") * COLS
    padded = jnp.pad(heights, ((1, 2), (1, 2)), mode="wrap")
    near = lax.dynamic_slice(padded, (start_y, start_x), (ROWS + 3, COLS + 3))
    y = start_y - 1 + lax.broadcasted_iota(jnp.int32, near.shape, 0)
    x = start_x - 1 + lax.broadcasted_iota(jnp.int32, near.shape, 1)
    edge_y = (y == -1) | (y == total_y - 1)
    edge_x = (x == -1) | (x == total_x - 1)

    def cut(array, first, dy, dx):
        row, col = first + 1 + dy, first + 1 + dx
        return array[row : row + ROWS, col : col + COLS]

    out = []
    for first in (1, 0):
        high, own = [], []
        for dy, dx in SIDES:
            wall = jnp.zeros((ROWS, COLS), bool)
            if dy:
                wall = wall | cut(edge_y, first, min(dy, 0), 0)
            if dx:
                wall = wall | cut(edge_x, first, 0, min(dx, 0))
            high.append(jnp.where(wall, FAR, cut(near, first, dy, dx)))
            own.append(jnp.where(wall, FAR, cut(near, first, 0, 0)))
        for part in (high, own):
            stacked = jnp.stack(part)
            out.append(jnp.roll(stacked, (first, first), (1, 2)) if first else stacked)
    return out


def call(kernel, outs, n_scalars, operands, scratch=(), flops=0):
    specs = [
        pl.BlockSpec(memory_space=pltpu.SMEM if k < n_scalars else pltpu.VMEM)
        for k in range(len(operands))
    ]
    return pl.pallas_call(
        kernel,
        out_shape=[jax.ShapeDtypeStruct(shape, jnp.float32) for shape in outs],
        in_specs=specs,
        out_specs=[pl.BlockSpec(memory_space=pltpu.VMEM)] * len(outs),
        scratch_shapes=[pltpu.VMEM(shape, jnp.float32) for shape in scratch],
        compiler_params=pltpu.CompilerParams(vmem_limit_bytes=32 << 20),
        cost_estimate=pl.CostEstimate(flops=flops, bytes_accessed=1 << 20, transcendentals=0),
    )(*operands)


def total_over(axes, rows):
    parts = lax.all_to_all(rows, axes, split_axis=0, concat_axis=0, tiled=True)
    return jnp.sum(parts, 0, keepdims=True)


def on_device(state, adjoint_seed, eddy_rate, smag_coeff, heights):
    total_x = COLS * lax.axis_size("gx")
    total_y = ROWS * lax.axis_size("gy")
    total_z = DEPTH * lax.axis_size("gz")
    scale = 1.0 / (2.0 * UREF * total_x * total_y)
    sens_scale = -3.0 / math.sqrt(total_x * total_y * total_z)
    place = (lax.axis_index("gz") * DEPTH).astype(jnp.int32).reshape(1)
    smag = smag_coeff.reshape(1)
    mid_high, mid_own, end_high, end_own = heights_by_side(heights)

    tile = (ROWS, COLS)
    (columns,) = call(
        up_columns_kernel,
        [(ROWS, strips(N_UP) * COLS)],
        0,
        (state, adjoint_seed, eddy_rate),
    )
    columns = lax.ppermute(columns, "gx", minus_one("gx"))
    z_msg, y_msg, yz_msg = call(
        up_faces_kernel,
        [
            (len(UP_Z) + strips(N_UP), *tile),
            (N_UP + 1, *tile),
            (-(-N_UP // 2) + 1, *tile),
        ],
        0,
        (state, adjoint_seed, eddy_rate, columns),
    )
    z_msg = lax.ppermute(z_msg, "gz", minus_one("gz"))
    y_msg = lax.ppermute(y_msg, "gy", minus_one("gy"))
    yz_msg = lax.ppermute(yz_msg, ("gy", "gz"), pair_pairs(minus_one("gy"), minus_one("gz")))

    n_first = lax.axis_size("gy") * lax.axis_size("gz")
    back, back_columns, sums = call(
        functools.partial(middle_kernel, total_z, scale, sens_scale),
        [(N_BACK, DEPTH, *tile), (ROWS, strips(N_BACK) * COLS), (n_first, COLS)],
        2,
        (
            place,
            smag,
            state,
            adjoint_seed,
            eddy_rate,
            columns,
            y_msg,
            z_msg,
            yz_msg,
            mid_high,
            mid_own,
        ),
        [(Q, DEPTH + 2, *tile)] * 3 + [(Q, 2, *tile)] * 3 + [(Q, *tile)] * 3,
        flops=20_000_000,
    )
    back_columns = lax.ppermute(back_columns, "gx", plus_one("gx"))
    sums = total_over(("gy", "gz"), sums)
    z_msg, y_msg, yz_msg = call(
        back_faces_kernel,
        [
            (len(BACK_Z) + strips(N_BACK), *tile),
            (N_BACK + 1, *tile),
            (-(-N_BACK // 2) + 1, *tile),
        ],
        0,
        (back, back_columns),
    )
    z_msg = lax.ppermute(z_msg, "gz", plus_one("gz"))
    y_msg = lax.ppermute(y_msg, "gy", plus_one("gy"))
    yz_msg = lax.ppermute(yz_msg, ("gy", "gz"), pair_pairs(plus_one("gy"), plus_one("gz")))
    sums = total_over(("gx",), jnp.broadcast_to(sums, (lax.axis_size("gx"), COLS)))
    adjoint_state, gradient = call(
        functools.partial(last_kernel, total_z, scale),
        [(Q, DEPTH, *tile), (DEPTH, *tile)],
        2,
        (
            place,
            smag,
            state,
            eddy_rate,
            back,
            back_columns,
            y_msg,
            z_msg,
            yz_msg,
            end_high,
            end_own,
        ),
        flops=20_000_000,
    )
    return adjoint_state, gradient, sums[0, :2]


def solution(mesh):
    return jax.shard_map(
        on_device,
        mesh=mesh,
        in_specs=(
            P(None, "gz", "gy", "gx"),
            P(None, "gz", "gy", "gx"),
            P("gz", "gy", "gx"),
            P(),
            P(),
        ),
        out_specs=(P(None, "gz", "gy", "gx"), P("gz", "gy", "gx"), P()),
        check_vma=False,
    )
```

```python
import functools
import math

import jax
import jax.numpy as jnp
from jax import lax
from jax.experimental import pallas as pl
from jax.experimental.pallas import tpu as pltpu
from jax.sharding import PartitionSpec as P

VEL = [
    (0, 0, 0),
    (1, 0, 0),
    (-1, 0, 0),
    (0, 1, 0),
    (0, -1, 0),
    (0, 0, 1),
    (0, 0, -1),
    (1, 1, 0),
    (-1, -1, 0),
    (1, -1, 0),
    (-1, 1, 0),
    (1, 0, 1),
    (-1, 0, -1),
    (1, 0, -1),
    (-1, 0, 1),
    (0, 1, 1),
    (0, -1, -1),
    (0, 1, -1),
    (0, -1, 1),
]
OPPOSITE = [0, 2, 1, 4, 3, 6, 5, 8, 7, 10, 9, 12, 11, 14, 13, 16, 15, 18, 17]
LATTICE_WEIGHTS = [1.0 / 3.0] + [1.0 / 18.0] * 6 + [1.0 / 36.0] * 12
UREF = 0.08
NU_BASE = 0.004
Q = 19
DEPTH = 4
ROWS = 8
COLS = 128
FAR = 1 << 20
SIDES = [(dy, dx) for dy in (-1, 0, 1) for dx in (-1, 0, 1)]

LAYER = [("f", i) for i in range(Q)] + [("e", 0)] + [("g", i) for i in range(Q)]
BACK = [("a", i) for i in range(Q)] + [("d", 0)]
FIELDS = [(name, i) for name in "ptg" for i in range(Q)] + [("e", 0)]


def crossing_items(axes, back):
    down = [i for i in range(Q) if all(VEL[i][a] == -1 for a in axes)]
    if back:
        return [("a", i) for i in down]
    up = [i for i in range(Q) if all(VEL[i][a] == 1 for a in axes)]
    return [(name, i) for i in down for name in "pt"] + [("g", i) for i in up]


def face_plan(back):
    near = BACK if back else LAYER
    vertical = [(item, 0) for item in near] + [(item, 1) for item in crossing_items([2], back)]
    spanwise = [(item, z, 0) for item in near for z in range(DEPTH)]
    spanwise += [(item, z, 1) for item in crossing_items([1], back) for z in range(DEPTH)]
    corner = [(item, 0, 0) for item in near]
    corner += [(item, 0, 1) for item in crossing_items([1], back)]
    corner += [(item, 1, 0) for item in crossing_items([2], back)]
    corner += [(item, 1, 1) for item in crossing_items([1, 2], back)]
    return vertical, spanwise, corner


def places(keys):
    return {key: at for at, key in enumerate(keys)}


def tiles_of(keys):
    return -(-len(keys) // ROWS)


PLANS = {back: face_plan(back) for back in (False, True)}
PLACES = {back: [places(keys) for keys in PLANS[back]] for back in (False, True)}


def strips(back):
    return -(-len(BACK if back else LAYER) * DEPTH * 2 // COLS)


def face_shapes(back):
    vertical, spanwise, corner = PLANS[back]
    return [
        (len(vertical) + strips(back), ROWS, COLS),
        (tiles_of(spanwise) + 1, ROWS, COLS),
        (tiles_of(corner) + 1, ROWS, COLS),
    ]


def signed(terms):
    total = None
    for factor, value in terms:
        if factor == 0:
            continue
        piece = value if factor == 1 else (-value if factor == -1 else factor * value)
        total = piece if total is None else total + piece
    return total


def along(idx, vec):
    return signed([(VEL[idx][axis], vec[axis]) for axis in range(3)])


def flow(pops):
    rho = signed([(1, p) for p in pops])
    inverse = 1.0 / rho
    vel = [signed([(VEL[i][axis], pops[i]) for i in range(Q)]) * inverse for axis in range(3)]
    return rho, vel


def shapes(vel):
    base = 1.0 - 1.5 * (vel[0] * vel[0] + vel[1] * vel[1] + vel[2] * vel[2])
    out = [base] + [None] * (Q - 1)
    for i in range(1, Q, 2):
        cu = along(i, vel)
        even = base + 4.5 * cu * cu
        out[i] = even + 3.0 * cu
        out[i + 1] = even - 3.0 * cu
    return out


def departures(pops):
    rho, vel = flow(pops)
    shape = shapes(vel)
    return [LATTICE_WEIGHTS[i] * rho * shape[i] - pops[i] for i in range(Q)]


def collide_adjoint(pops, omega, cot):
    rho, vel = flow(pops)
    shape = shapes(vel)
    weighted = [LATTICE_WEIGHTS[i] * cot[i] for i in range(Q)]
    level = signed([(1, weighted[i] * shape[i]) for i in range(Q)])
    mass = signed([(1, w) for w in weighted])
    first = [signed([(VEL[i][axis], weighted[i]) for i in range(Q)]) for axis in range(3)]

    def second(a, b):
        return signed([(VEL[i][a] * VEL[i][b], weighted[i]) for i in range(Q)])

    pair = {(a, b): second(a, b) for a in range(3) for b in range(a, 3)}
    slope = []
    for a in range(3):
        mixed = signed([(1, pair[min(a, b), max(a, b)] * vel[b]) for b in range(3)])
        slope.append(3.0 * first[a] + 9.0 * mixed - 3.0 * mass * vel[a])
    base = omega * (level - (slope[0] * vel[0] + slope[1] * vel[1] + slope[2] * vel[2]))
    tilt = [omega * s for s in slope]
    keep = 1.0 - omega
    adjoint = []
    for i in range(Q):
        part = along(i, tilt)
        adjoint.append(keep * cot[i] + (base if part is None else base + part))
    away = [LATTICE_WEIGHTS[i] * rho * shape[i] - pops[i] for i in range(Q)]
    grad = signed([(1, cot[i] * away[i]) for i in range(Q)])
    return adjoint, grad, away


def relaxation(smag, eddy):
    return 1.0 / (0.5 + 3.0 * (NU_BASE + smag * eddy))


def row_ids():
    return lax.broadcasted_iota(jnp.int32, (ROWS, COLS), 0)


def lane_ids():
    return lax.broadcasted_iota(jnp.int32, (ROWS, COLS), 1)


def turn(tile, amount, axis):
    size = tile.shape[axis]
    if isinstance(amount, int):
        amount %= size
        return tile if amount == 0 else pltpu.roll(tile, amount, axis)
    return pltpu.roll(tile, lax.rem(amount + size, size), axis)


def pack_columns(out_ref, planes, start):
    lanes = lane_ids()
    per = COLS // 2
    for strip in range(-(-len(planes) // per)):
        total = None
        for j, plane in enumerate(planes[strip * per : (strip + 1) * per]):
            moved = turn(plane(), 2 * j - start, 1)
            total = moved if total is None else jnp.where(lanes >= 2 * j, moved, total)
        out_ref[:, strip * COLS : (strip + 1) * COLS] = total


def pack_rows(pieces):
    rows = row_ids()
    total = None
    for j, (piece, row) in enumerate(pieces):
        moved = turn(piece, j - row, 0)
        total = moved if total is None else jnp.where(rows >= j, moved, total)
    return total


def pack_planes(back, plane, x_ref, z_ref):
    vertical = PLANS[back][0]
    for at, (item, layer) in enumerate(vertical):
        z_ref[at] = plane(item, DEPTH - 1 - layer if back else layer)
    for v in range(strips(back)):
        z_ref[len(vertical) + v] = x_ref[:, v * COLS : (v + 1) * COLS]


def pack_border(keys, plane, row_at, x_ref, out_ref):
    columns = [x_ref[:, v * COLS : (v + 1) * COLS] for v in range(x_ref.shape[1] // COLS)]
    for at in range(0, len(keys), ROWS):
        out_ref[at // ROWS] = pack_rows(
            [(plane(item, z), row_at[r]) for item, z, r in keys[at : at + ROWS]]
        )
    out_ref[tiles_of(keys)] = pack_rows([(tile, row_at[r]) for tile in columns for r in (0, 1)])


def fetch_kernel(
    state_ref, seed_ref, eddy_ref, state_out, seed_out, eddy_out, columns_ref, sems
):
    copies = [
        pltpu.make_async_copy(src, dst, sems.at[k])
        for k, (src, dst) in enumerate(
            ((state_ref, state_out), (eddy_ref, eddy_out), (seed_ref, seed_out))
        )
    ]
    for copy in copies:
        copy.start()
    for copy in copies:
        copy.wait()
    planes = (
        [functools.partial(lambda i, z: state_out[i, z], i, z) for i in range(Q) for z in range(DEPTH)]
        + [functools.partial(lambda z: eddy_out[z], z) for z in range(DEPTH)]
        + [functools.partial(lambda i, z: seed_out[i, z], i, z) for i in range(Q) for z in range(DEPTH)]
    )
    pack_columns(columns_ref, planes, 0)


def collide_fields(smag, pops, eddy):
    omega = relaxation(smag, eddy)
    away = departures(pops)
    heat = omega * omega * eddy
    post = [pops[i] + omega * away[i] for i in range(Q)]
    return post, [heat * away[i] for i in range(Q)]


def first_kernel(
    total_y, total_x, place_ref, smag_ref, state_ref, eddy_ref, near_ref, post_ref, tang_ref, high_ref, own_ref
):
    smag = smag_ref[0]
    for z in range(DEPTH):
        post, tang = collide_fields(smag, [state_ref[i, z] for i in range(Q)], eddy_ref[z])
        for i in range(Q):
            post_ref[i, z] = post[i]
            tang_ref[i, z] = tang[i]
    rows, lanes = row_ids(), lane_ids()
    start_y, start_x = place_ref[1], place_ref[2]

    @functools.cache
    def cut(row, col):
        left, right = near_ref[row : row + ROWS, :COLS], near_ref[row : row + ROWS, COLS:]
        if col == 0:
            return left
        return jnp.where(lanes < COLS - col, turn(left, -col, 1), turn(right, -col, 1))

    for k, first in enumerate((1, 0)):
        for side, (dy, dx) in enumerate(SIDES):
            high = cut(first + 1 + dy, first + 1 + dx)
            own = cut(first + 1, first + 1)
            if dy:
                y = start_y + first + min(dy, 0) + rows
                wall = (y == -1) | (y == total_y - 1)
                high, own = jnp.where(wall, FAR, high), jnp.where(wall, FAR, own)
            if dx:
                x = start_x + first + min(dx, 0) + lanes
                wall = (x == -1) | (x == total_x - 1)
                high, own = jnp.where(wall, FAR, high), jnp.where(wall, FAR, own)
            high_ref[k, side] = turn(turn(high, first, 0), first, 1)
            own_ref[k, side] = turn(turn(own, first, 0), first, 1)


def up_plane(state_ref, seed_ref, eddy_ref, post_ref, tang_ref):
    fields = {"f": state_ref, "g": seed_ref, "p": post_ref, "t": tang_ref}

    def plane(item, z):
        name, i = item
        return eddy_ref[z] if name == "e" else fields[name][i, z]

    return plane


def up_faces_kernel(
    state_ref, seed_ref, eddy_ref, post_ref, tang_ref, x_ref, z_ref, y_ref, yz_ref
):
    plane = up_plane(state_ref, seed_ref, eddy_ref, post_ref, tang_ref)
    pack_planes(False, plane, x_ref, z_ref)
    pack_border(PLANS[False][1], plane, (0, 1), x_ref, y_ref)
    pack_border(PLANS[False][2], plane, (0, 1), x_ref, yz_ref)


def back_rows_kernel(back_ref, x_ref, y_ref):
    def plane(item, z):
        return back_ref[BACK.index(item), z]

    pack_border(PLANS[True][1], plane, (0, ROWS - 1), x_ref, y_ref)


def back_planes_kernel(back_ref, x_ref, y_ref, z_ref):
    pack_planes(True, lambda item, z: back_ref[BACK.index(item), z], x_ref, z_ref)
    vertical, _, corner = PLANS[True]
    y_at = PLACES[True][1]
    first = len(vertical) + strips(True)
    for at in range(0, len(corner), ROWS):
        spots = [y_at[item, DEPTH - 1 - layer, r] for item, layer, r in corner[at : at + ROWS]]
        z_ref[first + at // ROWS] = pack_rows([(y_ref[k // ROWS], k % ROWS) for k in spots])
    z_ref[first + tiles_of(corner)] = y_ref[tiles_of(y_at)]


def level_of(start_z, total_z, plane):
    level = start_z + plane
    return lax.rem(level + total_z, total_z)


def wall_between(start_z, total_z, plane, step):
    upper = start_z + plane + (1 if step > 0 else 0)
    return (upper == total_z) | (upper == 0)


def masks_at(high_ref, own_ref, frame, start_z, total_z, plane):
    solid, way = {}, {}
    here = level_of(start_z, total_z, plane)
    for i in range(Q):
        dx, dy, dz = VEL[i]
        side = SIDES.index((dy, dx))
        there, mine = here, here
        if dz:
            wall = wall_between(start_z, total_z, plane, dz)
            there = jnp.where(wall, -1, level_of(start_z, total_z, plane + dz))
            mine = jnp.where(wall, -1, here)
        solid[VEL[i]] = there < high_ref[frame, side]
        way[VEL[i]] = mine >= own_ref[frame, side]
    return solid, way


def drag_links(solid, way, scale):
    fluid = way[VEL[0]]
    return {
        i: jnp.where(fluid & solid[VEL[i]], 2.0 * scale * VEL[i][0], 0.0)
        for i in range(Q)
        if VEL[i][0] != 0
    }


def pushed(i, own, target, solid, way, links):
    value = jnp.where(way[VEL[i]], target, 0.0) + jnp.where(solid[VEL[i]], own, 0.0)
    return value + links[i] if i in links else value


def middle_kernel(
    total_z,
    scale,
    sens_scale,
    place_ref,
    smag_ref,
    post_ref,
    tang_ref,
    seed_ref,
    eddy_ref,
    x_ref,
    y_ref,
    z_ref,
    yz_ref,
    high_ref,
    own_ref,
    back_ref,
    columns_ref,
    sums_ref,
    main,
    y_tiles,
    x_tiles,
):
    smag = smag_ref[0]
    start_z = place_ref[0]
    rows, lanes = row_ids(), lane_ids()
    z_at, y_at, yz_at = PLACES[False]
    per = COLS // (2 * DEPTH)
    pops_items = [("f", i) for i in range(Q)]

    def collided(tile):
        post, tang = collide_fields(smag, [tile(item) for item in pops_items], tile(("e", 0)))
        out = {("p", i): post[i] for i in range(Q)}
        out.update({("t", i): tang[i] for i in range(Q)})
        out.update({item: tile(item) for item in LAYER if item[0] in "eg"})
        return out

    above = collided(lambda item: z_ref[z_at[item, 0]])

    def copy_planes(z, carry):
        for ref, first in ((post_ref, 0), (tang_ref, Q), (seed_ref, 2 * Q)):
            for i in range(Q):
                main[first + i, z] = ref[i, z]
        main[3 * Q, z] = eddy_ref[z]
        return carry

    lax.fori_loop(0, DEPTH, copy_planes, 0)
    for at, item in enumerate(FIELDS):
        main[at, DEPTH] = above[item]
        if (item, 1) in z_at:
            main[at, DEPTH + 1] = z_ref[z_at[item, 1]]

    def y_piece(key, row):
        at = y_at[key]
        return turn(y_ref[at // ROWS], row - at % ROWS, 0)

    def yz_piece(key, row):
        at = yz_at[key]
        return turn(yz_ref[at // ROWS], row - at % ROWS, 0)

    y_near = collided(lambda item: y_piece((item, 0, 0), 0))
    y_above = collided(lambda item: yz_piece((item, 0, 0), 0))

    for at, item in enumerate(FIELDS):
        tile = y_near[item]
        if (item, 0, 1) in y_at:
            tile = jnp.where(rows < DEPTH, tile, y_piece((item, 0, 1), DEPTH))
        y_tiles[at, 0] = tile
        tile = y_above[item]
        for z, r in ((1, 0), (0, 1), (1, 1)):
            if (item, z, r) in yz_at:
                row = DEPTH * r + z
                tile = jnp.where(rows == row, yz_piece((item, z, r), row), tile)
        y_tiles[at, 1] = tile

    n_strips = strips(False)
    yx_tiles = [turn(y_ref[tiles_of(y_at)], -2 * v, 0) for v in range(n_strips)]
    yzx_tiles = [turn(yz_ref[tiles_of(yz_at)], -2 * v, 0) for v in range(n_strips)]

    def column_tile(item):
        v, at = divmod(LAYER.index(item), per)
        at *= 2 * DEPTH
        near = turn(x_ref[:, v * COLS : (v + 1) * COLS], -at, 1)
        high = turn(z_ref[len(z_at) + v], 8 - at, 1)
        near_rows = turn(yx_tiles[v], 16 - at, 1)
        high_rows = turn(yzx_tiles[v], 24 - at, 1)
        return jnp.where(
            lanes < 16,
            jnp.where(lanes < 8, near, high),
            jnp.where(lanes < 24, near_rows, high_rows),
        )

    sides = collided(column_tile)
    for at, item in enumerate(FIELDS):
        x_tiles[at] = sides[item]

    def viewer(plane_of):
        @functools.cache
        def view(item, dz, dy, dx):
            at, plane = FIELDS.index(item), plane_of[dz]
            tile = main[at, plane]
            if dx >= 0:
                tile = jnp.where(lanes <= dx, turn(x_tiles[at], -2 * plane, 1), tile)
            if dy >= 0:
                k = plane // DEPTH
                z = plane - k * DEPTH
                low = turn(y_tiles[at, k], -z, 0)
                if dy == 1:
                    low = jnp.where(rows == 0, low, turn(y_tiles[at, k], 1 - DEPTH - z, 0))
                if dx >= 0:
                    low = jnp.where(lanes <= dx, turn(x_tiles[at], -2 * plane - 16, 1), low)
                tile = jnp.where(rows <= dy, low, tile)
            return turn(turn(tile, -dx, 1), -dy, 0)

        return view

    def step(z, carry):
        drag, sens = carry
        plane = z + 1
        view = viewer({dz: plane + dz for dz in (-1, 0, 1)})
        solid, way = masks_at(high_ref, own_ref, 0, start_z, total_z, plane)
        links = drag_links(solid, way, scale)

        def pulled(name, i):
            dx, dy, dz = VEL[i]
            away = view((name, i), -dz, -dy, -dx)
            if i == 0:
                return away
            return jnp.where(solid[-dx, -dy, -dz], view((name, OPPOSITE[i]), 0, 0, 0), away)

        f_one = [pulled("p", i) for i in range(Q)]
        cot = []
        for i in range(Q):
            dx, dy, dz = VEL[i]
            own = view(("g", OPPOSITE[i]), 0, 0, 0)
            cot.append(pushed(i, own, view(("g", i), dz, dy, dx), solid, way, links))
        eddy = view(("e", 0), 0, 0, 0)
        omega = relaxation(smag, eddy)
        adjoint, grad, away = collide_adjoint(f_one, omega, cot)
        for i in range(Q):
            back_ref[i, z] = adjoint[i]
        back_ref[Q, z] = grad
        for i in links:
            drag = drag + links[i] * (view(("p", i), 0, 0, 0) + f_one[i] + omega * away[i])
            sens = sens + links[i] * view(("t", i), 0, 0, 0)
        sens = sens + omega * omega * eddy * grad
        for i in range(Q):
            sens = sens + adjoint[i] * pulled("t", i)
        return drag, sens

    zero = jnp.zeros((ROWS, COLS), jnp.float32)
    drag, sens = lax.fori_loop(0, DEPTH, step, (zero, zero))
    sums_ref[...] = jnp.where(
        lax.broadcasted_iota(jnp.int32, sums_ref.shape, 1) == 0,
        jnp.sum(drag),
        jnp.sum(sens) * sens_scale,
    )
    planes = [
        functools.partial(lambda c, z: back_ref[c, z], c, z)
        for c in range(len(BACK))
        for z in range(DEPTH)
    ]
    pack_columns(columns_ref, planes, COLS - 1)


def last_kernel(
    total_z,
    scale,
    place_ref,
    smag_ref,
    state_ref,
    eddy_ref,
    back_ref,
    x_ref,
    y_ref,
    z_ref,
    high_ref,
    own_ref,
    out_ref,
    grad_ref,
    main,
    low_rows,
    strip_tiles,
):
    smag = smag_ref[0]
    start_z = place_ref[0]
    rows, lanes = row_ids(), lane_ids()
    z_at, y_at, yz_at = PLACES[True]
    yz_ref = z_ref.at[pl.ds(len(z_at) + strips(True), tiles_of(yz_at) + 1)]
    per = COLS // 2 // DEPTH

    def copy_planes(z, carry):
        for at in range(len(BACK)):
            main[at, z + 2] = back_ref[at, z]
        return carry

    lax.fori_loop(0, DEPTH, copy_planes, 0)
    for at, item in enumerate(BACK):
        for plane in range(-1, DEPTH + 1):
            if plane >= 1:
                places_of, ref, layer = y_at, y_ref, plane - 1
            else:
                places_of, ref, layer = yz_at, yz_ref, -plane
                if (item, layer) in z_at:
                    main[at, plane + 1] = z_ref[z_at[item, layer]]
            low = None
            for r, row in ((0, 0), (1, ROWS - 1)):
                if (item, layer, r) in places_of:
                    k = places_of[item, layer, r]
                    piece = turn(ref[k // ROWS], row - k % ROWS, 0)
                    low = piece if low is None else jnp.where(rows == 0, low, piece)
            if low is not None:
                low_rows[at, plane + 1] = low
    for v in range(strips(True)):
        strip_tiles[0, v] = x_ref[:, v * COLS : (v + 1) * COLS]
        strip_tiles[1, v] = z_ref[len(z_at) + v]
        for k, tile in ((2, y_ref[tiles_of(y_at)]), (3, yz_ref[tiles_of(yz_at)])):
            first = turn(tile, -2 * v, 0)
            strip_tiles[k, v] = jnp.where(rows == 0, first, turn(first, -2, 0))

    def step(z, carry):
        @functools.cache
        def view(item, dz, dy, dx):
            at, plane = BACK.index(item), z + dz
            lower = jnp.where(plane >= 1, 0, 1)
            layer = lax.rem(plane + DEPTH - 1, DEPTH)
            shift = -2 * (DEPTH * (at % per) + layer) - 1
            keep = (lanes == 0) if dx == 0 else (lanes == 0) | (lanes == COLS - 1)

            def with_columns(tile, kind):
                if dx > 0:
                    return tile
                return jnp.where(keep, turn(strip_tiles[kind + lower, at // per], shift, 1), tile)

            tile = with_columns(main[at, plane + 1], 0)
            if dy <= 0:
                low = with_columns(low_rows[at, plane + 1], 2)
                edge = (rows == 0) if dy == 0 else (rows == 0) | (rows == ROWS - 1)
                tile = jnp.where(edge, low, tile)
            return turn(turn(tile, -dx, 1), -dy, 0)

        solid, way = masks_at(high_ref, own_ref, 1, start_z, total_z, z)
        links = drag_links(solid, way, scale)
        cot = []
        for i in range(Q):
            dx, dy, dz = VEL[i]
            own = view(("a", OPPOSITE[i]), 0, 0, 0)
            cot.append(pushed(i, own, view(("a", i), dz, dy, dx), solid, way, links))
        omega = relaxation(smag, eddy_ref[z])
        adjoint, grad, _ = collide_adjoint([state_ref[i, z] for i in range(Q)], omega, cot)
        for i in range(Q):
            out_ref[i, z] = adjoint[i]
        grad_ref[z] = -3.0 * omega * omega * (grad + view(("d", 0), 0, 0, 0))
        return carry

    lax.fori_loop(0, DEPTH, step, 0)


def plus_one(axis):
    count = lax.axis_size(axis)
    return [(i, (i + 1) % count) for i in range(count)]


def minus_one(axis):
    return [(target, source) for source, target in plus_one(axis)]


def pair_pairs(first, second):
    count = lax.axis_size("gz")
    return [(a * count + b, c * count + d) for a, c in first for b, d in second]


def heights_near(heights):
    padded = jnp.pad(heights, ((1, 2), (1, 2)), mode="wrap")
    start = (lax.axis_index("gy") * ROWS, lax.axis_index("gx") * COLS)
    near = lax.dynamic_slice(padded, start, (ROWS + 3, COLS + 3))
    return jnp.pad(near, ((0, ROWS - 3), (0, COLS - 3)))


def call(kernel, outs, operands, scalars=0, far=False, scratch=(), flops=0):
    def kind(k):
        if k < scalars:
            return pltpu.SMEM
        return pltpu.HBM if far else pltpu.VMEM

    outs = [out if isinstance(out[-1], type) else (out, jnp.float32) for out in outs]
    return pl.pallas_call(
        kernel,
        out_shape=[jax.ShapeDtypeStruct(*out) for out in outs],
        in_specs=[pl.BlockSpec(memory_space=kind(k)) for k in range(len(operands))],
        out_specs=[pl.BlockSpec(memory_space=pltpu.VMEM)] * len(outs),
        scratch_shapes=list(scratch),
        compiler_params=pltpu.CompilerParams(vmem_limit_bytes=32 << 20),
        cost_estimate=pl.CostEstimate(flops=flops, bytes_accessed=1 << 20, transcendentals=0),
    )(*operands)


def exchange_faces(messages, step):
    vertical, spanwise, corner = messages
    vertical = lax.ppermute(vertical, "gz", step("gz"))
    spanwise = lax.ppermute(spanwise, "gy", step("gy"))
    corner = lax.ppermute(corner, ("gy", "gz"), pair_pairs(step("gy"), step("gz")))
    return vertical, spanwise, corner


def on_device(state, adjoint_seed, eddy_rate, smag_coeff, heights):
    total_x = COLS * lax.axis_size("gx")
    total_y = ROWS * lax.axis_size("gy")
    total_z = DEPTH * lax.axis_size("gz")
    scale = 1.0 / (2.0 * UREF * total_x * total_y)
    sens_scale = -3.0 / math.sqrt(total_x * total_y * total_z)
    tile = (ROWS, COLS)
    place = jnp.stack(
        [
            lax.axis_index("gz") * DEPTH,
            lax.axis_index("gy") * ROWS,
            lax.axis_index("gx") * COLS,
        ]
    ).astype(jnp.int32)
    smag = smag_coeff.reshape(1)
    block = state.shape
    layer = eddy_rate.shape

    state, seed, eddy, columns = call(
        fetch_kernel,
        [block, block, layer, (ROWS, strips(False) * COLS)],
        (state, adjoint_seed, eddy_rate),
        far=True,
        scratch=[pltpu.SemaphoreType.DMA((3,))],
    )
    columns = lax.ppermute(columns, "gx", minus_one("gx"))
    beside = ((2, len(SIDES), ROWS, COLS), jnp.int32)
    post, tang, high, own = call(
        functools.partial(first_kernel, total_y, total_x),
        [block, block, beside, beside],
        (place, smag, state, eddy, heights_near(heights)),
        scalars=2,
        flops=8_000_000,
    )
    messages = call(
        up_faces_kernel, face_shapes(False), (state, seed, eddy, post, tang, columns)
    )
    vertical, spanwise, corner = exchange_faces(messages, minus_one)
    n_first = lax.axis_size("gy") * lax.axis_size("gz")
    back, back_columns, sums = call(
        functools.partial(middle_kernel, total_z, scale, sens_scale),
        [(len(BACK), *layer), (ROWS, strips(True) * COLS), (n_first, COLS)],
        (place, smag, post, tang, seed, eddy, columns, spanwise, vertical, corner, high, own),
        scalars=2,
        scratch=[
            pltpu.VMEM(shape, jnp.float32)
            for shape in (
                (len(FIELDS), DEPTH + 2, ROWS, COLS),
                (len(FIELDS), 2, ROWS, COLS),
                (len(FIELDS), ROWS, COLS),
            )
        ],
        flops=20_000_000,
    )
    back_columns = lax.ppermute(back_columns, "gx", plus_one("gx"))
    sums = lax.all_to_all(sums, ("gy", "gz"), split_axis=0, concat_axis=0, tiled=True)
    shape_z, shape_y, shape_yz = face_shapes(True)
    (spanwise,) = call(back_rows_kernel, [shape_y], (back, back_columns))
    spanwise = lax.ppermute(spanwise, "gy", plus_one("gy"))
    (vertical,) = call(
        back_planes_kernel,
        [(shape_z[0] + shape_yz[0], *tile)],
        (back, back_columns, spanwise),
    )
    vertical, sums = lax.optimization_barrier((vertical, sums))
    vertical = lax.ppermute(vertical, "gz", plus_one("gz"))
    sums = jnp.broadcast_to(jnp.sum(sums, 0, keepdims=True), (lax.axis_size("gx"), COLS))
    sums = lax.all_to_all(sums, "gx", split_axis=0, concat_axis=0, tiled=True)
    adjoint_state, gradient = call(
        functools.partial(last_kernel, total_z, scale),
        [block, layer],
        (place, smag, state, eddy, back, back_columns, spanwise, vertical, high, own),
        scalars=2,
        scratch=[
            pltpu.VMEM(shape, jnp.float32)
            for shape in (
                (len(BACK), DEPTH + 2, ROWS, COLS),
                (len(BACK), DEPTH + 2, ROWS, COLS),
                (4, strips(True), ROWS, COLS),
            )
        ],
        flops=20_000_000,
    )
    gradient, sums = lax.optimization_barrier((gradient, sums))
    return adjoint_state, gradient, jnp.sum(sums[:, :2], 0)


def solution(mesh):
    return jax.shard_map(
        on_device,
        mesh=mesh,
        in_specs=(
            P(None, "gz", "gy", "gx"),
            P(None, "gz", "gy", "gx"),
            P("gz", "gy", "gx"),
            P(),
            P(),
        ),
        out_specs=(P(None, "gz", "gy", "gx"), P("gz", "gy", "gx"), P()),
        check_vma=False,
    )
```

```python
import functools
import math

import jax
import jax.numpy as jnp
from jax import lax
from jax.experimental import pallas as pl
from jax.experimental.pallas import tpu as pltpu
from jax.sharding import PartitionSpec as P

VEL = [
    (0, 0, 0),
    (1, 0, 0),
    (-1, 0, 0),
    (0, 1, 0),
    (0, -1, 0),
    (0, 0, 1),
    (0, 0, -1),
    (1, 1, 0),
    (-1, -1, 0),
    (1, -1, 0),
    (-1, 1, 0),
    (1, 0, 1),
    (-1, 0, -1),
    (1, 0, -1),
    (-1, 0, 1),
    (0, 1, 1),
    (0, -1, -1),
    (0, 1, -1),
    (0, -1, 1),
]
OPPOSITE = [0, 2, 1, 4, 3, 6, 5, 8, 7, 10, 9, 12, 11, 14, 13, 16, 15, 18, 17]
LATTICE_WEIGHTS = [1.0 / 3.0] + [1.0 / 18.0] * 6 + [1.0 / 36.0] * 12
UREF = 0.08
NU_BASE = 0.004
Q = 19
DEPTH = 4
ROWS = 8
COLS = 128
FAR = 1 << 20
SIDES = [(dy, dx) for dy in (-1, 0, 1) for dx in (-1, 0, 1)]

LAYER = [("f", i) for i in range(Q)] + [("g", i) for i in range(Q)] + [("e", 0)]
BACK = [("a", i) for i in range(Q)] + [("d", 0)]
FIELDS = [(name, i) for name in "ptg" for i in range(Q)] + [("e", 0)]


def crossing_items(axes, back):
    down = [i for i in range(Q) if all(VEL[i][a] == -1 for a in axes)]
    if back:
        return [("a", i) for i in down]
    up = [i for i in range(Q) if all(VEL[i][a] == 1 for a in axes)]
    return [(name, i) for i in down for name in "pt"] + [("g", i) for i in up]


def face_plan(back):
    near = BACK if back else LAYER
    vertical = [(item, 0) for item in near] + [(item, 1) for item in crossing_items([2], back)]
    spanwise = [(item, z, 0) for item in near for z in range(DEPTH)]
    spanwise += [(item, z, 1) for item in crossing_items([1], back) for z in range(DEPTH)]
    corner = [(item, 0, 0) for item in near]
    corner += [(item, 0, 1) for item in crossing_items([1], back)]
    corner += [(item, 1, 0) for item in crossing_items([2], back)]
    corner += [(item, 1, 1) for item in crossing_items([1, 2], back)]
    return vertical, spanwise, corner


def places(keys):
    return {key: at for at, key in enumerate(keys)}


def early_and_rest():
    vertical = PLANS[False][0]
    return [k for k in vertical if is_early(k)], [k for k in vertical if not is_early(k)]


def tiles_of(keys):
    return -(-len(keys) // ROWS)


def is_early(key):
    return key[0][0] in "fg"


PLANS = {back: face_plan(back) for back in (False, True)}
PLACES = {back: [places(keys) for keys in PLANS[back]] for back in (False, True)}


def strips(back):
    return -(-len(BACK if back else LAYER) * DEPTH * 2 // COLS)


def face_shapes(back):
    vertical, spanwise, corner = PLANS[back]
    planes = vertical if back else early_and_rest()[1]
    return [
        (len(planes) + strips(back), ROWS, COLS),
        (tiles_of(spanwise) + 1, ROWS, COLS),
        (tiles_of(corner) + 1, ROWS, COLS),
    ]


def signed(terms):
    total = None
    for factor, value in terms:
        if factor == 0:
            continue
        piece = value if factor == 1 else (-value if factor == -1 else factor * value)
        total = piece if total is None else total + piece
    return total


def along(idx, vec):
    return signed([(VEL[idx][axis], vec[axis]) for axis in range(3)])


def flow(pops):
    rho = signed([(1, p) for p in pops])
    inverse = 1.0 / rho
    vel = [signed([(VEL[i][axis], pops[i]) for i in range(Q)]) * inverse for axis in range(3)]
    return rho, vel


def shapes(vel):
    base = 1.0 - 1.5 * (vel[0] * vel[0] + vel[1] * vel[1] + vel[2] * vel[2])
    out = [base] + [None] * (Q - 1)
    for i in range(1, Q, 2):
        cu = along(i, vel)
        even = base + 4.5 * cu * cu
        out[i] = even + 3.0 * cu
        out[i + 1] = even - 3.0 * cu
    return out


def departures(pops):
    rho, vel = flow(pops)
    shape = shapes(vel)
    return [LATTICE_WEIGHTS[i] * rho * shape[i] - pops[i] for i in range(Q)]


def collide_adjoint(pops, omega, cot):
    rho, vel = flow(pops)
    shape = shapes(vel)
    weighted = [LATTICE_WEIGHTS[i] * cot[i] for i in range(Q)]
    level = signed([(1, weighted[i] * shape[i]) for i in range(Q)])
    mass = signed([(1, w) for w in weighted])
    first = [signed([(VEL[i][axis], weighted[i]) for i in range(Q)]) for axis in range(3)]

    def second(a, b):
        return signed([(VEL[i][a] * VEL[i][b], weighted[i]) for i in range(Q)])

    pair = {(a, b): second(a, b) for a in range(3) for b in range(a, 3)}
    slope = []
    for a in range(3):
        mixed = signed([(1, pair[min(a, b), max(a, b)] * vel[b]) for b in range(3)])
        slope.append(3.0 * first[a] + 9.0 * mixed - 3.0 * mass * vel[a])
    base = omega * (level - (slope[0] * vel[0] + slope[1] * vel[1] + slope[2] * vel[2]))
    tilt = [omega * s for s in slope]
    keep = 1.0 - omega
    adjoint = []
    for i in range(Q):
        part = along(i, tilt)
        adjoint.append(keep * cot[i] + (base if part is None else base + part))
    away = [LATTICE_WEIGHTS[i] * rho * shape[i] - pops[i] for i in range(Q)]
    grad = signed([(1, cot[i] * away[i]) for i in range(Q)])
    return adjoint, grad, away


def relaxation(smag, eddy):
    return 1.0 / (0.5 + 3.0 * (NU_BASE + smag * eddy))


def row_ids():
    return lax.broadcasted_iota(jnp.int32, (ROWS, COLS), 0)


def lane_ids():
    return lax.broadcasted_iota(jnp.int32, (ROWS, COLS), 1)


def turn(tile, amount, axis):
    size = tile.shape[axis]
    if isinstance(amount, int):
        amount %= size
        return tile if amount == 0 else pltpu.roll(tile, amount, axis)
    return pltpu.roll(tile, lax.rem(amount + size, size), axis)


def pack_columns(out_ref, planes, start):
    lanes = lane_ids()
    per = COLS // 2
    for strip in range(-(-len(planes) // per)):
        total = None
        for j, plane in enumerate(planes[strip * per : (strip + 1) * per]):
            moved = turn(plane(), 2 * j - start, 1)
            total = moved if total is None else jnp.where(lanes >= 2 * j, moved, total)
        out_ref[:, strip * COLS : (strip + 1) * COLS] = total


def pack_rows(pieces):
    rows = row_ids()
    total = None
    for j, (piece, row) in enumerate(pieces):
        moved = turn(piece, j - row, 0)
        total = moved if total is None else jnp.where(rows >= j, moved, total)
    return total


def pack_planes(keys, plane, x_ref, z_ref):
    for at, (item, layer) in enumerate(keys):
        z_ref[at] = plane(item, layer)
    for v in range(x_ref.shape[1] // COLS):
        z_ref[len(keys) + v] = x_ref[:, v * COLS : (v + 1) * COLS]


def pack_border(keys, plane, row_at, x_ref, out_ref):
    columns = [x_ref[:, v * COLS : (v + 1) * COLS] for v in range(x_ref.shape[1] // COLS)]
    for at in range(0, len(keys), ROWS):
        out_ref[at // ROWS] = pack_rows(
            [(plane(item, z), row_at[r]) for item, z, r in keys[at : at + ROWS]]
        )
    out_ref[tiles_of(keys)] = pack_rows([(tile, row_at[r]) for tile in columns for r in (0, 1)])


def fetch_kernel(
    state_ref, seed_ref, state_out, seed_out, columns_ref, early_ref, sems
):
    copies = [
        pltpu.make_async_copy(src, dst, sems.at[k])
        for k, (src, dst) in enumerate(((state_ref, state_out), (seed_ref, seed_out)))
    ]
    for copy in copies:
        copy.start()
    for copy in copies:
        copy.wait()

    def plane(item, z):
        name, i = item
        return {"f": state_out, "g": seed_out}[name][i, z]

    planes = [
        functools.partial(plane, item, z) for item in LAYER if item[0] != "e" for z in range(DEPTH)
    ]
    pack_columns(columns_ref, planes, 0)
    for at, (item, layer) in enumerate(early_and_rest()[0]):
        early_ref[at] = plane(item, layer)


def eddy_columns_kernel(columns_ref, eddy_ref, out_ref):
    lanes = lane_ids()
    first = 2 * DEPTH * (len(LAYER) - 1)
    out_ref[:, :] = columns_ref[:, :]
    for z in range(DEPTH):
        strip, lane = divmod(first + 2 * z, COLS)
        spot = slice(strip * COLS, (strip + 1) * COLS)
        moved = turn(eddy_ref[z], lane, 1)
        out_ref[:, spot] = jnp.where(lanes // 2 == lane // 2, moved, out_ref[:, spot])


def collide_fields(smag, pops, eddy):
    omega = relaxation(smag, eddy)
    away = departures(pops)
    heat = omega * omega * eddy
    post = [pops[i] + omega * away[i] for i in range(Q)]
    return post, [heat * away[i] for i in range(Q)]


def first_kernel(
    total_y, total_x, place_ref, smag_ref, state_ref, eddy_ref, heights_ref, post_ref, tang_ref, high_ref, own_ref
):
    smag = smag_ref[0]
    for z in range(DEPTH):
        post, tang = collide_fields(smag, [state_ref[i, z] for i in range(Q)], eddy_ref[z])
        for i in range(Q):
            post_ref[i, z] = post[i]
            tang_ref[i, z] = tang[i]
    rows, lanes = row_ids(), lane_ids()
    start_y, start_x = place_ref[1], place_ref[2]

    def block(dy, dx):
        y = lax.rem(start_y + dy * ROWS + total_y, total_y)
        x = lax.rem(start_x + dx * COLS + total_x, total_x)
        return heights_ref[
            pl.ds(pl.multiple_of(y, ROWS), ROWS), pl.ds(pl.multiple_of(x, COLS), COLS)
        ]

    blocks = {side: block(*side) for side in SIDES}

    def beside(lower, own, upper, ids, axis, size, first, step):
        if first:
            if step < 0:
                return turn(own, 1, axis)
            return turn(jnp.where(ids <= step, upper, own), -step, axis)
        if step == 0:
            return own
        edge = jnp.where(ids == size - 1, lower, own) if step < 0 else jnp.where(ids == 0, upper, own)
        return turn(edge, -step, axis)

    for k, first in enumerate((1, 0)):
        across = {
            (dy, dx): beside(
                *(blocks[dy, n] for n in (-1, 0, 1)), lanes, 1, COLS, first, dx
            )
            for dy in (-1, 0, 1)
            for dx in (-1, 0, 1)
        }
        near = {
            (dy, dx): beside(
                *(across[n, dx] for n in (-1, 0, 1)), rows, 0, ROWS, first, dy
            )
            for dy, dx in SIDES
        }
        y = start_y + jnp.where((rows == 0) & (first == 1), ROWS, rows)
        x = start_x + jnp.where((lanes == 0) & (first == 1), COLS, lanes)
        for side, (dy, dx) in enumerate(SIDES):
            high, own = near[dy, dx], near[0, 0]
            if dy:
                low_y = y + min(dy, 0)
                wall = (low_y == -1) | (low_y == total_y - 1)
                high, own = jnp.where(wall, FAR, high), jnp.where(wall, FAR, own)
            if dx:
                low_x = x + min(dx, 0)
                wall = (low_x == -1) | (low_x == total_x - 1)
                high, own = jnp.where(wall, FAR, high), jnp.where(wall, FAR, own)
            high_ref[k, side] = high
            own_ref[k, side] = own


def up_plane(state_ref, seed_ref, eddy_ref, post_ref, tang_ref):
    fields = {"f": state_ref, "g": seed_ref, "p": post_ref, "t": tang_ref}

    def plane(item, z):
        name, i = item
        return eddy_ref[z] if name == "e" else fields[name][i, z]

    return plane


def up_faces_kernel(
    state_ref, seed_ref, eddy_ref, post_ref, tang_ref, x_ref, z_ref, y_ref, yz_ref
):
    plane = up_plane(state_ref, seed_ref, eddy_ref, post_ref, tang_ref)
    pack_planes(early_and_rest()[1], plane, x_ref, z_ref)
    pack_border(PLANS[False][1], plane, (0, 1), x_ref, y_ref)
    pack_border(PLANS[False][2], plane, (0, 1), x_ref, yz_ref)


def back_rows_kernel(back_ref, x_ref, y_ref):
    def plane(item, z):
        return back_ref[BACK.index(item), z]

    pack_border(PLANS[True][1], plane, (0, ROWS - 1), x_ref, y_ref)


def back_planes_kernel(back_ref, x_ref, y_ref, z_ref):
    vertical, _, corner = PLANS[True]

    def plane(item, layer):
        return back_ref[BACK.index(item), DEPTH - 1 - layer]

    pack_planes(vertical, plane, x_ref, z_ref)
    y_at = PLACES[True][1]
    first = len(vertical) + strips(True)
    for at in range(0, len(corner), ROWS):
        spots = [y_at[item, DEPTH - 1 - layer, r] for item, layer, r in corner[at : at + ROWS]]
        z_ref[first + at // ROWS] = pack_rows([(y_ref[k // ROWS], k % ROWS) for k in spots])
    z_ref[first + tiles_of(corner)] = y_ref[tiles_of(y_at)]


def level_of(start_z, total_z, plane):
    level = start_z + plane
    return lax.rem(level + total_z, total_z)


def wall_between(start_z, total_z, plane, step):
    upper = start_z + plane + (1 if step > 0 else 0)
    return (upper == total_z) | (upper == 0)


def masks_at(high_ref, own_ref, frame, start_z, total_z, plane):
    solid, way = {}, {}
    here = level_of(start_z, total_z, plane)
    for i in range(Q):
        dx, dy, dz = VEL[i]
        side = SIDES.index((dy, dx))
        there, mine = here, here
        if dz:
            wall = wall_between(start_z, total_z, plane, dz)
            there = jnp.where(wall, -1, level_of(start_z, total_z, plane + dz))
            mine = jnp.where(wall, -1, here)
        solid[VEL[i]] = there < high_ref[frame, side]
        way[VEL[i]] = mine >= own_ref[frame, side]
    return solid, way


def drag_links(solid, way, scale):
    fluid = way[VEL[0]]
    return {
        i: jnp.where(fluid & solid[VEL[i]], 2.0 * scale * VEL[i][0], 0.0)
        for i in range(Q)
        if VEL[i][0] != 0
    }


def pushed(i, own, target, solid, way, links):
    value = jnp.where(way[VEL[i]], target, 0.0) + jnp.where(solid[VEL[i]], own, 0.0)
    return value + links[i] if i in links else value


def middle_kernel(
    total_z,
    scale,
    sens_scale,
    place_ref,
    smag_ref,
    post_ref,
    tang_ref,
    seed_ref,
    eddy_ref,
    x_ref,
    y_ref,
    early_ref,
    z_ref,
    yz_ref,
    high_ref,
    own_ref,
    back_ref,
    columns_ref,
    sums_ref,
    main,
    y_tiles,
    x_tiles,
):
    smag = smag_ref[0]
    start_z = place_ref[0]
    rows, lanes = row_ids(), lane_ids()
    _, y_at, yz_at = PLACES[False]
    early_at, rest_at = (places(keys) for keys in early_and_rest())
    per = COLS // (2 * DEPTH)
    pops_items = [("f", i) for i in range(Q)]

    def collided(tile):
        post, tang = collide_fields(smag, [tile(item) for item in pops_items], tile(("e", 0)))
        out = {("p", i): post[i] for i in range(Q)}
        out.update({("t", i): tang[i] for i in range(Q)})
        out.update({item: tile(item) for item in LAYER if item[0] in "eg"})
        return out

    above = collided(
        lambda item: (z_ref[rest_at[item, 0]] if item[0] == "e" else early_ref[early_at[item, 0]])
    )

    def copy_planes(z, carry):
        for ref, first in ((post_ref, 0), (tang_ref, Q), (seed_ref, 2 * Q)):
            for i in range(Q):
                main[first + i, z] = ref[i, z]
        main[3 * Q, z] = eddy_ref[z]
        return carry

    lax.fori_loop(0, DEPTH, copy_planes, 0)
    for at, item in enumerate(FIELDS):
        main[at, DEPTH] = above[item]
        if (item, 1) in early_at:
            main[at, DEPTH + 1] = early_ref[early_at[item, 1]]
        if (item, 1) in rest_at:
            main[at, DEPTH + 1] = z_ref[rest_at[item, 1]]

    def y_piece(key, row):
        at = y_at[key]
        return turn(y_ref[at // ROWS], row - at % ROWS, 0)

    def yz_piece(key, row):
        at = yz_at[key]
        return turn(yz_ref[at // ROWS], row - at % ROWS, 0)

    y_near = collided(lambda item: y_piece((item, 0, 0), 0))
    y_above = collided(lambda item: yz_piece((item, 0, 0), 0))

    for at, item in enumerate(FIELDS):
        tile = y_near[item]
        if (item, 0, 1) in y_at:
            tile = jnp.where(rows < DEPTH, tile, y_piece((item, 0, 1), DEPTH))
        y_tiles[at, 0] = tile
        tile = y_above[item]
        for z, r in ((1, 0), (0, 1), (1, 1)):
            if (item, z, r) in yz_at:
                row = DEPTH * r + z
                tile = jnp.where(rows == row, yz_piece((item, z, r), row), tile)
        y_tiles[at, 1] = tile

    n_strips = strips(False)
    yx_tiles = [turn(y_ref[tiles_of(y_at)], -2 * v, 0) for v in range(n_strips)]
    yzx_tiles = [turn(yz_ref[tiles_of(yz_at)], -2 * v, 0) for v in range(n_strips)]

    def column_tile(item):
        v, at = divmod(LAYER.index(item), per)
        at *= 2 * DEPTH
        near = turn(x_ref[:, v * COLS : (v + 1) * COLS], -at, 1)
        high = turn(z_ref[len(rest_at) + v], 8 - at, 1)
        near_rows = turn(yx_tiles[v], 16 - at, 1)
        high_rows = turn(yzx_tiles[v], 24 - at, 1)
        return jnp.where(
            lanes < 16,
            jnp.where(lanes < 8, near, high),
            jnp.where(lanes < 24, near_rows, high_rows),
        )

    sides = collided(column_tile)
    for at, item in enumerate(FIELDS):
        x_tiles[at] = sides[item]

    def viewer(plane_of):
        @functools.cache
        def view(item, dz, dy, dx):
            at, plane = FIELDS.index(item), plane_of[dz]
            tile = main[at, plane]
            if dx >= 0:
                tile = jnp.where(lanes <= dx, turn(x_tiles[at], -2 * plane, 1), tile)
            if dy >= 0:
                k = plane // DEPTH
                z = plane - k * DEPTH
                low = turn(y_tiles[at, k], -z, 0)
                if dy == 1:
                    low = jnp.where(rows == 0, low, turn(y_tiles[at, k], 1 - DEPTH - z, 0))
                if dx >= 0:
                    low = jnp.where(lanes <= dx, turn(x_tiles[at], -2 * plane - 16, 1), low)
                tile = jnp.where(rows <= dy, low, tile)
            return turn(turn(tile, -dx, 1), -dy, 0)

        return view

    def step(z, carry):
        drag, sens = carry
        plane = z + 1
        view = viewer({dz: plane + dz for dz in (-1, 0, 1)})
        solid, way = masks_at(high_ref, own_ref, 0, start_z, total_z, plane)
        links = drag_links(solid, way, scale)

        def pulled(name, i):
            dx, dy, dz = VEL[i]
            away = view((name, i), -dz, -dy, -dx)
            if i == 0:
                return away
            return jnp.where(solid[-dx, -dy, -dz], view((name, OPPOSITE[i]), 0, 0, 0), away)

        f_one = [pulled("p", i) for i in range(Q)]
        cot = []
        for i in range(Q):
            dx, dy, dz = VEL[i]
            own = view(("g", OPPOSITE[i]), 0, 0, 0)
            cot.append(pushed(i, own, view(("g", i), dz, dy, dx), solid, way, links))
        eddy = view(("e", 0), 0, 0, 0)
        omega = relaxation(smag, eddy)
        adjoint, grad, away = collide_adjoint(f_one, omega, cot)
        for i in range(Q):
            back_ref[i, z] = adjoint[i]
        back_ref[Q, z] = grad
        for i in links:
            drag = drag + links[i] * (view(("p", i), 0, 0, 0) + f_one[i] + omega * away[i])
            sens = sens + links[i] * view(("t", i), 0, 0, 0)
        sens = sens + omega * omega * eddy * grad
        for i in range(Q):
            sens = sens + adjoint[i] * pulled("t", i)
        return drag, sens

    zero = jnp.zeros((ROWS, COLS), jnp.float32)
    drag, sens = lax.fori_loop(0, DEPTH, step, (zero, zero))
    sums_ref[...] = jnp.where(
        lax.broadcasted_iota(jnp.int32, sums_ref.shape, 1) == 0,
        jnp.sum(drag),
        jnp.sum(sens) * sens_scale,
    )
    planes = [
        functools.partial(lambda c, z: back_ref[c, z], c, z)
        for c in range(len(BACK))
        for z in range(DEPTH)
    ]
    pack_columns(columns_ref, planes, COLS - 1)


def last_kernel(
    total_z,
    scale,
    place_ref,
    smag_ref,
    state_ref,
    eddy_ref,
    back_ref,
    x_ref,
    y_ref,
    z_ref,
    high_ref,
    own_ref,
    out_ref,
    grad_ref,
    main,
    low_rows,
    strip_tiles,
):
    smag = smag_ref[0]
    start_z = place_ref[0]
    rows, lanes = row_ids(), lane_ids()
    z_at, y_at, yz_at = PLACES[True]
    yz_ref = z_ref.at[pl.ds(len(z_at) + strips(True), tiles_of(yz_at) + 1)]
    per = COLS // 2 // DEPTH

    def copy_planes(z, carry):
        for at in range(len(BACK)):
            main[at, z + 2] = back_ref[at, z]
        return carry

    lax.fori_loop(0, DEPTH, copy_planes, 0)
    for at, item in enumerate(BACK):
        for plane in range(-1, DEPTH + 1):
            if plane >= 1:
                places_of, ref, layer = y_at, y_ref, plane - 1
            else:
                places_of, ref, layer = yz_at, yz_ref, -plane
                if (item, layer) in z_at:
                    main[at, plane + 1] = z_ref[z_at[item, layer]]
            low = None
            for r, row in ((0, 0), (1, ROWS - 1)):
                if (item, layer, r) in places_of:
                    k = places_of[item, layer, r]
                    piece = turn(ref[k // ROWS], row - k % ROWS, 0)
                    low = piece if low is None else jnp.where(rows == 0, low, piece)
            if low is not None:
                low_rows[at, plane + 1] = low
    for v in range(strips(True)):
        strip_tiles[0, v] = x_ref[:, v * COLS : (v + 1) * COLS]
        strip_tiles[1, v] = z_ref[len(z_at) + v]
        for k, tile in ((2, y_ref[tiles_of(y_at)]), (3, yz_ref[tiles_of(yz_at)])):
            first = turn(tile, -2 * v, 0)
            strip_tiles[k, v] = jnp.where(rows == 0, first, turn(first, -2, 0))

    def step(z, carry):
        @functools.cache
        def view(item, dz, dy, dx):
            at, plane = BACK.index(item), z + dz
            lower = jnp.where(plane >= 1, 0, 1)
            layer = lax.rem(plane + DEPTH - 1, DEPTH)
            shift = -2 * (DEPTH * (at % per) + layer) - 1
            keep = (lanes == 0) if dx == 0 else (lanes == 0) | (lanes == COLS - 1)

            def with_columns(tile, kind):
                if dx > 0:
                    return tile
                return jnp.where(keep, turn(strip_tiles[kind + lower, at // per], shift, 1), tile)

            tile = with_columns(main[at, plane + 1], 0)
            if dy <= 0:
                low = with_columns(low_rows[at, plane + 1], 2)
                edge = (rows == 0) if dy == 0 else (rows == 0) | (rows == ROWS - 1)
                tile = jnp.where(edge, low, tile)
            return turn(turn(tile, -dx, 1), -dy, 0)

        solid, way = masks_at(high_ref, own_ref, 1, start_z, total_z, z)
        links = drag_links(solid, way, scale)
        cot = []
        for i in range(Q):
            dx, dy, dz = VEL[i]
            own = view(("a", OPPOSITE[i]), 0, 0, 0)
            cot.append(pushed(i, own, view(("a", i), dz, dy, dx), solid, way, links))
        omega = relaxation(smag, eddy_ref[z])
        adjoint, grad, _ = collide_adjoint([state_ref[i, z] for i in range(Q)], omega, cot)
        for i in range(Q):
            out_ref[i, z] = adjoint[i]
        grad_ref[z] = -3.0 * omega * omega * (grad + view(("d", 0), 0, 0, 0))
        return carry

    lax.fori_loop(0, DEPTH, step, 0)


def plus_one(axis):
    count = lax.axis_size(axis)
    return [(i, (i + 1) % count) for i in range(count)]


def minus_one(axis):
    return [(target, source) for source, target in plus_one(axis)]


def pair_pairs(first, second):
    count = lax.axis_size("gz")
    return [(a * count + b, c * count + d) for a, c in first for b, d in second]


def call(kernel, outs, operands, scalars=0, far=False, scratch=(), flops=0, limit=32 << 20):
    def kind(k):
        if k < scalars:
            return pltpu.SMEM
        return pltpu.HBM if far else pltpu.VMEM

    outs = [out if isinstance(out[-1], type) else (out, jnp.float32) for out in outs]
    return pl.pallas_call(
        kernel,
        out_shape=[jax.ShapeDtypeStruct(*out) for out in outs],
        in_specs=[pl.BlockSpec(memory_space=kind(k)) for k in range(len(operands))],
        out_specs=[pl.BlockSpec(memory_space=pltpu.VMEM)] * len(outs),
        scratch_shapes=list(scratch),
        compiler_params=pltpu.CompilerParams(vmem_limit_bytes=limit),
        cost_estimate=pl.CostEstimate(flops=flops, bytes_accessed=1 << 20, transcendentals=0),
    )(*operands)


def exchange_faces(messages, step):
    vertical, spanwise, corner = messages
    vertical = lax.ppermute(vertical, "gz", step("gz"))
    spanwise = lax.ppermute(spanwise, "gy", step("gy"))
    corner = lax.ppermute(corner, ("gy", "gz"), pair_pairs(step("gy"), step("gz")))
    return vertical, spanwise, corner


def on_device(state, adjoint_seed, eddy_rate, smag_coeff, heights):
    total_x = COLS * lax.axis_size("gx")
    total_y = ROWS * lax.axis_size("gy")
    total_z = DEPTH * lax.axis_size("gz")
    scale = 1.0 / (2.0 * UREF * total_x * total_y)
    sens_scale = -3.0 / math.sqrt(total_x * total_y * total_z)
    tile = (ROWS, COLS)
    place = jnp.stack(
        [
            lax.axis_index("gz") * DEPTH,
            lax.axis_index("gy") * ROWS,
            lax.axis_index("gx") * COLS,
        ]
    ).astype(jnp.int32)
    smag = smag_coeff.reshape(1)
    block = state.shape
    layer = eddy_rate.shape

    eddy = eddy_rate
    state, seed, columns, early = call(
        fetch_kernel,
        [
            block,
            block,
            (ROWS, strips(False) * COLS),
            (len(early_and_rest()[0]), *tile),
        ],
        (state, adjoint_seed),
        far=True,
        scratch=[pltpu.SemaphoreType.DMA((2,))],
        limit=(52 << 20) + (960 << 10),
    )
    (columns,) = call(eddy_columns_kernel, [columns.shape], (columns, eddy))
    columns = lax.ppermute(columns, "gx", minus_one("gx"))
    early = lax.ppermute(early, "gz", minus_one("gz"))
    beside = ((2, len(SIDES), ROWS, COLS), jnp.int32)
    post, tang, high, own = call(
        functools.partial(first_kernel, total_y, total_x),
        [block, block, beside, beside],
        (place, smag, state, eddy, heights),
        scalars=2,
        flops=8_000_000,
    )
    messages = call(
        up_faces_kernel, face_shapes(False), (state, seed, eddy, post, tang, columns)
    )
    vertical, spanwise, corner = exchange_faces(messages, minus_one)
    n_first = lax.axis_size("gy") * lax.axis_size("gz")
    back, back_columns, sums = call(
        functools.partial(middle_kernel, total_z, scale, sens_scale),
        [(len(BACK), *layer), (ROWS, strips(True) * COLS), (n_first, COLS)],
        (place, smag, post, tang, seed, eddy, columns, spanwise, early, vertical, corner, high, own),
        scalars=2,
        scratch=[
            pltpu.VMEM(shape, jnp.float32)
            for shape in (
                (len(FIELDS), DEPTH + 2, ROWS, COLS),
                (len(FIELDS), 2, ROWS, COLS),
                (len(FIELDS), ROWS, COLS),
            )
        ],
        flops=20_000_000,
    )
    back_columns = lax.ppermute(back_columns, "gx", plus_one("gx"))
    sums = lax.all_to_all(sums, ("gy", "gz"), split_axis=0, concat_axis=0, tiled=True)
    shape_z, shape_y, shape_yz = face_shapes(True)
    (spanwise,) = call(back_rows_kernel, [shape_y], (back, back_columns))
    spanwise = lax.ppermute(spanwise, "gy", plus_one("gy"))
    (vertical,) = call(
        back_planes_kernel,
        [(shape_z[0] + shape_yz[0], *tile)],
        (back, back_columns, spanwise),
    )
    vertical, sums = lax.optimization_barrier((vertical, sums))
    vertical = lax.ppermute(vertical, "gz", plus_one("gz"))
    sums = jnp.broadcast_to(jnp.sum(sums, 0, keepdims=True), (lax.axis_size("gx"), COLS))
    sums = lax.all_to_all(sums, "gx", split_axis=0, concat_axis=0, tiled=True)
    adjoint_state, gradient = call(
        functools.partial(last_kernel, total_z, scale),
        [block, layer],
        (place, smag, state, eddy, back, back_columns, spanwise, vertical, high, own),
        scalars=2,
        scratch=[
            pltpu.VMEM(shape, jnp.float32)
            for shape in (
                (len(BACK), DEPTH + 2, ROWS, COLS),
                (len(BACK), DEPTH + 2, ROWS, COLS),
                (4, strips(True), ROWS, COLS),
            )
        ],
        flops=20_000_000,
    )
    gradient, sums = lax.optimization_barrier((gradient, sums))
    return adjoint_state, gradient, jnp.sum(sums[:, :2], 0)


def solution(mesh):
    return jax.shard_map(
        on_device,
        mesh=mesh,
        in_specs=(
            P(None, "gz", "gy", "gx"),
            P(None, "gz", "gy", "gx"),
            P("gz", "gy", "gx"),
            P(),
            P(),
        ),
        out_specs=(P(None, "gz", "gy", "gx"), P("gz", "gy", "gx"), P()),
        check_vma=False,
    )
```

```python
import functools
import math

import jax
import jax.numpy as jnp
from jax import lax
from jax.experimental import pallas as pl
from jax.experimental.pallas import tpu as pltpu
from jax.sharding import PartitionSpec as P

VEL = [
    (0, 0, 0),
    (1, 0, 0),
    (-1, 0, 0),
    (0, 1, 0),
    (0, -1, 0),
    (0, 0, 1),
    (0, 0, -1),
    (1, 1, 0),
    (-1, -1, 0),
    (1, -1, 0),
    (-1, 1, 0),
    (1, 0, 1),
    (-1, 0, -1),
    (1, 0, -1),
    (-1, 0, 1),
    (0, 1, 1),
    (0, -1, -1),
    (0, 1, -1),
    (0, -1, 1),
]
OPPOSITE = [0, 2, 1, 4, 3, 6, 5, 8, 7, 10, 9, 12, 11, 14, 13, 16, 15, 18, 17]
LATTICE_WEIGHTS = [1.0 / 3.0] + [1.0 / 18.0] * 6 + [1.0 / 36.0] * 12
UREF = 0.08
NU_BASE = 0.004
Q = 19
DEPTH = 4
ROWS = 8
COLS = 128
FAR = 1 << 20
SIDES = [(dy, dx) for dy in (-1, 0, 1) for dx in (-1, 0, 1)]

LAYER = [("f", i) for i in range(Q)] + [("g", i) for i in range(Q)] + [("e", 0)]
BACK = [("a", i) for i in range(Q)] + [("d", 0)]
FIELDS = [(name, i) for name in "ptg" for i in range(Q)] + [("e", 0)]


def crossing_items(axes, back):
    down = [i for i in range(Q) if all(VEL[i][a] == -1 for a in axes)]
    if back:
        return [("a", i) for i in down]
    up = [i for i in range(Q) if all(VEL[i][a] == 1 for a in axes)]
    return [(name, i) for i in down for name in "pt"] + [("g", i) for i in up]


def face_plan(back):
    near = BACK if back else LAYER
    vertical = [(item, 0) for item in near] + [(item, 1) for item in crossing_items([2], back)]
    spanwise = [(item, z, 0) for item in near for z in range(DEPTH)]
    spanwise += [(item, z, 1) for item in crossing_items([1], back) for z in range(DEPTH)]
    corner = [(item, 0, 0) for item in near]
    corner += [(item, 0, 1) for item in crossing_items([1], back)]
    corner += [(item, 1, 0) for item in crossing_items([2], back)]
    corner += [(item, 1, 1) for item in crossing_items([1, 2], back)]
    return vertical, spanwise, corner


def places(keys):
    return {key: at for at, key in enumerate(keys)}


def early_and_rest():
    vertical = PLANS[False][0]
    return [k for k in vertical if is_early(k)], [k for k in vertical if not is_early(k)]


def tiles_of(keys):
    return -(-len(keys) // ROWS)


def is_early(key):
    return key[0][0] in "fg"


PLANS = {back: face_plan(back) for back in (False, True)}
PLACES = {back: [places(keys) for keys in PLANS[back]] for back in (False, True)}


def strips(back):
    return -(-len(BACK if back else LAYER) * DEPTH * 2 // COLS)


def face_shapes(back):
    vertical, spanwise, corner = PLANS[back]
    planes = vertical if back else early_and_rest()[1]
    return [
        (len(planes) + strips(back), ROWS, COLS),
        (tiles_of(spanwise) + 1, ROWS, COLS),
        (tiles_of(corner) + 1, ROWS, COLS),
    ]


def signed(terms):
    total = None
    for factor, value in terms:
        if factor == 0:
            continue
        piece = value if factor == 1 else (-value if factor == -1 else factor * value)
        total = piece if total is None else total + piece
    return total


def along(idx, vec):
    return signed([(VEL[idx][axis], vec[axis]) for axis in range(3)])


def flow(pops):
    rho = signed([(1, p) for p in pops])
    inverse = 1.0 / rho
    vel = [signed([(VEL[i][axis], pops[i]) for i in range(Q)]) * inverse for axis in range(3)]
    return rho, vel


def shapes(vel):
    base = 1.0 - 1.5 * (vel[0] * vel[0] + vel[1] * vel[1] + vel[2] * vel[2])
    out = [base] + [None] * (Q - 1)
    for i in range(1, Q, 2):
        cu = along(i, vel)
        even = base + 4.5 * cu * cu
        out[i] = even + 3.0 * cu
        out[i + 1] = even - 3.0 * cu
    return out


def departures(pops):
    rho, vel = flow(pops)
    shape = shapes(vel)
    return [LATTICE_WEIGHTS[i] * rho * shape[i] - pops[i] for i in range(Q)]


def collide_adjoint(pops, omega, cot):
    rho, vel = flow(pops)
    shape = shapes(vel)
    weighted = [LATTICE_WEIGHTS[i] * cot[i] for i in range(Q)]
    level = signed([(1, weighted[i] * shape[i]) for i in range(Q)])
    mass = signed([(1, w) for w in weighted])
    first = [signed([(VEL[i][axis], weighted[i]) for i in range(Q)]) for axis in range(3)]

    def second(a, b):
        return signed([(VEL[i][a] * VEL[i][b], weighted[i]) for i in range(Q)])

    pair = {(a, b): second(a, b) for a in range(3) for b in range(a, 3)}
    slope = []
    for a in range(3):
        mixed = signed([(1, pair[min(a, b), max(a, b)] * vel[b]) for b in range(3)])
        slope.append(3.0 * first[a] + 9.0 * mixed - 3.0 * mass * vel[a])
    base = omega * (level - (slope[0] * vel[0] + slope[1] * vel[1] + slope[2] * vel[2]))
    tilt = [omega * s for s in slope]
    keep = 1.0 - omega
    adjoint = []
    for i in range(Q):
        part = along(i, tilt)
        adjoint.append(keep * cot[i] + (base if part is None else base + part))
    away = [LATTICE_WEIGHTS[i] * rho * shape[i] - pops[i] for i in range(Q)]
    grad = signed([(1, cot[i] * away[i]) for i in range(Q)])
    return adjoint, grad, away


def relaxation(smag, eddy):
    return 1.0 / (0.5 + 3.0 * (NU_BASE + smag * eddy))


def row_ids():
    return lax.broadcasted_iota(jnp.int32, (ROWS, COLS), 0)


def lane_ids():
    return lax.broadcasted_iota(jnp.int32, (ROWS, COLS), 1)


def turn(tile, amount, axis):
    size = tile.shape[axis]
    if isinstance(amount, int):
        amount %= size
        return tile if amount == 0 else pltpu.roll(tile, amount, axis)
    return pltpu.roll(tile, lax.rem(amount + size, size), axis)


def pack_columns(out_ref, planes, start):
    lanes = lane_ids()
    per = COLS // 2
    for strip in range(-(-len(planes) // per)):
        total = None
        for j, plane in enumerate(planes[strip * per : (strip + 1) * per]):
            moved = turn(plane(), 2 * j - start, 1)
            total = moved if total is None else jnp.where(lanes >= 2 * j, moved, total)
        out_ref[:, strip * COLS : (strip + 1) * COLS] = total


def pack_rows(pieces):
    rows = row_ids()
    total = None
    for j, (piece, row) in enumerate(pieces):
        moved = turn(piece, j - row, 0)
        total = moved if total is None else jnp.where(rows >= j, moved, total)
    return total


def pack_planes(keys, plane, x_ref, z_ref):
    for at, (item, layer) in enumerate(keys):
        z_ref[at] = plane(item, layer)
    for v in range(x_ref.shape[1] // COLS):
        z_ref[len(keys) + v] = x_ref[:, v * COLS : (v + 1) * COLS]


def pack_border(keys, plane, row_at, x_ref, out_ref):
    columns = [x_ref[:, v * COLS : (v + 1) * COLS] for v in range(x_ref.shape[1] // COLS)]
    for at in range(0, len(keys), ROWS):
        out_ref[at // ROWS] = pack_rows(
            [(plane(item, z), row_at[r]) for item, z, r in keys[at : at + ROWS]]
        )
    out_ref[tiles_of(keys)] = pack_rows([(tile, row_at[r]) for tile in columns for r in (0, 1)])


def fetch_kernel(
    state_ref, seed_ref, state_out, seed_out, columns_ref, early_ref, sems
):
    copies = [
        pltpu.make_async_copy(src, dst, sems.at[k])
        for k, (src, dst) in enumerate(((state_ref, state_out), (seed_ref, seed_out)))
    ]
    for copy in copies:
        copy.start()
    for copy in copies:
        copy.wait()

    def plane(item, z):
        name, i = item
        return {"f": state_out, "g": seed_out}[name][i, z]

    planes = [
        functools.partial(plane, item, z) for item in LAYER if item[0] != "e" for z in range(DEPTH)
    ]
    pack_columns(columns_ref, planes, 0)
    for at, (item, layer) in enumerate(early_and_rest()[0]):
        early_ref[at] = plane(item, layer)


def eddy_columns_kernel(columns_ref, eddy_ref, out_ref):
    lanes = lane_ids()
    first = 2 * DEPTH * (len(LAYER) - 1)
    out_ref[:, :] = columns_ref[:, :]
    for z in range(DEPTH):
        strip, lane = divmod(first + 2 * z, COLS)
        spot = slice(strip * COLS, (strip + 1) * COLS)
        moved = turn(eddy_ref[z], lane, 1)
        out_ref[:, spot] = jnp.where(lanes // 2 == lane // 2, moved, out_ref[:, spot])


def collide_fields(smag, pops, eddy):
    omega = relaxation(smag, eddy)
    away = departures(pops)
    heat = omega * omega * eddy
    post = [pops[i] + omega * away[i] for i in range(Q)]
    return post, [heat * away[i] for i in range(Q)]


def first_kernel(
    total_y, total_x, smag_ref, state_ref, eddy_ref, heights_ref, post_ref, tang_ref, high_ref, own_ref
):
    smag = smag_ref[0]
    for z in range(DEPTH):
        post, tang = collide_fields(smag, [state_ref[i, z] for i in range(Q)], eddy_ref[z])
        for i in range(Q):
            post_ref[i, z] = post[i]
            tang_ref[i, z] = tang[i]
    rows, lanes = row_ids(), lane_ids()
    start_y = lax.axis_index("gy") * ROWS
    start_x = lax.axis_index("gx") * COLS

    def block(dy, dx):
        y = lax.rem(start_y + dy * ROWS + total_y, total_y)
        x = lax.rem(start_x + dx * COLS + total_x, total_x)
        return heights_ref[
            pl.ds(pl.multiple_of(y, ROWS), ROWS), pl.ds(pl.multiple_of(x, COLS), COLS)
        ]

    blocks = {side: block(*side) for side in SIDES}

    def beside(lower, own, upper, ids, axis, size, first, step):
        if first:
            if step < 0:
                return turn(own, 1, axis)
            return turn(jnp.where(ids <= step, upper, own), -step, axis)
        if step == 0:
            return own
        edge = jnp.where(ids == size - 1, lower, own) if step < 0 else jnp.where(ids == 0, upper, own)
        return turn(edge, -step, axis)

    for k, first in enumerate((1, 0)):
        across = {
            (dy, dx): beside(
                *(blocks[dy, n] for n in (-1, 0, 1)), lanes, 1, COLS, first, dx
            )
            for dy in (-1, 0, 1)
            for dx in (-1, 0, 1)
        }
        near = {
            (dy, dx): beside(
                *(across[n, dx] for n in (-1, 0, 1)), rows, 0, ROWS, first, dy
            )
            for dy, dx in SIDES
        }
        y = start_y + jnp.where((rows == 0) & (first == 1), ROWS, rows)
        x = start_x + jnp.where((lanes == 0) & (first == 1), COLS, lanes)
        for side, (dy, dx) in enumerate(SIDES):
            high, own = near[dy, dx], near[0, 0]
            if dy:
                low_y = y + min(dy, 0)
                wall = (low_y == -1) | (low_y == total_y - 1)
                high, own = jnp.where(wall, FAR, high), jnp.where(wall, FAR, own)
            if dx:
                low_x = x + min(dx, 0)
                wall = (low_x == -1) | (low_x == total_x - 1)
                high, own = jnp.where(wall, FAR, high), jnp.where(wall, FAR, own)
            high_ref[k, side] = high
            own_ref[k, side] = own


def up_plane(state_ref, seed_ref, eddy_ref, post_ref, tang_ref):
    fields = {"f": state_ref, "g": seed_ref, "p": post_ref, "t": tang_ref}

    def plane(item, z):
        name, i = item
        return eddy_ref[z] if name == "e" else fields[name][i, z]

    return plane


def up_faces_kernel(
    state_ref, seed_ref, eddy_ref, post_ref, tang_ref, x_ref, z_ref, y_ref, yz_ref
):
    plane = up_plane(state_ref, seed_ref, eddy_ref, post_ref, tang_ref)
    pack_planes(early_and_rest()[1], plane, x_ref, z_ref)
    pack_border(PLANS[False][1], plane, (0, 1), x_ref, y_ref)
    pack_border(PLANS[False][2], plane, (0, 1), x_ref, yz_ref)


def back_rows_kernel(back_ref, x_ref, y_ref):
    def plane(item, z):
        return back_ref[BACK.index(item), z]

    pack_border(PLANS[True][1], plane, (0, ROWS - 1), x_ref, y_ref)


def back_planes_kernel(back_ref, x_ref, y_ref, z_ref):
    vertical, _, corner = PLANS[True]

    def plane(item, layer):
        return back_ref[BACK.index(item), DEPTH - 1 - layer]

    pack_planes(vertical, plane, x_ref, z_ref)
    y_at = PLACES[True][1]
    first = len(vertical) + strips(True)
    for at in range(0, len(corner), ROWS):
        spots = [y_at[item, DEPTH - 1 - layer, r] for item, layer, r in corner[at : at + ROWS]]
        z_ref[first + at // ROWS] = pack_rows([(y_ref[k // ROWS], k % ROWS) for k in spots])
    z_ref[first + tiles_of(corner)] = y_ref[tiles_of(y_at)]


def level_of(start_z, total_z, plane):
    level = start_z + plane
    return lax.rem(level + total_z, total_z)


def wall_between(start_z, total_z, plane, step):
    upper = start_z + plane + (1 if step > 0 else 0)
    return (upper == total_z) | (upper == 0)


def masks_at(high_ref, own_ref, frame, start_z, total_z, plane):
    solid, way = {}, {}
    here = level_of(start_z, total_z, plane)
    for i in range(Q):
        dx, dy, dz = VEL[i]
        side = SIDES.index((dy, dx))
        there, mine = here, here
        if dz:
            wall = wall_between(start_z, total_z, plane, dz)
            there = jnp.where(wall, -1, level_of(start_z, total_z, plane + dz))
            mine = jnp.where(wall, -1, here)
        solid[VEL[i]] = there < high_ref[frame, side]
        way[VEL[i]] = mine >= own_ref[frame, side]
    return solid, way


def drag_links(solid, way, scale):
    fluid = way[VEL[0]]
    return {
        i: jnp.where(fluid & solid[VEL[i]], 2.0 * scale * VEL[i][0], 0.0)
        for i in range(Q)
        if VEL[i][0] != 0
    }


def pushed(i, own, target, solid, way, links):
    value = jnp.where(way[VEL[i]], target, 0.0) + jnp.where(solid[VEL[i]], own, 0.0)
    return value + links[i] if i in links else value


def middle_kernel(
    total_z,
    scale,
    sens_scale,
    smag_ref,
    post_ref,
    tang_ref,
    seed_ref,
    eddy_ref,
    x_ref,
    y_ref,
    early_ref,
    z_ref,
    yz_ref,
    high_ref,
    own_ref,
    back_ref,
    columns_ref,
    sums_ref,
    main,
    y_tiles,
    x_tiles,
):
    smag = smag_ref[0]
    start_z = lax.axis_index("gz") * DEPTH
    rows, lanes = row_ids(), lane_ids()
    _, y_at, yz_at = PLACES[False]
    early_at, rest_at = (places(keys) for keys in early_and_rest())
    per = COLS // (2 * DEPTH)
    pops_items = [("f", i) for i in range(Q)]

    def collided(tile):
        post, tang = collide_fields(smag, [tile(item) for item in pops_items], tile(("e", 0)))
        out = {("p", i): post[i] for i in range(Q)}
        out.update({("t", i): tang[i] for i in range(Q)})
        out.update({item: tile(item) for item in LAYER if item[0] in "eg"})
        return out

    above = collided(
        lambda item: (z_ref[rest_at[item, 0]] if item[0] == "e" else early_ref[early_at[item, 0]])
    )

    def copy_planes(z, carry):
        for ref, first in ((post_ref, 0), (tang_ref, Q), (seed_ref, 2 * Q)):
            for i in range(Q):
                main[first + i, z] = ref[i, z]
        main[3 * Q, z] = eddy_ref[z]
        return carry

    lax.fori_loop(0, DEPTH, copy_planes, 0)
    for at, item in enumerate(FIELDS):
        main[at, DEPTH] = above[item]
        if (item, 1) in early_at:
            main[at, DEPTH + 1] = early_ref[early_at[item, 1]]
        if (item, 1) in rest_at:
            main[at, DEPTH + 1] = z_ref[rest_at[item, 1]]

    def y_piece(key, row):
        at = y_at[key]
        return turn(y_ref[at // ROWS], row - at % ROWS, 0)

    def yz_piece(key, row):
        at = yz_at[key]
        return turn(yz_ref[at // ROWS], row - at % ROWS, 0)

    y_near = collided(lambda item: y_piece((item, 0, 0), 0))
    y_above = collided(lambda item: yz_piece((item, 0, 0), 0))

    for at, item in enumerate(FIELDS):
        tile = y_near[item]
        if (item, 0, 1) in y_at:
            tile = jnp.where(rows < DEPTH, tile, y_piece((item, 0, 1), DEPTH))
        y_tiles[at, 0] = tile
        tile = y_above[item]
        for z, r in ((1, 0), (0, 1), (1, 1)):
            if (item, z, r) in yz_at:
                row = DEPTH * r + z
                tile = jnp.where(rows == row, yz_piece((item, z, r), row), tile)
        y_tiles[at, 1] = tile

    n_strips = strips(False)
    yx_tiles = [turn(y_ref[tiles_of(y_at)], -2 * v, 0) for v in range(n_strips)]
    yzx_tiles = [turn(yz_ref[tiles_of(yz_at)], -2 * v, 0) for v in range(n_strips)]

    def column_tile(item):
        v, at = divmod(LAYER.index(item), per)
        at *= 2 * DEPTH
        near = turn(x_ref[:, v * COLS : (v + 1) * COLS], -at, 1)
        high = turn(z_ref[len(rest_at) + v], 8 - at, 1)
        near_rows = turn(yx_tiles[v], 16 - at, 1)
        high_rows = turn(yzx_tiles[v], 24 - at, 1)
        return jnp.where(
            lanes < 16,
            jnp.where(lanes < 8, near, high),
            jnp.where(lanes < 24, near_rows, high_rows),
        )

    sides = collided(column_tile)
    for at, item in enumerate(FIELDS):
        x_tiles[at] = sides[item]

    def viewer(plane_of):
        @functools.cache
        def view(item, dz, dy, dx):
            at, plane = FIELDS.index(item), plane_of[dz]
            tile = main[at, plane]
            if dx >= 0:
                tile = jnp.where(lanes <= dx, turn(x_tiles[at], -2 * plane, 1), tile)
            if dy >= 0:
                k = plane // DEPTH
                z = plane - k * DEPTH
                low = turn(y_tiles[at, k], -z, 0)
                if dy == 1:
                    low = jnp.where(rows == 0, low, turn(y_tiles[at, k], 1 - DEPTH - z, 0))
                if dx >= 0:
                    low = jnp.where(lanes <= dx, turn(x_tiles[at], -2 * plane - 16, 1), low)
                tile = jnp.where(rows <= dy, low, tile)
            return turn(turn(tile, -dx, 1), -dy, 0)

        return view

    def step(z, carry):
        drag, sens = carry
        plane = z + 1
        view = viewer({dz: plane + dz for dz in (-1, 0, 1)})
        solid, way = masks_at(high_ref, own_ref, 0, start_z, total_z, plane)
        links = drag_links(solid, way, scale)

        def pulled(name, i):
            dx, dy, dz = VEL[i]
            away = view((name, i), -dz, -dy, -dx)
            if i == 0:
                return away
            return jnp.where(solid[-dx, -dy, -dz], view((name, OPPOSITE[i]), 0, 0, 0), away)

        f_one = [pulled("p", i) for i in range(Q)]
        cot = []
        for i in range(Q):
            dx, dy, dz = VEL[i]
            own = view(("g", OPPOSITE[i]), 0, 0, 0)
            cot.append(pushed(i, own, view(("g", i), dz, dy, dx), solid, way, links))
        eddy = view(("e", 0), 0, 0, 0)
        omega = relaxation(smag, eddy)
        adjoint, grad, away = collide_adjoint(f_one, omega, cot)
        for i in range(Q):
            back_ref[i, z] = adjoint[i]
        back_ref[Q, z] = grad
        for i in links:
            drag = drag + links[i] * (view(("p", i), 0, 0, 0) + f_one[i] + omega * away[i])
            sens = sens + links[i] * view(("t", i), 0, 0, 0)
        sens = sens + omega * omega * eddy * grad
        for i in range(Q):
            sens = sens + adjoint[i] * pulled("t", i)
        return drag, sens

    zero = jnp.zeros((ROWS, COLS), jnp.float32)
    drag, sens = lax.fori_loop(0, DEPTH, step, (zero, zero))
    sums_ref[...] = jnp.where(
        lax.broadcasted_iota(jnp.int32, sums_ref.shape, 1) == 0,
        jnp.sum(drag),
        jnp.sum(sens) * sens_scale,
    )
    planes = [
        functools.partial(lambda c, z: back_ref[c, z], c, z)
        for c in range(len(BACK))
        for z in range(DEPTH)
    ]
    pack_columns(columns_ref, planes, COLS - 1)


def last_kernel(
    total_z,
    scale,
    smag_ref,
    state_ref,
    eddy_ref,
    back_ref,
    x_ref,
    y_ref,
    z_ref,
    high_ref,
    own_ref,
    out_ref,
    grad_ref,
    main,
    low_rows,
    strip_tiles,
):
    smag = smag_ref[0]
    start_z = lax.axis_index("gz") * DEPTH
    rows, lanes = row_ids(), lane_ids()
    z_at, y_at, yz_at = PLACES[True]
    yz_ref = z_ref.at[pl.ds(len(z_at) + strips(True), tiles_of(yz_at) + 1)]
    per = COLS // 2 // DEPTH

    def copy_planes(z, carry):
        for at in range(len(BACK)):
            main[at, z + 2] = back_ref[at, z]
        return carry

    lax.fori_loop(0, DEPTH, copy_planes, 0)
    for at, item in enumerate(BACK):
        for plane in range(-1, DEPTH + 1):
            if plane >= 1:
                places_of, ref, layer = y_at, y_ref, plane - 1
            else:
                places_of, ref, layer = yz_at, yz_ref, -plane
                if (item, layer) in z_at:
                    main[at, plane + 1] = z_ref[z_at[item, layer]]
            low = None
            for r, row in ((0, 0), (1, ROWS - 1)):
                if (item, layer, r) in places_of:
                    k = places_of[item, layer, r]
                    piece = turn(ref[k // ROWS], row - k % ROWS, 0)
                    low = piece if low is None else jnp.where(rows == 0, low, piece)
            if low is not None:
                low_rows[at, plane + 1] = low
    for v in range(strips(True)):
        strip_tiles[0, v] = x_ref[:, v * COLS : (v + 1) * COLS]
        strip_tiles[1, v] = z_ref[len(z_at) + v]
        for k, tile in ((2, y_ref[tiles_of(y_at)]), (3, yz_ref[tiles_of(yz_at)])):
            first = turn(tile, -2 * v, 0)
            strip_tiles[k, v] = jnp.where(rows == 0, first, turn(first, -2, 0))

    def step(z, carry):
        @functools.cache
        def view(item, dz, dy, dx):
            at, plane = BACK.index(item), z + dz
            lower = jnp.where(plane >= 1, 0, 1)
            layer = lax.rem(plane + DEPTH - 1, DEPTH)
            shift = -2 * (DEPTH * (at % per) + layer) - 1
            keep = (lanes == 0) if dx == 0 else (lanes == 0) | (lanes == COLS - 1)

            def with_columns(tile, kind):
                if dx > 0:
                    return tile
                return jnp.where(keep, turn(strip_tiles[kind + lower, at // per], shift, 1), tile)

            tile = with_columns(main[at, plane + 1], 0)
            if dy <= 0:
                low = with_columns(low_rows[at, plane + 1], 2)
                edge = (rows == 0) if dy == 0 else (rows == 0) | (rows == ROWS - 1)
                tile = jnp.where(edge, low, tile)
            return turn(turn(tile, -dx, 1), -dy, 0)

        solid, way = masks_at(high_ref, own_ref, 1, start_z, total_z, z)
        links = drag_links(solid, way, scale)
        cot = []
        for i in range(Q):
            dx, dy, dz = VEL[i]
            own = view(("a", OPPOSITE[i]), 0, 0, 0)
            cot.append(pushed(i, own, view(("a", i), dz, dy, dx), solid, way, links))
        omega = relaxation(smag, eddy_ref[z])
        adjoint, grad, _ = collide_adjoint([state_ref[i, z] for i in range(Q)], omega, cot)
        for i in range(Q):
            out_ref[i, z] = adjoint[i]
        grad_ref[z] = -3.0 * omega * omega * (grad + view(("d", 0), 0, 0, 0))
        return carry

    lax.fori_loop(0, DEPTH, step, 0)


def plus_one(axis):
    count = lax.axis_size(axis)
    return [(i, (i + 1) % count) for i in range(count)]


def minus_one(axis):
    return [(target, source) for source, target in plus_one(axis)]


def pair_pairs(first, second):
    count = lax.axis_size("gz")
    return [(a * count + b, c * count + d) for a, c in first for b, d in second]


def call(kernel, outs, operands, scalars=0, far=False, scratch=(), flops=0, limit=32 << 20):
    def kind(k):
        if k < scalars:
            return pltpu.SMEM
        return pltpu.HBM if far else pltpu.VMEM

    outs = [out if isinstance(out[-1], type) else (out, jnp.float32) for out in outs]
    return pl.pallas_call(
        kernel,
        out_shape=[jax.ShapeDtypeStruct(*out) for out in outs],
        in_specs=[pl.BlockSpec(memory_space=kind(k)) for k in range(len(operands))],
        out_specs=[pl.BlockSpec(memory_space=pltpu.VMEM)] * len(outs),
        scratch_shapes=list(scratch),
        compiler_params=pltpu.CompilerParams(vmem_limit_bytes=limit),
        cost_estimate=pl.CostEstimate(flops=flops, bytes_accessed=1 << 20, transcendentals=0),
    )(*operands)


def exchange_faces(messages, step):
    vertical, spanwise, corner = messages
    vertical = lax.ppermute(vertical, "gz", step("gz"))
    spanwise = lax.ppermute(spanwise, "gy", step("gy"))
    corner = lax.ppermute(corner, ("gy", "gz"), pair_pairs(step("gy"), step("gz")))
    return vertical, spanwise, corner


def on_device(state, adjoint_seed, eddy_rate, smag_coeff, heights):
    total_x = COLS * lax.axis_size("gx")
    total_y = ROWS * lax.axis_size("gy")
    total_z = DEPTH * lax.axis_size("gz")
    scale = 1.0 / (2.0 * UREF * total_x * total_y)
    sens_scale = -3.0 / math.sqrt(total_x * total_y * total_z)
    tile = (ROWS, COLS)
    smag = smag_coeff.reshape(1)
    block = state.shape
    layer = eddy_rate.shape

    eddy = eddy_rate
    state, seed, columns, early = call(
        fetch_kernel,
        [
            block,
            block,
            (ROWS, strips(False) * COLS),
            (len(early_and_rest()[0]), *tile),
        ],
        (state, adjoint_seed),
        far=True,
        scratch=[pltpu.SemaphoreType.DMA((2,))],
        limit=(52 << 20) + (960 << 10),
    )
    (columns,) = call(eddy_columns_kernel, [columns.shape], (columns, eddy))
    columns, early = lax.optimization_barrier((columns, early))
    columns = lax.ppermute(columns, "gx", minus_one("gx"))
    early = lax.ppermute(early, "gz", minus_one("gz"))
    beside = ((2, len(SIDES), ROWS, COLS), jnp.int32)
    post, tang, high, own = call(
        functools.partial(first_kernel, total_y, total_x),
        [block, block, beside, beside],
        (smag, state, eddy, heights),
        scalars=1,
        flops=8_000_000,
    )
    messages = call(
        up_faces_kernel, face_shapes(False), (state, seed, eddy, post, tang, columns)
    )
    vertical, spanwise, corner = exchange_faces(messages, minus_one)
    n_first = lax.axis_size("gy") * lax.axis_size("gz")
    back, back_columns, sums = call(
        functools.partial(middle_kernel, total_z, scale, sens_scale),
        [(len(BACK), *layer), (ROWS, strips(True) * COLS), (n_first, COLS)],
        (smag, post, tang, seed, eddy, columns, spanwise, early, vertical, corner, high, own),
        scalars=1,
        scratch=[
            pltpu.VMEM(shape, jnp.float32)
            for shape in (
                (len(FIELDS), DEPTH + 2, ROWS, COLS),
                (len(FIELDS), 2, ROWS, COLS),
                (len(FIELDS), ROWS, COLS),
            )
        ],
        flops=20_000_000,
    )
    back_columns = lax.ppermute(back_columns, "gx", plus_one("gx"))
    sums = lax.all_to_all(sums, ("gy", "gz"), split_axis=0, concat_axis=0, tiled=True)
    shape_z, shape_y, shape_yz = face_shapes(True)
    (spanwise,) = call(back_rows_kernel, [shape_y], (back, back_columns))
    spanwise = lax.ppermute(spanwise, "gy", plus_one("gy"))
    (vertical,) = call(
        back_planes_kernel,
        [(shape_z[0] + shape_yz[0], *tile)],
        (back, back_columns, spanwise),
    )
    vertical, sums = lax.optimization_barrier((vertical, sums))
    vertical = lax.ppermute(vertical, "gz", plus_one("gz"))
    sums = jnp.broadcast_to(jnp.sum(sums, 0, keepdims=True), (lax.axis_size("gx"), COLS))
    sums = lax.all_to_all(sums, "gx", split_axis=0, concat_axis=0, tiled=True)
    adjoint_state, gradient = call(
        functools.partial(last_kernel, total_z, scale),
        [block, layer],
        (smag, state, eddy, back, back_columns, spanwise, vertical, high, own),
        scalars=1,
        scratch=[
            pltpu.VMEM(shape, jnp.float32)
            for shape in (
                (len(BACK), DEPTH + 2, ROWS, COLS),
                (len(BACK), DEPTH + 2, ROWS, COLS),
                (4, strips(True), ROWS, COLS),
            )
        ],
        flops=20_000_000,
    )
    gradient, sums = lax.optimization_barrier((gradient, sums))
    return adjoint_state, gradient, jnp.sum(sums[:, :2], 0)


def solution(mesh):
    return jax.shard_map(
        on_device,
        mesh=mesh,
        in_specs=(
            P(None, "gz", "gy", "gx"),
            P(None, "gz", "gy", "gx"),
            P("gz", "gy", "gx"),
            P(),
            P(),
        ),
        out_specs=(P(None, "gz", "gy", "gx"), P("gz", "gy", "gx"), P()),
        check_vma=False,
    )
```

```python
import functools
import math

import jax
import jax.numpy as jnp
from jax import lax
from jax.experimental import pallas as pl
from jax.experimental.pallas import tpu as pltpu
from jax.sharding import PartitionSpec as P

VEL = [
    (0, 0, 0),
    (1, 0, 0),
    (-1, 0, 0),
    (0, 1, 0),
    (0, -1, 0),
    (0, 0, 1),
    (0, 0, -1),
    (1, 1, 0),
    (-1, -1, 0),
    (1, -1, 0),
    (-1, 1, 0),
    (1, 0, 1),
    (-1, 0, -1),
    (1, 0, -1),
    (-1, 0, 1),
    (0, 1, 1),
    (0, -1, -1),
    (0, 1, -1),
    (0, -1, 1),
]
OPPOSITE = [0, 2, 1, 4, 3, 6, 5, 8, 7, 10, 9, 12, 11, 14, 13, 16, 15, 18, 17]
LATTICE_WEIGHTS = [1.0 / 3.0] + [1.0 / 18.0] * 6 + [1.0 / 36.0] * 12
UREF = 0.08
NU_BASE = 0.004
Q = 19
DEPTH = 4
ROWS = 8
COLS = 128
FAR = 1 << 20
SIDES = [(dy, dx) for dy in (-1, 0, 1) for dx in (-1, 0, 1)]

LAYER = [("f", i) for i in range(Q)] + [("g", i) for i in range(Q)] + [("e", 0)]
BACK = [("a", i) for i in range(Q)] + [("d", 0)]
FIELDS = [(name, i) for name in "ptg" for i in range(Q)] + [("e", 0)]


def crossing_items(axes, back):
    down = [i for i in range(Q) if all(VEL[i][a] == -1 for a in axes)]
    if back:
        return [("a", i) for i in down]
    up = [i for i in range(Q) if all(VEL[i][a] == 1 for a in axes)]
    return [(name, i) for i in down for name in "pt"] + [("g", i) for i in up]


def face_plan(back):
    near = BACK if back else LAYER
    vertical = [(item, 0) for item in near] + [(item, 1) for item in crossing_items([2], back)]
    spanwise = [(item, z, 0) for item in near for z in range(DEPTH)]
    spanwise += [(item, z, 1) for item in crossing_items([1], back) for z in range(DEPTH)]
    corner = [(item, 0, 0) for item in near]
    corner += [(item, 0, 1) for item in crossing_items([1], back)]
    corner += [(item, 1, 0) for item in crossing_items([2], back)]
    corner += [(item, 1, 1) for item in crossing_items([1, 2], back)]
    return vertical, spanwise, corner


def places(keys):
    return {key: at for at, key in enumerate(keys)}


def early_and_rest():
    vertical = PLANS[False][0]
    return [k for k in vertical if is_early(k)], [k for k in vertical if not is_early(k)]


def tiles_of(keys):
    return -(-len(keys) // ROWS)


def is_early(key):
    return key[0][0] in "fg"


PLANS = {back: face_plan(back) for back in (False, True)}
PLACES = {back: [places(keys) for keys in PLANS[back]] for back in (False, True)}


def strips(back):
    return -(-len(BACK if back else LAYER) * DEPTH * 2 // COLS)


def face_shapes(back):
    vertical, spanwise, corner = PLANS[back]
    planes = vertical if back else early_and_rest()[1]
    return [
        (len(planes) + strips(back), ROWS, COLS),
        (tiles_of(spanwise) + 1, ROWS, COLS),
        (tiles_of(corner) + 1, ROWS, COLS),
    ]


def signed(terms):
    total = None
    for factor, value in terms:
        if factor == 0:
            continue
        piece = value if factor == 1 else (-value if factor == -1 else factor * value)
        total = piece if total is None else total + piece
    return total


def along(idx, vec):
    return signed([(VEL[idx][axis], vec[axis]) for axis in range(3)])


def flow(pops):
    rho = signed([(1, p) for p in pops])
    inverse = 1.0 / rho
    vel = [signed([(VEL[i][axis], pops[i]) for i in range(Q)]) * inverse for axis in range(3)]
    return rho, vel


def shapes(vel):
    base = 1.0 - 1.5 * (vel[0] * vel[0] + vel[1] * vel[1] + vel[2] * vel[2])
    out = [base] + [None] * (Q - 1)
    for i in range(1, Q, 2):
        cu = along(i, vel)
        even = base + 4.5 * cu * cu
        out[i] = even + 3.0 * cu
        out[i + 1] = even - 3.0 * cu
    return out


def departures(pops):
    rho, vel = flow(pops)
    shape = shapes(vel)
    return [LATTICE_WEIGHTS[i] * rho * shape[i] - pops[i] for i in range(Q)]


def collide_adjoint(pops, omega, cot):
    rho, vel = flow(pops)
    shape = shapes(vel)
    weighted = [LATTICE_WEIGHTS[i] * cot[i] for i in range(Q)]
    level = signed([(1, weighted[i] * shape[i]) for i in range(Q)])
    mass = signed([(1, w) for w in weighted])
    first = [signed([(VEL[i][axis], weighted[i]) for i in range(Q)]) for axis in range(3)]

    def second(a, b):
        return signed([(VEL[i][a] * VEL[i][b], weighted[i]) for i in range(Q)])

    pair = {(a, b): second(a, b) for a in range(3) for b in range(a, 3)}
    slope = []
    for a in range(3):
        mixed = signed([(1, pair[min(a, b), max(a, b)] * vel[b]) for b in range(3)])
        slope.append(3.0 * first[a] + 9.0 * mixed - 3.0 * mass * vel[a])
    base = omega * (level - (slope[0] * vel[0] + slope[1] * vel[1] + slope[2] * vel[2]))
    tilt = [omega * s for s in slope]
    keep = 1.0 - omega
    adjoint = []
    for i in range(Q):
        part = along(i, tilt)
        adjoint.append(keep * cot[i] + (base if part is None else base + part))
    away = [LATTICE_WEIGHTS[i] * rho * shape[i] - pops[i] for i in range(Q)]
    grad = signed([(1, cot[i] * away[i]) for i in range(Q)])
    return adjoint, grad, away


def relaxation(smag, eddy):
    return 1.0 / (0.5 + 3.0 * (NU_BASE + smag * eddy))


def row_ids():
    return lax.broadcasted_iota(jnp.int32, (ROWS, COLS), 0)


def lane_ids():
    return lax.broadcasted_iota(jnp.int32, (ROWS, COLS), 1)


def turn(tile, amount, axis):
    size = tile.shape[axis]
    if isinstance(amount, int):
        amount %= size
        return tile if amount == 0 else pltpu.roll(tile, amount, axis)
    return pltpu.roll(tile, lax.rem(amount + size, size), axis)


def pack_columns(out_ref, planes, start):
    lanes = lane_ids()
    per = COLS // 2
    for strip in range(-(-len(planes) // per)):
        total = None
        for j, plane in enumerate(planes[strip * per : (strip + 1) * per]):
            moved = turn(plane(), 2 * j - start, 1)
            total = moved if total is None else jnp.where(lanes >= 2 * j, moved, total)
        out_ref[:, strip * COLS : (strip + 1) * COLS] = total


def pack_rows(pieces):
    rows = row_ids()
    total = None
    for j, (piece, row) in enumerate(pieces):
        moved = turn(piece, j - row, 0)
        total = moved if total is None else jnp.where(rows >= j, moved, total)
    return total


def pack_planes(keys, plane, x_ref, z_ref):
    for at, (item, layer) in enumerate(keys):
        z_ref[at] = plane(item, layer)
    for v in range(x_ref.shape[1] // COLS):
        z_ref[len(keys) + v] = x_ref[:, v * COLS : (v + 1) * COLS]


def pack_border(keys, plane, row_at, x_ref, out_ref):
    columns = [x_ref[:, v * COLS : (v + 1) * COLS] for v in range(x_ref.shape[1] // COLS)]
    for at in range(0, len(keys), ROWS):
        out_ref[at // ROWS] = pack_rows(
            [(plane(item, z), row_at[r]) for item, z, r in keys[at : at + ROWS]]
        )
    out_ref[tiles_of(keys)] = pack_rows([(tile, row_at[r]) for tile in columns for r in (0, 1)])


def fetch_kernel(
    state_ref, seed_ref, state_out, seed_out, columns_ref, early_ref, sems
):
    copies = [
        pltpu.make_async_copy(src, dst, sems.at[k])
        for k, (src, dst) in enumerate(((state_ref, state_out), (seed_ref, seed_out)))
    ]
    for copy in copies:
        copy.start()
    for copy in copies:
        copy.wait()

    def plane(item, z):
        name, i = item
        return {"f": state_out, "g": seed_out}[name][i, z]

    planes = [
        functools.partial(plane, item, z) for item in LAYER if item[0] != "e" for z in range(DEPTH)
    ]
    pack_columns(columns_ref, planes, 0)
    for at, (item, layer) in enumerate(early_and_rest()[0]):
        early_ref[at] = plane(item, layer)


def eddy_columns_kernel(columns_ref, eddy_ref, out_ref):
    lanes = lane_ids()
    first = 2 * DEPTH * (len(LAYER) - 1)
    out_ref[:, :] = columns_ref[:, :]
    for z in range(DEPTH):
        strip, lane = divmod(first + 2 * z, COLS)
        spot = slice(strip * COLS, (strip + 1) * COLS)
        moved = turn(eddy_ref[z], lane, 1)
        out_ref[:, spot] = jnp.where(lanes // 2 == lane // 2, moved, out_ref[:, spot])


def collide_fields(smag, pops, eddy):
    omega = relaxation(smag, eddy)
    away = departures(pops)
    heat = omega * omega * eddy
    post = [pops[i] + omega * away[i] for i in range(Q)]
    return post, [heat * away[i] for i in range(Q)]


def first_kernel(
    total_y, total_x, smag_ref, state_ref, eddy_ref, heights_ref, post_ref, tang_ref, high_ref, own_ref
):
    smag = smag_ref[0]
    for z in range(DEPTH):
        post, tang = collide_fields(smag, [state_ref[i, z] for i in range(Q)], eddy_ref[z])
        for i in range(Q):
            post_ref[i, z] = post[i]
            tang_ref[i, z] = tang[i]
    rows, lanes = row_ids(), lane_ids()
    start_y = lax.axis_index("gy") * ROWS
    start_x = lax.axis_index("gx") * COLS

    def block(dy, dx):
        y = lax.rem(start_y + dy * ROWS + total_y, total_y)
        x = lax.rem(start_x + dx * COLS + total_x, total_x)
        return heights_ref[
            pl.ds(pl.multiple_of(y, ROWS), ROWS), pl.ds(pl.multiple_of(x, COLS), COLS)
        ]

    blocks = {side: block(*side) for side in SIDES}

    def beside(lower, own, upper, ids, axis, size, first, step):
        if first:
            if step < 0:
                return turn(own, 1, axis)
            return turn(jnp.where(ids <= step, upper, own), -step, axis)
        if step == 0:
            return own
        edge = jnp.where(ids == size - 1, lower, own) if step < 0 else jnp.where(ids == 0, upper, own)
        return turn(edge, -step, axis)

    for k, first in enumerate((1, 0)):
        across = {
            (dy, dx): beside(
                *(blocks[dy, n] for n in (-1, 0, 1)), lanes, 1, COLS, first, dx
            )
            for dy in (-1, 0, 1)
            for dx in (-1, 0, 1)
        }
        near = {
            (dy, dx): beside(
                *(across[n, dx] for n in (-1, 0, 1)), rows, 0, ROWS, first, dy
            )
            for dy, dx in SIDES
        }
        y = start_y + jnp.where((rows == 0) & (first == 1), ROWS, rows)
        x = start_x + jnp.where((lanes == 0) & (first == 1), COLS, lanes)
        for side, (dy, dx) in enumerate(SIDES):
            high, own = near[dy, dx], near[0, 0]
            if dy:
                low_y = y + min(dy, 0)
                wall = (low_y == -1) | (low_y == total_y - 1)
                high, own = jnp.where(wall, FAR, high), jnp.where(wall, FAR, own)
            if dx:
                low_x = x + min(dx, 0)
                wall = (low_x == -1) | (low_x == total_x - 1)
                high, own = jnp.where(wall, FAR, high), jnp.where(wall, FAR, own)
            high_ref[k, side] = high
            own_ref[k, side] = own


def up_plane(state_ref, seed_ref, eddy_ref, post_ref, tang_ref):
    fields = {"f": state_ref, "g": seed_ref, "p": post_ref, "t": tang_ref}

    def plane(item, z):
        name, i = item
        return eddy_ref[z] if name == "e" else fields[name][i, z]

    return plane


def up_faces_kernel(
    state_ref, seed_ref, eddy_ref, post_ref, tang_ref, x_ref, z_ref, y_ref, yz_ref
):
    plane = up_plane(state_ref, seed_ref, eddy_ref, post_ref, tang_ref)
    pack_planes(early_and_rest()[1], plane, x_ref, z_ref)
    pack_border(PLANS[False][1], plane, (0, 1), x_ref, y_ref)
    pack_border(PLANS[False][2], plane, (0, 1), x_ref, yz_ref)


def back_rows_kernel(back_ref, x_ref, y_ref):
    def plane(item, z):
        return back_ref[BACK.index(item), z]

    pack_border(PLANS[True][1], plane, (0, ROWS - 1), x_ref, y_ref)


def back_planes_kernel(back_ref, x_ref, y_ref, z_ref):
    vertical, _, corner = PLANS[True]

    def plane(item, layer):
        return back_ref[BACK.index(item), DEPTH - 1 - layer]

    pack_planes(vertical, plane, x_ref, z_ref)
    y_at = PLACES[True][1]
    first = len(vertical) + strips(True)
    for at in range(0, len(corner), ROWS):
        spots = [y_at[item, DEPTH - 1 - layer, r] for item, layer, r in corner[at : at + ROWS]]
        z_ref[first + at // ROWS] = pack_rows([(y_ref[k // ROWS], k % ROWS) for k in spots])
    z_ref[first + tiles_of(corner)] = y_ref[tiles_of(y_at)]


def level_of(start_z, total_z, plane):
    level = start_z + plane
    return lax.rem(level + total_z, total_z)


def wall_between(start_z, total_z, plane, step):
    upper = start_z + plane + (1 if step > 0 else 0)
    return (upper == total_z) | (upper == 0)


def masks_at(high_ref, own_ref, frame, start_z, total_z, plane):
    solid, way = {}, {}
    here = level_of(start_z, total_z, plane)
    for i in range(Q):
        dx, dy, dz = VEL[i]
        side = SIDES.index((dy, dx))
        there, mine = here, here
        if dz:
            wall = wall_between(start_z, total_z, plane, dz)
            there = jnp.where(wall, -1, level_of(start_z, total_z, plane + dz))
            mine = jnp.where(wall, -1, here)
        solid[VEL[i]] = there < high_ref[frame, side]
        way[VEL[i]] = mine >= own_ref[frame, side]
    return solid, way


def drag_links(solid, way, scale):
    fluid = way[VEL[0]]
    return {
        i: jnp.where(fluid & solid[VEL[i]], 2.0 * scale * VEL[i][0], 0.0)
        for i in range(Q)
        if VEL[i][0] != 0
    }


def pushed(i, own, target, solid, way, links):
    value = jnp.where(way[VEL[i]], target, 0.0) + jnp.where(solid[VEL[i]], own, 0.0)
    return value + links[i] if i in links else value


def middle_kernel(
    total_z,
    scale,
    sens_scale,
    smag_ref,
    post_ref,
    tang_ref,
    seed_ref,
    eddy_ref,
    x_ref,
    y_ref,
    early_ref,
    z_ref,
    yz_ref,
    high_ref,
    own_ref,
    back_ref,
    columns_ref,
    sums_ref,
    main,
    y_tiles,
    x_tiles,
):
    smag = smag_ref[0]
    start_z = lax.axis_index("gz") * DEPTH
    rows, lanes = row_ids(), lane_ids()
    _, y_at, yz_at = PLACES[False]
    early_at, rest_at = (places(keys) for keys in early_and_rest())
    per = COLS // (2 * DEPTH)
    pops_items = [("f", i) for i in range(Q)]

    def collided(tile):
        post, tang = collide_fields(smag, [tile(item) for item in pops_items], tile(("e", 0)))
        out = {("p", i): post[i] for i in range(Q)}
        out.update({("t", i): tang[i] for i in range(Q)})
        out.update({item: tile(item) for item in LAYER if item[0] in "eg"})
        return out

    above = collided(
        lambda item: (z_ref[rest_at[item, 0]] if item[0] == "e" else early_ref[early_at[item, 0]])
    )

    def copy_planes(z, carry):
        for ref, first in ((post_ref, 0), (tang_ref, Q), (seed_ref, 2 * Q)):
            for i in range(Q):
                main[first + i, z] = ref[i, z]
        main[3 * Q, z] = eddy_ref[z]
        return carry

    lax.fori_loop(0, DEPTH, copy_planes, 0)
    for at, item in enumerate(FIELDS):
        main[at, DEPTH] = above[item]
        if (item, 1) in early_at:
            main[at, DEPTH + 1] = early_ref[early_at[item, 1]]
        if (item, 1) in rest_at:
            main[at, DEPTH + 1] = z_ref[rest_at[item, 1]]

    def y_piece(key, row):
        at = y_at[key]
        return turn(y_ref[at // ROWS], row - at % ROWS, 0)

    def yz_piece(key, row):
        at = yz_at[key]
        return turn(yz_ref[at // ROWS], row - at % ROWS, 0)

    y_near = collided(lambda item: y_piece((item, 0, 0), 0))
    y_above = collided(lambda item: yz_piece((item, 0, 0), 0))

    for at, item in enumerate(FIELDS):
        tile = y_near[item]
        if (item, 0, 1) in y_at:
            tile = jnp.where(rows < DEPTH, tile, y_piece((item, 0, 1), DEPTH))
        y_tiles[at, 0] = tile
        tile = y_above[item]
        for z, r in ((1, 0), (0, 1), (1, 1)):
            if (item, z, r) in yz_at:
                row = DEPTH * r + z
                tile = jnp.where(rows == row, yz_piece((item, z, r), row), tile)
        y_tiles[at, 1] = tile

    n_strips = strips(False)
    yx_tiles = [turn(y_ref[tiles_of(y_at)], -2 * v, 0) for v in range(n_strips)]
    yzx_tiles = [turn(yz_ref[tiles_of(yz_at)], -2 * v, 0) for v in range(n_strips)]

    def column_tile(item):
        v, at = divmod(LAYER.index(item), per)
        at *= 2 * DEPTH
        near = turn(x_ref[:, v * COLS : (v + 1) * COLS], -at, 1)
        high = turn(z_ref[len(rest_at) + v], 8 - at, 1)
        near_rows = turn(yx_tiles[v], 16 - at, 1)
        high_rows = turn(yzx_tiles[v], 24 - at, 1)
        return jnp.where(
            lanes < 16,
            jnp.where(lanes < 8, near, high),
            jnp.where(lanes < 24, near_rows, high_rows),
        )

    sides = collided(column_tile)
    for at, item in enumerate(FIELDS):
        x_tiles[at] = sides[item]

    def viewer(plane_of):
        @functools.cache
        def view(item, dz, dy, dx):
            at, plane = FIELDS.index(item), plane_of[dz]
            tile = main[at, plane]
            if dx >= 0:
                tile = jnp.where(lanes <= dx, turn(x_tiles[at], -2 * plane, 1), tile)
            if dy >= 0:
                k = plane // DEPTH
                z = plane - k * DEPTH
                low = turn(y_tiles[at, k], -z, 0)
                if dy == 1:
                    low = jnp.where(rows == 0, low, turn(y_tiles[at, k], 1 - DEPTH - z, 0))
                if dx >= 0:
                    low = jnp.where(lanes <= dx, turn(x_tiles[at], -2 * plane - 16, 1), low)
                tile = jnp.where(rows <= dy, low, tile)
            return turn(turn(tile, -dx, 1), -dy, 0)

        return view

    def step(z, carry):
        drag, sens = carry
        plane = z + 1
        view = viewer({dz: plane + dz for dz in (-1, 0, 1)})
        solid, way = masks_at(high_ref, own_ref, 0, start_z, total_z, plane)
        links = drag_links(solid, way, scale)

        def pulled(name, i):
            dx, dy, dz = VEL[i]
            away = view((name, i), -dz, -dy, -dx)
            if i == 0:
                return away
            return jnp.where(solid[-dx, -dy, -dz], view((name, OPPOSITE[i]), 0, 0, 0), away)

        f_one = [pulled("p", i) for i in range(Q)]
        cot = []
        for i in range(Q):
            dx, dy, dz = VEL[i]
            own = view(("g", OPPOSITE[i]), 0, 0, 0)
            cot.append(pushed(i, own, view(("g", i), dz, dy, dx), solid, way, links))
        eddy = view(("e", 0), 0, 0, 0)
        omega = relaxation(smag, eddy)
        adjoint, grad, away = collide_adjoint(f_one, omega, cot)
        for i in range(Q):
            back_ref[i, z] = adjoint[i]
        back_ref[Q, z] = grad
        for i in links:
            drag = drag + links[i] * (view(("p", i), 0, 0, 0) + f_one[i] + omega * away[i])
            sens = sens + links[i] * view(("t", i), 0, 0, 0)
        sens = sens + omega * omega * eddy * grad
        for i in range(Q):
            sens = sens + adjoint[i] * pulled("t", i)
        return drag, sens

    zero = jnp.zeros((ROWS, COLS), jnp.float32)
    drag, sens = lax.fori_loop(0, DEPTH, step, (zero, zero))
    sums_ref[...] = jnp.where(
        lax.broadcasted_iota(jnp.int32, sums_ref.shape, 1) == 0,
        jnp.sum(drag),
        jnp.sum(sens) * sens_scale,
    )
    planes = [
        functools.partial(lambda c, z: back_ref[c, z], c, z)
        for c in range(len(BACK))
        for z in range(DEPTH)
    ]
    pack_columns(columns_ref, planes, COLS - 1)


def last_kernel(
    total_z,
    scale,
    smag_ref,
    state_ref,
    eddy_ref,
    back_ref,
    x_ref,
    y_ref,
    z_ref,
    high_ref,
    own_ref,
    out_ref,
    grad_ref,
    main,
    low_rows,
    strip_tiles,
):
    smag = smag_ref[0]
    start_z = lax.axis_index("gz") * DEPTH
    rows, lanes = row_ids(), lane_ids()
    z_at, y_at, yz_at = PLACES[True]
    yz_ref = z_ref.at[pl.ds(len(z_at) + strips(True), tiles_of(yz_at) + 1)]
    per = COLS // 2 // DEPTH

    def copy_planes(z, carry):
        for at in range(len(BACK)):
            main[at, z + 2] = back_ref[at, z]
        return carry

    lax.fori_loop(0, DEPTH, copy_planes, 0)
    for at, item in enumerate(BACK):
        for plane in range(-1, DEPTH + 1):
            if plane >= 1:
                places_of, ref, layer = y_at, y_ref, plane - 1
            else:
                places_of, ref, layer = yz_at, yz_ref, -plane
                if (item, layer) in z_at:
                    main[at, plane + 1] = z_ref[z_at[item, layer]]
            low = None
            for r, row in ((0, 0), (1, ROWS - 1)):
                if (item, layer, r) in places_of:
                    k = places_of[item, layer, r]
                    piece = turn(ref[k // ROWS], row - k % ROWS, 0)
                    low = piece if low is None else jnp.where(rows == 0, low, piece)
            if low is not None:
                low_rows[at, plane + 1] = low
    for v in range(strips(True)):
        strip_tiles[0, v] = x_ref[:, v * COLS : (v + 1) * COLS]
        strip_tiles[1, v] = z_ref[len(z_at) + v]
        for k, tile in ((2, y_ref[tiles_of(y_at)]), (3, yz_ref[tiles_of(yz_at)])):
            first = turn(tile, -2 * v, 0)
            strip_tiles[k, v] = jnp.where(rows == 0, first, turn(first, -2, 0))

    def step(z, carry):
        @functools.cache
        def view(item, dz, dy, dx):
            at, plane = BACK.index(item), z + dz
            lower = jnp.where(plane >= 1, 0, 1)
            layer = lax.rem(plane + DEPTH - 1, DEPTH)
            shift = -2 * (DEPTH * (at % per) + layer) - 1
            keep = (lanes == 0) if dx == 0 else (lanes == 0) | (lanes == COLS - 1)

            def with_columns(tile, kind):
                if dx > 0:
                    return tile
                return jnp.where(keep, turn(strip_tiles[kind + lower, at // per], shift, 1), tile)

            tile = with_columns(main[at, plane + 1], 0)
            if dy <= 0:
                low = with_columns(low_rows[at, plane + 1], 2)
                edge = (rows == 0) if dy == 0 else (rows == 0) | (rows == ROWS - 1)
                tile = jnp.where(edge, low, tile)
            return turn(turn(tile, -dx, 1), -dy, 0)

        solid, way = masks_at(high_ref, own_ref, 1, start_z, total_z, z)
        links = drag_links(solid, way, scale)
        cot = []
        for i in range(Q):
            dx, dy, dz = VEL[i]
            own = view(("a", OPPOSITE[i]), 0, 0, 0)
            cot.append(pushed(i, own, view(("a", i), dz, dy, dx), solid, way, links))
        omega = relaxation(smag, eddy_ref[z])
        adjoint, grad, _ = collide_adjoint([state_ref[i, z] for i in range(Q)], omega, cot)
        for i in range(Q):
            out_ref[i, z] = adjoint[i]
        grad_ref[z] = -3.0 * omega * omega * (grad + view(("d", 0), 0, 0, 0))
        return carry

    lax.fori_loop(0, DEPTH, step, 0, unroll=2)


def plus_one(axis):
    count = lax.axis_size(axis)
    return [(i, (i + 1) % count) for i in range(count)]


def minus_one(axis):
    return [(target, source) for source, target in plus_one(axis)]


def pair_pairs(first, second):
    count = lax.axis_size("gz")
    return [(a * count + b, c * count + d) for a, c in first for b, d in second]


def call(kernel, outs, operands, scalars=0, far=False, scratch=(), flops=0, limit=32 << 20):
    def kind(k):
        if k < scalars:
            return pltpu.SMEM
        return pltpu.HBM if far else pltpu.VMEM

    outs = [out if isinstance(out[-1], type) else (out, jnp.float32) for out in outs]
    return pl.pallas_call(
        kernel,
        out_shape=[jax.ShapeDtypeStruct(*out) for out in outs],
        in_specs=[pl.BlockSpec(memory_space=kind(k)) for k in range(len(operands))],
        out_specs=[pl.BlockSpec(memory_space=pltpu.VMEM)] * len(outs),
        scratch_shapes=list(scratch),
        compiler_params=pltpu.CompilerParams(vmem_limit_bytes=limit),
        cost_estimate=pl.CostEstimate(flops=flops, bytes_accessed=1 << 20, transcendentals=0),
    )(*operands)


def exchange_faces(messages, step):
    vertical, spanwise, corner = messages
    vertical = lax.ppermute(vertical, "gz", step("gz"))
    spanwise = lax.ppermute(spanwise, "gy", step("gy"))
    corner = lax.ppermute(corner, ("gy", "gz"), pair_pairs(step("gy"), step("gz")))
    return vertical, spanwise, corner


def on_device(state, adjoint_seed, eddy_rate, smag_coeff, heights):
    total_x = COLS * lax.axis_size("gx")
    total_y = ROWS * lax.axis_size("gy")
    total_z = DEPTH * lax.axis_size("gz")
    scale = 1.0 / (2.0 * UREF * total_x * total_y)
    sens_scale = -3.0 / math.sqrt(total_x * total_y * total_z)
    tile = (ROWS, COLS)
    smag = smag_coeff.reshape(1)
    block = state.shape
    layer = eddy_rate.shape

    eddy = eddy_rate
    state, seed, columns, early = call(
        fetch_kernel,
        [
            block,
            block,
            (ROWS, strips(False) * COLS),
            (len(early_and_rest()[0]), *tile),
        ],
        (state, adjoint_seed),
        far=True,
        scratch=[pltpu.SemaphoreType.DMA((2,))],
        limit=(52 << 20) + (960 << 10),
    )
    (columns,) = call(eddy_columns_kernel, [columns.shape], (columns, eddy))
    columns, early = lax.optimization_barrier((columns, early))
    columns = lax.ppermute(columns, "gx", minus_one("gx"))
    early = lax.ppermute(early, "gz", minus_one("gz"))
    beside = ((2, len(SIDES), ROWS, COLS), jnp.int32)
    post, tang, high, own = call(
        functools.partial(first_kernel, total_y, total_x),
        [block, block, beside, beside],
        (smag, state, eddy, heights),
        scalars=1,
        flops=8_000_000,
    )
    messages = call(
        up_faces_kernel, face_shapes(False), (state, seed, eddy, post, tang, columns)
    )
    vertical, spanwise, corner = exchange_faces(messages, minus_one)
    n_first = lax.axis_size("gy") * lax.axis_size("gz")
    back, back_columns, sums = call(
        functools.partial(middle_kernel, total_z, scale, sens_scale),
        [(len(BACK), *layer), (ROWS, strips(True) * COLS), (n_first, COLS)],
        (smag, post, tang, seed, eddy, columns, spanwise, early, vertical, corner, high, own),
        scalars=1,
        scratch=[
            pltpu.VMEM(shape, jnp.float32)
            for shape in (
                (len(FIELDS), DEPTH + 2, ROWS, COLS),
                (len(FIELDS), 2, ROWS, COLS),
                (len(FIELDS), ROWS, COLS),
            )
        ],
        flops=20_000_000,
    )
    back_columns = lax.ppermute(back_columns, "gx", plus_one("gx"))
    sums = lax.all_to_all(sums, ("gy", "gz"), split_axis=0, concat_axis=0, tiled=True)
    shape_z, shape_y, shape_yz = face_shapes(True)
    (spanwise,) = call(back_rows_kernel, [shape_y], (back, back_columns))
    spanwise = lax.ppermute(spanwise, "gy", plus_one("gy"))
    (vertical,) = call(
        back_planes_kernel,
        [(shape_z[0] + shape_yz[0], *tile)],
        (back, back_columns, spanwise),
    )
    vertical, sums = lax.optimization_barrier((vertical, sums))
    vertical = lax.ppermute(vertical, "gz", plus_one("gz"))
    sums = jnp.broadcast_to(jnp.sum(sums, 0, keepdims=True), (lax.axis_size("gx"), COLS))
    sums = lax.all_to_all(sums, "gx", split_axis=0, concat_axis=0, tiled=True)
    adjoint_state, gradient = call(
        functools.partial(last_kernel, total_z, scale),
        [block, layer],
        (smag, state, eddy, back, back_columns, spanwise, vertical, high, own),
        scalars=1,
        scratch=[
            pltpu.VMEM(shape, jnp.float32)
            for shape in (
                (len(BACK), DEPTH + 2, ROWS, COLS),
                (len(BACK), DEPTH + 2, ROWS, COLS),
                (4, strips(True), ROWS, COLS),
            )
        ],
        flops=20_000_000,
    )
    gradient, sums = lax.optimization_barrier((gradient, sums))
    return adjoint_state, gradient, jnp.sum(sums[:, :2], 0)


def solution(mesh):
    return jax.shard_map(
        on_device,
        mesh=mesh,
        in_specs=(
            P(None, "gz", "gy", "gx"),
            P(None, "gz", "gy", "gx"),
            P("gz", "gy", "gx"),
            P(),
            P(),
        ),
        out_specs=(P(None, "gz", "gy", "gx"), P("gz", "gy", "gx"), P()),
        check_vma=False,
    )
```

```python
import functools
import math

import jax
import jax.numpy as jnp
from jax import lax
from jax.experimental import pallas as pl
from jax.experimental.pallas import tpu as pltpu
from jax.sharding import PartitionSpec as P

VEL = [
    (0, 0, 0),
    (1, 0, 0),
    (-1, 0, 0),
    (0, 1, 0),
    (0, -1, 0),
    (0, 0, 1),
    (0, 0, -1),
    (1, 1, 0),
    (-1, -1, 0),
    (1, -1, 0),
    (-1, 1, 0),
    (1, 0, 1),
    (-1, 0, -1),
    (1, 0, -1),
    (-1, 0, 1),
    (0, 1, 1),
    (0, -1, -1),
    (0, 1, -1),
    (0, -1, 1),
]
OPPOSITE = [0, 2, 1, 4, 3, 6, 5, 8, 7, 10, 9, 12, 11, 14, 13, 16, 15, 18, 17]
LATTICE_WEIGHTS = [1.0 / 3.0] + [1.0 / 18.0] * 6 + [1.0 / 36.0] * 12
UREF = 0.08
NU_BASE = 0.004
Q = 19
DEPTH = 4
ROWS = 8
COLS = 128
FAR = 1 << 20
SIDES = [(dy, dx) for dy in (-1, 0, 1) for dx in (-1, 0, 1)]

LAYER = [("f", i) for i in range(Q)] + [("g", i) for i in range(Q)] + [("e", 0)]
BACK = [("a", i) for i in range(Q)] + [("d", 0)]
FIELDS = [(name, i) for name in "ptg" for i in range(Q)] + [("e", 0)]


def crossing_items(axes, back):
    down = [i for i in range(Q) if all(VEL[i][a] == -1 for a in axes)]
    if back:
        return [("a", i) for i in down]
    up = [i for i in range(Q) if all(VEL[i][a] == 1 for a in axes)]
    return [(name, i) for i in down for name in "pt"] + [("g", i) for i in up]


def face_plan(back):
    near = BACK if back else LAYER
    vertical = [(item, 0) for item in near] + [(item, 1) for item in crossing_items([2], back)]
    spanwise = [(item, z, 0) for item in near for z in range(DEPTH)]
    spanwise += [(item, z, 1) for item in crossing_items([1], back) for z in range(DEPTH)]
    corner = [(item, 0, 0) for item in near]
    corner += [(item, 0, 1) for item in crossing_items([1], back)]
    corner += [(item, 1, 0) for item in crossing_items([2], back)]
    corner += [(item, 1, 1) for item in crossing_items([1, 2], back)]
    return vertical, spanwise, corner


def places(keys):
    return {key: at for at, key in enumerate(keys)}


def early_and_rest():
    vertical = PLANS[False][0]
    return [k for k in vertical if is_early(k)], [k for k in vertical if not is_early(k)]


def tiles_of(keys):
    return -(-len(keys) // ROWS)


def is_early(key):
    return key[0][0] in "fg"


PLANS = {back: face_plan(back) for back in (False, True)}
PLACES = {back: [places(keys) for keys in PLANS[back]] for back in (False, True)}


def strips(back):
    return -(-len(BACK if back else LAYER) * DEPTH * 2 // COLS)


def face_shapes(back):
    vertical, spanwise, corner = PLANS[back]
    planes = vertical if back else early_and_rest()[1]
    return [
        (len(planes) + strips(back), ROWS, COLS),
        (tiles_of(spanwise) + 1, ROWS, COLS),
        (tiles_of(corner) + 1, ROWS, COLS),
    ]


def signed(terms):
    total = None
    for factor, value in terms:
        if factor == 0:
            continue
        piece = value if factor == 1 else (-value if factor == -1 else factor * value)
        total = piece if total is None else total + piece
    return total


def along(idx, vec):
    return signed([(VEL[idx][axis], vec[axis]) for axis in range(3)])


def flow(pops):
    rho = signed([(1, p) for p in pops])
    inverse = 1.0 / rho
    vel = [signed([(VEL[i][axis], pops[i]) for i in range(Q)]) * inverse for axis in range(3)]
    return rho, vel


def shapes(vel):
    base = 1.0 - 1.5 * (vel[0] * vel[0] + vel[1] * vel[1] + vel[2] * vel[2])
    out = [base] + [None] * (Q - 1)
    for i in range(1, Q, 2):
        cu = along(i, vel)
        even = base + 4.5 * cu * cu
        out[i] = even + 3.0 * cu
        out[i + 1] = even - 3.0 * cu
    return out


def departures(pops):
    rho, vel = flow(pops)
    shape = shapes(vel)
    return [LATTICE_WEIGHTS[i] * rho * shape[i] - pops[i] for i in range(Q)]


def collide_adjoint(pops, omega, cot):
    rho, vel = flow(pops)
    shape = shapes(vel)
    weighted = [LATTICE_WEIGHTS[i] * cot[i] for i in range(Q)]
    level = signed([(1, weighted[i] * shape[i]) for i in range(Q)])
    mass = signed([(1, w) for w in weighted])
    first = [signed([(VEL[i][axis], weighted[i]) for i in range(Q)]) for axis in range(3)]

    def second(a, b):
        return signed([(VEL[i][a] * VEL[i][b], weighted[i]) for i in range(Q)])

    pair = {(a, b): second(a, b) for a in range(3) for b in range(a, 3)}
    slope = []
    for a in range(3):
        mixed = signed([(1, pair[min(a, b), max(a, b)] * vel[b]) for b in range(3)])
        slope.append(3.0 * first[a] + 9.0 * mixed - 3.0 * mass * vel[a])
    base = omega * (level - (slope[0] * vel[0] + slope[1] * vel[1] + slope[2] * vel[2]))
    tilt = [omega * s for s in slope]
    keep = 1.0 - omega
    adjoint = []
    for i in range(Q):
        part = along(i, tilt)
        adjoint.append(keep * cot[i] + (base if part is None else base + part))
    away = [LATTICE_WEIGHTS[i] * rho * shape[i] - pops[i] for i in range(Q)]
    grad = signed([(1, cot[i] * away[i]) for i in range(Q)])
    return adjoint, grad, away


def relaxation(smag, eddy):
    return 1.0 / (0.5 + 3.0 * (NU_BASE + smag * eddy))


def row_ids():
    return lax.broadcasted_iota(jnp.int32, (ROWS, COLS), 0)


def lane_ids():
    return lax.broadcasted_iota(jnp.int32, (ROWS, COLS), 1)


def turn(tile, amount, axis):
    size = tile.shape[axis]
    if isinstance(amount, int):
        amount %= size
        return tile if amount == 0 else pltpu.roll(tile, amount, axis)
    return pltpu.roll(tile, lax.rem(amount + size, size), axis)


def pack_columns(out_ref, planes, start):
    lanes = lane_ids()
    per = COLS // 2
    for strip in range(-(-len(planes) // per)):
        total = None
        for j, plane in enumerate(planes[strip * per : (strip + 1) * per]):
            moved = turn(plane(), 2 * j - start, 1)
            total = moved if total is None else jnp.where(lanes >= 2 * j, moved, total)
        out_ref[:, strip * COLS : (strip + 1) * COLS] = total


def pack_rows(pieces):
    rows = row_ids()
    total = None
    for j, (piece, row) in enumerate(pieces):
        moved = turn(piece, j - row, 0)
        total = moved if total is None else jnp.where(rows >= j, moved, total)
    return total


def pack_planes(keys, plane, x_ref, z_ref):
    for at, (item, layer) in enumerate(keys):
        z_ref[at] = plane(item, layer)
    for v in range(x_ref.shape[1] // COLS):
        z_ref[len(keys) + v] = x_ref[:, v * COLS : (v + 1) * COLS]


def pack_border(keys, plane, row_at, x_ref, out_ref):
    columns = [x_ref[:, v * COLS : (v + 1) * COLS] for v in range(x_ref.shape[1] // COLS)]
    for at in range(0, len(keys), ROWS):
        out_ref[at // ROWS] = pack_rows(
            [(plane(item, z), row_at[r]) for item, z, r in keys[at : at + ROWS]]
        )
    out_ref[tiles_of(keys)] = pack_rows([(tile, row_at[r]) for tile in columns for r in (0, 1)])


def fetch_kernel(
    state_ref, seed_ref, state_out, seed_out, columns_ref, early_ref, sems
):
    copies = [
        pltpu.make_async_copy(src, dst, sems.at[k])
        for k, (src, dst) in enumerate(((state_ref, state_out), (seed_ref, seed_out)))
    ]
    for copy in copies:
        copy.start()
    for copy in copies:
        copy.wait()

    def plane(item, z):
        name, i = item
        return {"f": state_out, "g": seed_out}[name][i, z]

    planes = [
        functools.partial(plane, item, z) for item in LAYER if item[0] != "e" for z in range(DEPTH)
    ]
    pack_columns(columns_ref, planes, 0)
    for at, (item, layer) in enumerate(early_and_rest()[0]):
        early_ref[at] = plane(item, layer)


def eddy_columns_kernel(columns_ref, eddy_ref, out_ref):
    lanes = lane_ids()
    first = 2 * DEPTH * (len(LAYER) - 1)
    out_ref[:, :] = columns_ref[:, :]
    for z in range(DEPTH):
        strip, lane = divmod(first + 2 * z, COLS)
        spot = slice(strip * COLS, (strip + 1) * COLS)
        moved = turn(eddy_ref[z], lane, 1)
        out_ref[:, spot] = jnp.where(lanes // 2 == lane // 2, moved, out_ref[:, spot])


def collide_fields(smag, pops, eddy):
    omega = relaxation(smag, eddy)
    away = departures(pops)
    heat = omega * omega * eddy
    post = [pops[i] + omega * away[i] for i in range(Q)]
    return post, [heat * away[i] for i in range(Q)]


def first_kernel(
    total_y, total_x, smag_ref, state_ref, eddy_ref, heights_ref, post_ref, tang_ref, high_ref, own_ref
):
    smag = smag_ref[0]
    for z in range(DEPTH):
        post, tang = collide_fields(smag, [state_ref[i, z] for i in range(Q)], eddy_ref[z])
        for i in range(Q):
            post_ref[i, z] = post[i]
            tang_ref[i, z] = tang[i]
    rows, lanes = row_ids(), lane_ids()
    start_y = lax.axis_index("gy") * ROWS
    start_x = lax.axis_index("gx") * COLS

    def block(dy, dx):
        y = lax.rem(start_y + dy * ROWS + total_y, total_y)
        x = lax.rem(start_x + dx * COLS + total_x, total_x)
        return heights_ref[
            pl.ds(pl.multiple_of(y, ROWS), ROWS), pl.ds(pl.multiple_of(x, COLS), COLS)
        ]

    blocks = {side: block(*side) for side in SIDES}

    def beside(lower, own, upper, ids, axis, size, first, step):
        if first:
            if step < 0:
                return turn(own, 1, axis)
            return turn(jnp.where(ids <= step, upper, own), -step, axis)
        if step == 0:
            return own
        edge = jnp.where(ids == size - 1, lower, own) if step < 0 else jnp.where(ids == 0, upper, own)
        return turn(edge, -step, axis)

    for k, first in enumerate((1, 0)):
        across = {
            (dy, dx): beside(
                *(blocks[dy, n] for n in (-1, 0, 1)), lanes, 1, COLS, first, dx
            )
            for dy in (-1, 0, 1)
            for dx in (-1, 0, 1)
        }
        near = {
            (dy, dx): beside(
                *(across[n, dx] for n in (-1, 0, 1)), rows, 0, ROWS, first, dy
            )
            for dy, dx in SIDES
        }
        y = start_y + jnp.where((rows == 0) & (first == 1), ROWS, rows)
        x = start_x + jnp.where((lanes == 0) & (first == 1), COLS, lanes)
        for side, (dy, dx) in enumerate(SIDES):
            high, own = near[dy, dx], near[0, 0]
            if dy:
                low_y = y + min(dy, 0)
                wall = (low_y == -1) | (low_y == total_y - 1)
                high, own = jnp.where(wall, FAR, high), jnp.where(wall, FAR, own)
            if dx:
                low_x = x + min(dx, 0)
                wall = (low_x == -1) | (low_x == total_x - 1)
                high, own = jnp.where(wall, FAR, high), jnp.where(wall, FAR, own)
            high_ref[k, side] = high
            own_ref[k, side] = own


def up_plane(state_ref, seed_ref, eddy_ref, post_ref, tang_ref):
    fields = {"f": state_ref, "g": seed_ref, "p": post_ref, "t": tang_ref}

    def plane(item, z):
        name, i = item
        return eddy_ref[z] if name == "e" else fields[name][i, z]

    return plane


def up_faces_kernel(
    state_ref, seed_ref, eddy_ref, post_ref, tang_ref, x_ref, z_ref, y_ref, yz_ref
):
    plane = up_plane(state_ref, seed_ref, eddy_ref, post_ref, tang_ref)
    pack_planes(early_and_rest()[1], plane, x_ref, z_ref)
    pack_border(PLANS[False][1], plane, (0, 1), x_ref, y_ref)
    pack_border(PLANS[False][2], plane, (0, 1), x_ref, yz_ref)


def back_rows_kernel(back_ref, x_ref, y_ref):
    def plane(item, z):
        return back_ref[BACK.index(item), z]

    pack_border(PLANS[True][1], plane, (0, ROWS - 1), x_ref, y_ref)


def back_planes_kernel(back_ref, x_ref, y_ref, z_ref):
    vertical, _, corner = PLANS[True]

    def plane(item, layer):
        return back_ref[BACK.index(item), DEPTH - 1 - layer]

    pack_planes(vertical, plane, x_ref, z_ref)
    y_at = PLACES[True][1]
    first = len(vertical) + strips(True)
    for at in range(0, len(corner), ROWS):
        spots = [y_at[item, DEPTH - 1 - layer, r] for item, layer, r in corner[at : at + ROWS]]
        z_ref[first + at // ROWS] = pack_rows([(y_ref[k // ROWS], k % ROWS) for k in spots])
    z_ref[first + tiles_of(corner)] = y_ref[tiles_of(y_at)]


def level_of(start_z, total_z, plane):
    level = start_z + plane
    return lax.rem(level + total_z, total_z)


def wall_between(start_z, total_z, plane, step):
    upper = start_z + plane + (1 if step > 0 else 0)
    return (upper == total_z) | (upper == 0)


def masks_at(high_ref, own_ref, frame, start_z, total_z, plane):
    solid, way = {}, {}
    here = level_of(start_z, total_z, plane)
    for i in range(Q):
        dx, dy, dz = VEL[i]
        side = SIDES.index((dy, dx))
        there, mine = here, here
        if dz:
            wall = wall_between(start_z, total_z, plane, dz)
            there = jnp.where(wall, -1, level_of(start_z, total_z, plane + dz))
            mine = jnp.where(wall, -1, here)
        solid[VEL[i]] = there < high_ref[frame, side]
        way[VEL[i]] = mine >= own_ref[frame, side]
    return solid, way


def drag_links(solid, way, scale):
    fluid = way[VEL[0]]
    return {
        i: jnp.where(fluid & solid[VEL[i]], 2.0 * scale * VEL[i][0], 0.0)
        for i in range(Q)
        if VEL[i][0] != 0
    }


def pushed(i, own, target, solid, way, links):
    value = jnp.where(way[VEL[i]], target, 0.0) + jnp.where(solid[VEL[i]], own, 0.0)
    return value + links[i] if i in links else value


def middle_kernel(
    total_z,
    scale,
    sens_scale,
    smag_ref,
    post_ref,
    tang_ref,
    seed_ref,
    eddy_ref,
    x_ref,
    y_ref,
    early_ref,
    z_ref,
    yz_ref,
    high_ref,
    own_ref,
    back_ref,
    columns_ref,
    sums_ref,
    main,
    y_tiles,
    x_tiles,
):
    smag = smag_ref[0]
    start_z = lax.axis_index("gz") * DEPTH
    rows, lanes = row_ids(), lane_ids()
    _, y_at, yz_at = PLACES[False]
    early_at, rest_at = (places(keys) for keys in early_and_rest())
    per = COLS // (2 * DEPTH)
    pops_items = [("f", i) for i in range(Q)]

    def collided(tile):
        post, tang = collide_fields(smag, [tile(item) for item in pops_items], tile(("e", 0)))
        out = {("p", i): post[i] for i in range(Q)}
        out.update({("t", i): tang[i] for i in range(Q)})
        out.update({item: tile(item) for item in LAYER if item[0] in "eg"})
        return out

    above = collided(
        lambda item: (z_ref[rest_at[item, 0]] if item[0] == "e" else early_ref[early_at[item, 0]])
    )

    def copy_planes(z, carry):
        for ref, first in ((post_ref, 0), (tang_ref, Q), (seed_ref, 2 * Q)):
            for i in range(Q):
                main[first + i, z] = ref[i, z]
        main[3 * Q, z] = eddy_ref[z]
        return carry

    lax.fori_loop(0, DEPTH, copy_planes, 0)
    for at, item in enumerate(FIELDS):
        main[at, DEPTH] = above[item]
        if (item, 1) in early_at:
            main[at, DEPTH + 1] = early_ref[early_at[item, 1]]
        if (item, 1) in rest_at:
            main[at, DEPTH + 1] = z_ref[rest_at[item, 1]]

    def y_piece(key, row):
        at = y_at[key]
        return turn(y_ref[at // ROWS], row - at % ROWS, 0)

    def yz_piece(key, row):
        at = yz_at[key]
        return turn(yz_ref[at // ROWS], row - at % ROWS, 0)

    y_near = collided(lambda item: y_piece((item, 0, 0), 0))
    y_above = collided(lambda item: yz_piece((item, 0, 0), 0))

    for at, item in enumerate(FIELDS):
        tile = y_near[item]
        if (item, 0, 1) in y_at:
            tile = jnp.where(rows < DEPTH, tile, y_piece((item, 0, 1), DEPTH))
        y_tiles[at, 0] = tile
        tile = y_above[item]
        for z, r in ((1, 0), (0, 1), (1, 1)):
            if (item, z, r) in yz_at:
                row = DEPTH * r + z
                tile = jnp.where(rows == row, yz_piece((item, z, r), row), tile)
        y_tiles[at, 1] = tile

    n_strips = strips(False)
    yx_tiles = [turn(y_ref[tiles_of(y_at)], -2 * v, 0) for v in range(n_strips)]
    yzx_tiles = [turn(yz_ref[tiles_of(yz_at)], -2 * v, 0) for v in range(n_strips)]

    def column_tile(item):
        v, at = divmod(LAYER.index(item), per)
        at *= 2 * DEPTH
        near = turn(x_ref[:, v * COLS : (v + 1) * COLS], -at, 1)
        high = turn(z_ref[len(rest_at) + v], 8 - at, 1)
        near_rows = turn(yx_tiles[v], 16 - at, 1)
        high_rows = turn(yzx_tiles[v], 24 - at, 1)
        return jnp.where(
            lanes < 16,
            jnp.where(lanes < 8, near, high),
            jnp.where(lanes < 24, near_rows, high_rows),
        )

    sides = collided(column_tile)
    for at, item in enumerate(FIELDS):
        x_tiles[at] = sides[item]

    def viewer(plane_of):
        @functools.cache
        def view(item, dz, dy, dx):
            at, plane = FIELDS.index(item), plane_of[dz]
            tile = main[at, plane]
            if dx >= 0:
                tile = jnp.where(lanes <= dx, turn(x_tiles[at], -2 * plane, 1), tile)
            if dy >= 0:
                k = plane // DEPTH
                z = plane - k * DEPTH
                low = turn(y_tiles[at, k], -z, 0)
                if dy == 1:
                    low = jnp.where(rows == 0, low, turn(y_tiles[at, k], 1 - DEPTH - z, 0))
                if dx >= 0:
                    low = jnp.where(lanes <= dx, turn(x_tiles[at], -2 * plane - 16, 1), low)
                tile = jnp.where(rows <= dy, low, tile)
            return turn(turn(tile, -dx, 1), -dy, 0)

        return view

    def step(z, carry):
        drag, sens = carry
        plane = z + 1
        view = viewer({dz: plane + dz for dz in (-1, 0, 1)})
        solid, way = masks_at(high_ref, own_ref, 0, start_z, total_z, plane)
        links = drag_links(solid, way, scale)

        def pulled(name, i):
            dx, dy, dz = VEL[i]
            away = view((name, i), -dz, -dy, -dx)
            if i == 0:
                return away
            return jnp.where(solid[-dx, -dy, -dz], view((name, OPPOSITE[i]), 0, 0, 0), away)

        f_one = [pulled("p", i) for i in range(Q)]
        cot = []
        for i in range(Q):
            dx, dy, dz = VEL[i]
            own = view(("g", OPPOSITE[i]), 0, 0, 0)
            cot.append(pushed(i, own, view(("g", i), dz, dy, dx), solid, way, links))
        eddy = view(("e", 0), 0, 0, 0)
        omega = relaxation(smag, eddy)
        adjoint, grad, away = collide_adjoint(f_one, omega, cot)
        for i in range(Q):
            back_ref[i, z] = adjoint[i]
        back_ref[Q, z] = grad
        for i in links:
            drag = drag + links[i] * (view(("p", i), 0, 0, 0) + f_one[i] + omega * away[i])
            sens = sens + links[i] * view(("t", i), 0, 0, 0)
        sens = sens + omega * omega * eddy * grad
        for i in range(Q):
            sens = sens + adjoint[i] * pulled("t", i)
        return drag, sens

    zero = jnp.zeros((ROWS, COLS), jnp.float32)
    drag, sens = lax.fori_loop(0, DEPTH, step, (zero, zero))
    sums_ref[...] = jnp.where(
        lax.broadcasted_iota(jnp.int32, sums_ref.shape, 1) == 0,
        jnp.sum(drag),
        jnp.sum(sens) * sens_scale,
    )
    planes = [
        functools.partial(lambda c, z: back_ref[c, z], c, z)
        for c in range(len(BACK))
        for z in range(DEPTH)
    ]
    pack_columns(columns_ref, planes, COLS - 1)


def last_kernel(
    total_z,
    scale,
    smag_ref,
    state_ref,
    eddy_ref,
    back_ref,
    x_ref,
    y_ref,
    z_ref,
    high_ref,
    own_ref,
    out_ref,
    grad_ref,
    main,
    low_rows,
    strip_tiles,
):
    smag = smag_ref[0]
    start_z = lax.axis_index("gz") * DEPTH
    rows, lanes = row_ids(), lane_ids()
    z_at, y_at, yz_at = PLACES[True]
    yz_ref = z_ref.at[pl.ds(len(z_at) + strips(True), tiles_of(yz_at) + 1)]
    per = COLS // 2 // DEPTH

    def copy_planes(z, carry):
        for at in range(len(BACK)):
            main[at, z + 2] = back_ref[at, z]
        return carry

    lax.fori_loop(0, DEPTH, copy_planes, 0)
    for at, item in enumerate(BACK):
        for plane in range(-1, DEPTH + 1):
            if plane >= 1:
                places_of, ref, layer = y_at, y_ref, plane - 1
            else:
                places_of, ref, layer = yz_at, yz_ref, -plane
                if (item, layer) in z_at:
                    main[at, plane + 1] = z_ref[z_at[item, layer]]
            low = None
            for r, row in ((0, 0), (1, ROWS - 1)):
                if (item, layer, r) in places_of:
                    k = places_of[item, layer, r]
                    piece = turn(ref[k // ROWS], row - k % ROWS, 0)
                    low = piece if low is None else jnp.where(rows == 0, low, piece)
            if low is not None:
                low_rows[at, plane + 1] = low
    for v in range(strips(True)):
        strip_tiles[0, v] = x_ref[:, v * COLS : (v + 1) * COLS]
        strip_tiles[1, v] = z_ref[len(z_at) + v]
        for k, tile in ((2, y_ref[tiles_of(y_at)]), (3, yz_ref[tiles_of(yz_at)])):
            first = turn(tile, -2 * v, 0)
            strip_tiles[k, v] = jnp.where(rows == 0, first, turn(first, -2, 0))

    def step(z, carry):
        @functools.cache
        def view(item, dz, dy, dx):
            at, plane = BACK.index(item), z + dz
            lower = jnp.where(plane >= 1, 0, 1)
            layer = lax.rem(plane + DEPTH - 1, DEPTH)
            shift = -2 * (DEPTH * (at % per) + layer) - 1
            keep = (lanes == 0) if dx == 0 else (lanes == 0) | (lanes == COLS - 1)

            def with_columns(tile, kind):
                if dx > 0:
                    return tile
                return jnp.where(keep, turn(strip_tiles[kind + lower, at // per], shift, 1), tile)

            tile = with_columns(main[at, plane + 1], 0)
            if dy <= 0:
                low = with_columns(low_rows[at, plane + 1], 2)
                edge = (rows == 0) if dy == 0 else (rows == 0) | (rows == ROWS - 1)
                tile = jnp.where(edge, low, tile)
            return turn(turn(tile, -dx, 1), -dy, 0)

        solid, way = masks_at(high_ref, own_ref, 1, start_z, total_z, z)
        links = drag_links(solid, way, scale)
        cot = []
        for i in range(Q):
            dx, dy, dz = VEL[i]
            own = view(("a", OPPOSITE[i]), 0, 0, 0)
            cot.append(pushed(i, own, view(("a", i), dz, dy, dx), solid, way, links))
        omega = relaxation(smag, eddy_ref[z])
        adjoint, grad, _ = collide_adjoint([state_ref[i, z] for i in range(Q)], omega, cot)
        for i in range(Q):
            out_ref[i, z] = adjoint[i]
        grad_ref[z] = -3.0 * omega * omega * (grad + view(("d", 0), 0, 0, 0))
        return carry

    lax.fori_loop(0, DEPTH, step, 0)


def plus_one(axis):
    count = lax.axis_size(axis)
    return [(i, (i + 1) % count) for i in range(count)]


def minus_one(axis):
    return [(target, source) for source, target in plus_one(axis)]


def pair_pairs(first, second):
    count = lax.axis_size("gz")
    return [(a * count + b, c * count + d) for a, c in first for b, d in second]


def call(kernel, outs, operands, scalars=0, far=False, scratch=(), flops=0, limit=32 << 20):
    def kind(k):
        if k < scalars:
            return pltpu.SMEM
        return pltpu.HBM if far else pltpu.VMEM

    outs = [out if isinstance(out[-1], type) else (out, jnp.float32) for out in outs]
    return pl.pallas_call(
        kernel,
        out_shape=[jax.ShapeDtypeStruct(*out) for out in outs],
        in_specs=[pl.BlockSpec(memory_space=kind(k)) for k in range(len(operands))],
        out_specs=[pl.BlockSpec(memory_space=pltpu.VMEM)] * len(outs),
        scratch_shapes=list(scratch),
        compiler_params=pltpu.CompilerParams(vmem_limit_bytes=limit),
        cost_estimate=pl.CostEstimate(flops=flops, bytes_accessed=1 << 20, transcendentals=0),
    )(*operands)


def exchange_faces(messages, step):
    vertical, spanwise, corner = messages
    vertical = lax.ppermute(vertical, "gz", step("gz"))
    spanwise = lax.ppermute(spanwise, "gy", step("gy"))
    corner = lax.ppermute(corner, ("gy", "gz"), pair_pairs(step("gy"), step("gz")))
    return vertical, spanwise, corner


def on_device(state, adjoint_seed, eddy_rate, smag_coeff, heights):
    total_x = COLS * lax.axis_size("gx")
    total_y = ROWS * lax.axis_size("gy")
    total_z = DEPTH * lax.axis_size("gz")
    scale = 1.0 / (2.0 * UREF * total_x * total_y)
    sens_scale = -3.0 / math.sqrt(total_x * total_y * total_z)
    tile = (ROWS, COLS)
    smag = smag_coeff.reshape(1)
    block = state.shape
    layer = eddy_rate.shape

    eddy = eddy_rate
    state, seed, columns, early = call(
        fetch_kernel,
        [
            block,
            block,
            (ROWS, strips(False) * COLS),
            (len(early_and_rest()[0]), *tile),
        ],
        (state, adjoint_seed),
        far=True,
        scratch=[pltpu.SemaphoreType.DMA((2,))],
        limit=(52 << 20) + (960 << 10),
    )
    (columns,) = call(eddy_columns_kernel, [columns.shape], (columns, eddy))
    columns = lax.ppermute(columns, "gx", minus_one("gx"))
    early = lax.ppermute(early, "gz", minus_one("gz"))
    beside = ((2, len(SIDES), ROWS, COLS), jnp.int32)
    post, tang, high, own = call(
        functools.partial(first_kernel, total_y, total_x),
        [block, block, beside, beside],
        (smag, state, eddy, heights),
        scalars=1,
        flops=8_000_000,
    )
    messages = call(
        up_faces_kernel, face_shapes(False), (state, seed, eddy, post, tang, columns)
    )
    vertical, spanwise, corner = exchange_faces(messages, minus_one)
    n_first = lax.axis_size("gy") * lax.axis_size("gz")
    back, back_columns, sums = call(
        functools.partial(middle_kernel, total_z, scale, sens_scale),
        [(len(BACK), *layer), (ROWS, strips(True) * COLS), (n_first, COLS)],
        (smag, post, tang, seed, eddy, columns, spanwise, early, vertical, corner, high, own),
        scalars=1,
        scratch=[
            pltpu.VMEM(shape, jnp.float32)
            for shape in (
                (len(FIELDS), DEPTH + 2, ROWS, COLS),
                (len(FIELDS), 2, ROWS, COLS),
                (len(FIELDS), ROWS, COLS),
            )
        ],
        flops=20_000_000,
    )
    back_columns = lax.ppermute(back_columns, "gx", plus_one("gx"))
    sums = lax.all_to_all(sums, ("gy", "gz"), split_axis=0, concat_axis=0, tiled=True)
    shape_z, shape_y, shape_yz = face_shapes(True)
    (spanwise,) = call(back_rows_kernel, [shape_y], (back, back_columns))
    spanwise = lax.ppermute(spanwise, "gy", plus_one("gy"))
    (vertical,) = call(
        back_planes_kernel,
        [(shape_z[0] + shape_yz[0], *tile)],
        (back, back_columns, spanwise),
    )
    vertical, sums = lax.optimization_barrier((vertical, sums))
    vertical = lax.ppermute(vertical, "gz", plus_one("gz"))
    sums = jnp.broadcast_to(jnp.sum(sums, 0, keepdims=True), (lax.axis_size("gx"), COLS))
    sums = lax.all_to_all(sums, "gx", split_axis=0, concat_axis=0, tiled=True)
    adjoint_state, gradient = call(
        functools.partial(last_kernel, total_z, scale),
        [block, layer],
        (smag, state, eddy, back, back_columns, spanwise, vertical, high, own),
        scalars=1,
        scratch=[
            pltpu.VMEM(shape, jnp.float32)
            for shape in (
                (len(BACK), DEPTH + 2, ROWS, COLS),
                (len(BACK), DEPTH + 2, ROWS, COLS),
                (4, strips(True), ROWS, COLS),
            )
        ],
        flops=20_000_000,
    )
    gradient, sums = lax.optimization_barrier((gradient, sums))
    return adjoint_state, gradient, jnp.sum(sums[:, :2], 0)


def solution(mesh):
    return jax.shard_map(
        on_device,
        mesh=mesh,
        in_specs=(
            P(None, "gz", "gy", "gx"),
            P(None, "gz", "gy", "gx"),
            P("gz", "gy", "gx"),
            P(),
            P(),
        ),
        out_specs=(P(None, "gz", "gy", "gx"), P("gz", "gy", "gx"), P()),
        check_vma=False,
    )
```
